256 devices in a mesh: group: 8 (over z), fsdp: 32 (over x, y, core).
Axes of the slice: x: 4, y: 4, z: 8, core: 2. Of those that a mesh axis runs over, the one named last changes fastest.
Arguments:
- grad: bfloat16 [256, 262144], P(None, ('group', 'fsdp')), may hold values from -60 to 60
- moment: float32 [256, 262144], P(None, ('group', 'fsdp')), may hold values from 0.1 to 10
- order: int32 [256], replicated, may hold values from 0 to 255, each once
- left_stat: float32 [256, 512, 512], P(('group', 'fsdp')), may hold values from -5 to 5
- right_stat: float32 [256, 512, 512], P(('group', 'fsdp')), may hold values from -5 to 5
- left_root: bfloat16 [256, 512, 512], P(('group', 'fsdp')), may hold values from -2 to 2
- right_root: bfloat16 [256, 512, 512], P(('group', 'fsdp')), may hold values from -2 to 2
Outputs:
- update: bfloat16 [256, 262144], P(None, ('group', 'fsdp'))
- moment_new: float32 [256, 262144], P(None, ('group', 'fsdp'))
- left_new: float32 [256, 512, 512], P(('group', 'fsdp'))
- right_new: float32 [256, 512, 512], P(('group', 'fsdp'))
The draws below stay inside these ranges and needn't reach their ends.
Inputs may be any that keep to these rules, and one draw needn't show every extreme that they name: `order`: every block is named by exactly one slot; slot s lies on the device of index s // 1 along group+fsdp.
All inputs are finite; a program needn't handle non-finite values.
Results may differ from the reference program's by a relative error of at most 0.0057.
Values may be sent and summed in bfloat16 or wider, within the bound.
A program may use at most 64 MiB of HBM per device.

```python
import math
import jax
import jax.numpy as jnp
from jax import lax

B = 512
NBLK = 256


def definite_blocks(key, lower, upper):
    first, second = jax.random.split(key)
    diag = jnp.exp(jax.random.uniform(first, (NBLK, B), jnp.float32, math.log(lower), math.log(upper)))
    noise = jnp.clip(jax.random.normal(second, (NBLK, B, B), jnp.float32), -4.0, 4.0)
    sym = (noise + jnp.swapaxes(noise, 1, 2)) * 0.7071
    weight = jnp.sqrt(diag[:, :, None] * diag[:, None, :])
    off = 0.5 / math.sqrt(B) * sym * weight
    eye = (jnp.arange(B)[:, None] == jnp.arange(B)[None, :]).astype(jnp.float32)
    return off * (1.0 - eye[None]) + eye[None] * diag[:, :, None]


def draw_grad(key, part):
    key = jax.random.fold_in(key, 11)
    first, second, third = jax.random.split(key, 3)
    rough = jnp.exp(jax.random.uniform(second, (NBLK, B, 1), jnp.float32, math.log(0.5), math.log(2.0)))
    rising = 10.0 ** (jnp.arange(B, dtype=jnp.float32) / B)
    row_scale = rising[None, :, None] * rough
    col_scale = jnp.exp(jax.random.uniform(third, (NBLK, 1, B), jnp.float32, 0.0, math.log(10.0)))
    base = jnp.clip(jax.random.normal(first, (NBLK, B, B), jnp.float32), -6.0, 6.0)
    values = 0.05 * base * row_scale * col_scale
    return values.reshape(NBLK, B * B).astype(jnp.bfloat16)


def draw_left_stat(key, part):
    key = jax.random.fold_in(key, 21)
    return definite_blocks(key, 0.5, 5.0)


def draw_right_stat(key, part):
    key = jax.random.fold_in(key, 22)
    return definite_blocks(key, 0.5, 5.0)


def draw_left_root(key, part):
    key = jax.random.fold_in(key, 23)
    return definite_blocks(key, 0.5, 2.0).astype(jnp.bfloat16)


def draw_right_root(key, part):
    key = jax.random.fold_in(key, 24)
    return definite_blocks(key, 0.5, 2.0).astype(jnp.bfloat16)


def shard_levels(own_key, extent, shards, smallest, high):
    gain, own = 1.0, jax.random.fold_in(own_key, 6)
    for position, parts in shards:
        steps = jnp.exp(jax.random.uniform(jax.random.fold_in(own, position), (parts,), jnp.float32, smallest / len(shards), high / len(shards)))
        gain = gain * jnp.repeat(steps, extent[position] // parts).reshape([-1 if axis == position else 1 for axis in range(len(extent))])
    return gain


def setup_inputs(seed: int = 0) -> dict:
    streams_of = jax.random.split(jax.random.key(seed), 8)
    return {
        "grad": draw_grad(jax.random.fold_in(streams_of[7], 71), 0),
        "moment": jnp.clip(jnp.exp(math.log(10.0) - 4.6051702 * jax.random.uniform(streams_of[1], (NBLK, B * B), jnp.float32) ** shard_levels(streams_of[1], (NBLK, B * B), ((1, 256),), -0.2, 0.2)), 0.1, 10.0),
        "order": jax.random.permutation(streams_of[2], NBLK).astype(jnp.int32),
        "left_stat": draw_left_stat(jax.random.fold_in(streams_of[7], 71), 0),
        "right_stat": draw_right_stat(jax.random.fold_in(streams_of[7], 71), 0),
        "left_root": draw_left_root(jax.random.fold_in(streams_of[7], 71), 0),
        "right_root": draw_right_root(jax.random.fold_in(streams_of[7], 71), 0),
    }


MOMENT_DECAY = 0.95
STAT_DECAY = 0.9
ADAM_EPS = 1e-08
PRECON_EPS = 1e-06

def one_slot(pieces):
    block, left, right, left_inv, right_inv = pieces
    gram_left = jnp.dot(block, block.T, preferred_element_type=jnp.float32)
    gram_right = jnp.dot(block.T, block, preferred_element_type=jnp.float32)
    left_next = STAT_DECAY * left + (1.0 - STAT_DECAY) * gram_left / B
    right_next = STAT_DECAY * right + (1.0 - STAT_DECAY) * gram_right / B
    half = jnp.dot(left_inv, block, preferred_element_type=jnp.float32).astype(jnp.bfloat16)
    full = jnp.dot(half, right_inv, preferred_element_type=jnp.float32)
    precon_sq = jnp.sum(full * full)
    return (left_next, right_next, full.astype(jnp.bfloat16), precon_sq)

def reference(grad, moment, order, left_stat, right_stat, left_root, right_root):
    gradient = grad.astype(jnp.float32)
    moment_new = MOMENT_DECAY * moment + (1.0 - MOMENT_DECAY) * gradient * gradient
    direction = gradient / (jnp.sqrt(moment_new) + ADAM_EPS)
    adam_sq = lax.optimization_barrier(jnp.sum(direction * direction, axis=1))
    slot_blocks = jnp.take(grad, order, axis=0).reshape(NBLK, B, B)
    left_new, right_new, precon, precon_sq = lax.map(one_slot, (slot_blocks, left_stat, right_stat, left_root, right_root))
    scale = jnp.sqrt(jnp.take(adam_sq, order)) / (jnp.sqrt(precon_sq) + PRECON_EPS)
    widened = lax.optimization_barrier(precon).astype(jnp.float32)
    scaled = (widened * scale[:, None, None]).astype(jnp.bfloat16).reshape(NBLK, B * B)
    update = jnp.zeros((NBLK, B * B), jnp.bfloat16).at[order].set(scaled)
    return (update, moment_new, left_new, right_new)
```

```python
import functools

import jax
import jax.numpy as jnp
from jax import lax
from jax.experimental import pallas as pl
from jax.experimental.pallas import tpu as pltpu
from jax.sharding import PartitionSpec as P

MOMENT_DECAY = 0.95
STAT_DECAY = 0.9
ADAM_EPS = 1e-08
PRECON_EPS = 1e-06

LANES = 128
SUBLANES = 8
MESH = pl.DeviceIdType.MESH


def matmul(a, b, a_dim=1, b_dim=0):
    return lax.dot_general(
        a, b, (((a_dim,), (b_dim,)), ((), ())), preferred_element_type=jnp.float32
    )


def widen(source, wide):
    depth, fan = source.shape[:2]
    step = min(fan, 32)
    for i in range(depth):
        for j in range(0, fan, step):
            part = source[i, j : j + step].astype(jnp.float32)
            start = (i * fan + j) * SUBLANES
            wide[start : start + step * SUBLANES, :] = part.reshape(step * SUBLANES, LANES)


def alternate(count):
    return sorted(range(1, count), key=lambda k: (-min(k, count - k), k))


def exchange(
    depth,
    across,
    grad_hbm,
    moment_hbm,
    order_hbm,
    left_stat_hbm,
    right_stat_hbm,
    left_root_hbm,
    right_root_hbm,
    landed_back,
    moment,
    left_stat,
    right_stat,
    order,
    grad,
    left_root,
    right_root,
    wide,
    sent,
    relay,
    landed,
    sent_back,
    relay_back,
    block,
    norms,
    norms_z,
    norms_z_sum,
    norms_f,
    load_sem,
    z_send,
    z_recv,
    f_send,
    f_recv,
    norm_send,
    norm_recv,
):
    fan = relay.shape[0]
    row = fan // across
    blocks = depth * fan
    side = block.shape[0]
    pieces = side // LANES
    g = lax.axis_index("group")
    f = lax.axis_index("fsdp")
    x = f // row
    me = g * fan + f

    loads = [
        pltpu.make_async_copy(source, target, load_sem.at[i])
        for i, (source, target) in enumerate(
            (
                (order_hbm, order),
                (grad_hbm, grad),
                (moment_hbm, moment),
                (left_root_hbm, left_root),
                (right_root_hbm, right_root),
                (left_stat_hbm, left_stat),
                (right_stat_hbm, right_stat),
            )
        )
    ]
    for load in loads:
        load.start()

    barrier = pltpu.get_barrier_semaphore()

    def greet_z(k, carry):
        pl.semaphore_signal(barrier, inc=1, device_id=((g + k) % depth, f), device_id_type=MESH)
        return carry

    def greet_f(k, carry):
        pl.semaphore_signal(barrier, inc=1, device_id=(g, (f + k) % fan), device_id_type=MESH)
        return carry

    lax.fori_loop(1, depth, greet_z, 0)
    lax.fori_loop(1, fan, greet_f, 0)

    loads[0].wait()
    which = lax.broadcasted_iota(jnp.int32, (blocks, blocks), 0)
    holds = jnp.where(which == order[...], 1.0, 0.0)
    slots_half = holds.T.astype(jnp.bfloat16)

    def narrow(target):
        step = min(blocks, 32)
        for i in range(0, blocks, step):
            part = wide[i * SUBLANES : (i + step) * SUBLANES, :]
            target[i : i + step] = part.reshape(step, SUBLANES, LANES).astype(jnp.bfloat16)

    def chunk_of(k):
        return ((x + k) % across) * row

    def send_z(k, source, through, way):
        start = chunk_of(k)

        for j in alternate(depth):
            to = (g + j) % depth
            pltpu.make_async_remote_copy(
                src_ref=source.at[pl.ds(to * fan + start, row)],
                dst_ref=through.at[pl.ds(start, row), g],
                send_sem=z_send.at[way],
                recv_sem=z_recv.at[way, k],
                device_id=(to, f),
                device_id_type=MESH,
            ).start()
        pltpu.make_async_copy(
            source.at[pl.ds(g * fan + start, row)],
            through.at[pl.ds(start, row), g],
            z_recv.at[way, k],
        ).start()

    def send_f(k, through, target, way):
        start = chunk_of(k)
        arrived = through.at[pl.ds(start, row)]
        pltpu.make_async_copy(arrived, arrived, z_recv.at[way, k]).wait()
        place = f % row

        for j in alternate(row) + ([] if k == 0 else [0]):
            to = start + (place + j) % row
            pltpu.make_async_remote_copy(
                src_ref=through.at[to],
                dst_ref=target.at[:, f],
                send_sem=f_send.at[way],
                recv_sem=f_recv.at[way],
                device_id=(g, to),
                device_id_type=MESH,
            ).start()
        if k == 0:
            pltpu.make_async_copy(through.at[f], target.at[:, f], f_recv.at[way]).start()

    def wait_all(target, way):
        pltpu.make_async_copy(target, target, f_recv.at[way]).wait()

    def wait_sent(source, through, way):
        part = source.at[pl.ds(0, (depth - 1) * fan)]
        pltpu.make_async_copy(part, part, z_send.at[way]).wait()
        part = through.at[pl.ds(0, fan - 1)]
        pltpu.make_async_copy(part, part, f_send.at[way]).wait()

    chunks = sorted(range(across), key=lambda k: -min(k, across - k))

    loads[1].wait()
    for c in range(0, SUBLANES, 2):
        pair = matmul(slots_half, grad[:, c * LANES : (c + 2) * LANES])
        wide[pl.ds(c, blocks, stride=SUBLANES), :] = pair[:, :LANES]
        wide[pl.ds(c + 1, blocks, stride=SUBLANES), :] = pair[:, LANES:]
    narrow(sent)
    pl.semaphore_wait(barrier, depth - 1 + fan - 1)
    for k in chunks[:2]:
        send_z(k, sent, relay, 0)

    loads[2].wait()
    tall = min(blocks, 32)
    share = jnp.zeros((1, blocks), jnp.float32)
    for i in range(0, blocks, tall):
        rows = pl.ds(i, tall)
        gradient = grad[rows, :].astype(jnp.float32)
        second = MOMENT_DECAY * moment[rows, :] + (1.0 - MOMENT_DECAY) * gradient * gradient
        moment[rows, :] = second
        direction = gradient / (jnp.sqrt(second) + ADAM_EPS)
        squares = jnp.sum(direction * direction, axis=1, keepdims=True)
        share = share + jnp.sum(holds[i : i + tall, :] * squares, axis=0, keepdims=True)
    norms[...] = share
    for i, k in enumerate(chunks):
        send_f(k, relay, landed, 0)
        if i + 2 < across:
            send_z(chunks[i + 2], sent, relay, 0)

    def norm_z(j, carry):
        pltpu.make_async_remote_copy(
            src_ref=norms,
            dst_ref=norms_z.at[g],
            send_sem=norm_send.at[0],
            recv_sem=norm_recv.at[0],
            device_id=((g + j) % depth, f),
            device_id_type=MESH,
        ).start()
        return carry

    lax.fori_loop(1, depth, norm_z, 0)
    pltpu.make_async_copy(norms, norms_z.at[g], norm_recv.at[0]).start()
    pltpu.make_async_copy(norms_z, norms_z, norm_recv.at[0]).wait()
    norms_z_sum[...] = jnp.sum(norms_z[...], axis=0)

    def norm_f(j, carry):
        pltpu.make_async_remote_copy(
            src_ref=norms_z_sum,
            dst_ref=norms_f.at[f],
            send_sem=norm_send.at[1],
            recv_sem=norm_recv.at[1],
            device_id=(g, (f + j) % fan),
            device_id_type=MESH,
        ).start()
        return carry

    lax.fori_loop(1, fan, norm_f, 0)
    pltpu.make_async_copy(norms_z_sum, norms_f.at[f], norm_recv.at[1]).start()

    wait_all(landed, 0)
    widen(landed, wide)
    for c in range(pieces):
        block[:, c * LANES : (c + 1) * LANES] = wide[pl.ds(c, side, stride=pieces), :].astype(
            jnp.bfloat16
        )
    loads[3].wait()
    loads[4].wait()
    half = matmul(left_root[...], block[...]).astype(jnp.bfloat16)
    full = matmul(half, right_root[...])
    precon_sq = jnp.sum(full * full, keepdims=True)
    precon = full.astype(jnp.bfloat16).astype(jnp.float32)
    pltpu.make_async_copy(norms_f, norms_f, norm_recv.at[1]).wait()
    totals = jnp.sum(norms_f[...], axis=0)
    lane = lax.broadcasted_iota(jnp.int32, (1, blocks), 1)
    adam_sq = jnp.sum(jnp.where(lane == me, totals, 0.0), keepdims=True)
    scale = jnp.sqrt(adam_sq) / (jnp.sqrt(precon_sq) + PRECON_EPS)
    scaled = precon * scale
    for c in range(pieces):
        wide[pl.ds(c, side, stride=pieces), :] = scaled[:, c * LANES : (c + 1) * LANES]
    narrow(sent_back)

    for k in chunks[:2]:
        send_z(k, sent_back, relay_back, 1)
    loads[5].wait()
    left = matmul(block[...], block[...], 1, 1)
    left_stat[...] = STAT_DECAY * left_stat[...] + (1.0 - STAT_DECAY) * left / side
    loads[6].wait()
    right = matmul(block[...], block[...], 0, 0)
    right_stat[...] = STAT_DECAY * right_stat[...] + (1.0 - STAT_DECAY) * right / side
    for i, k in enumerate(chunks):
        send_f(k, relay_back, landed_back, 1)
        if i + 2 < across:
            send_z(chunks[i + 2], sent_back, relay_back, 1)
    wait_all(landed_back, 1)
    wait_sent(sent, relay, 0)
    wait_sent(sent_back, relay_back, 1)
    part = norms_z.at[pl.ds(0, depth - 1)]
    pltpu.make_async_copy(part, part, norm_send.at[0]).wait()
    part = norms_f.at[pl.ds(0, fan - 1)]
    pltpu.make_async_copy(part, part, norm_send.at[1]).wait()


def write(
    landed,
    moment,
    left_stat,
    right_stat,
    order_hbm,
    update_hbm,
    moment_hbm,
    left_hbm,
    right_hbm,
    order,
    wide,
    update,
    sems,
):
    load = pltpu.make_async_copy(order_hbm, order, sems.at[0])
    load.start()
    stores = [
        pltpu.make_async_copy(moment, moment_hbm, sems.at[1]),
        pltpu.make_async_copy(left_stat, left_hbm, sems.at[2]),
        pltpu.make_async_copy(right_stat, right_hbm, sems.at[3]),
    ]
    for store in stores:
        store.start()
    widen(landed, wide)
    load.wait()
    blocks = update.shape[0]
    which = lax.broadcasted_iota(jnp.int32, (blocks, blocks), 0)
    holds = jnp.where(which == order[...], 1.0, 0.0).astype(jnp.bfloat16)
    for c in range(0, SUBLANES, 2):
        pair = jnp.concatenate(
            [wide[pl.ds(c + i, blocks, stride=SUBLANES), :] for i in range(2)], axis=1
        ).astype(jnp.bfloat16)
        columns = pl.ds(c * LANES, 2 * LANES)
        update[:, columns] = matmul(holds, pair).astype(jnp.bfloat16)
        stores.append(
            pltpu.make_async_copy(update.at[:, columns], update_hbm.at[:, columns], sems.at[4 + c // 2])
        )
        stores[-1].start()
    for store in stores:
        store.wait()


def shards(across, grad, moment, order, left_stat, right_stat, left_root, right_root):
    depth = lax.axis_size("group")
    fan = lax.axis_size("fsdp")
    blocks, entries = grad.shape
    side = left_stat.shape[-1]
    f32, bf16 = jnp.float32, jnp.bfloat16
    tile = (SUBLANES, LANES)
    hbm = pl.BlockSpec(memory_space=pltpu.HBM)
    vmem = pl.BlockSpec(memory_space=pltpu.VMEM)
    order = order.reshape(1, blocks)
    entry_shapes = jax.ShapeDtypeStruct((blocks, entries), f32)
    stat_shapes = jax.ShapeDtypeStruct((side, side), f32)
    landed, moment_new, left_new, right_new = pl.pallas_call(
        functools.partial(exchange, depth, across),
        out_shape=(
            jax.ShapeDtypeStruct((depth, fan, *tile), bf16),
            entry_shapes,
            stat_shapes,
            stat_shapes,
        ),
        in_specs=[hbm] * 7,
        out_specs=(vmem,) * 4,
        scratch_shapes=[
            pltpu.VMEM((1, blocks), jnp.int32),
            pltpu.VMEM((blocks, entries), bf16),
            pltpu.VMEM((side, side), bf16),
            pltpu.VMEM((side, side), bf16),
            pltpu.VMEM((blocks * SUBLANES, LANES), f32),
            pltpu.VMEM((blocks, *tile), bf16),
            pltpu.VMEM((fan, depth, *tile), bf16),
            pltpu.VMEM((depth, fan, *tile), bf16),
            pltpu.VMEM((blocks, *tile), bf16),
            pltpu.VMEM((fan, depth, *tile), bf16),
            pltpu.VMEM((side, side), bf16),
            pltpu.VMEM((1, blocks), f32),
            pltpu.VMEM((depth, 1, blocks), f32),
            pltpu.VMEM((1, blocks), f32),
            pltpu.VMEM((fan, 1, blocks), f32),
            pltpu.SemaphoreType.DMA((7,)),
            pltpu.SemaphoreType.DMA((2,)),
            pltpu.SemaphoreType.DMA((2, across)),
            pltpu.SemaphoreType.DMA((2,)),
            pltpu.SemaphoreType.DMA((2,)),
            pltpu.SemaphoreType.DMA((2,)),
            pltpu.SemaphoreType.DMA((2,)),
        ],
        compiler_params=pltpu.CompilerParams(
            collective_id=0, has_side_effects=True, vmem_limit_bytes=40 * 1024 * 1024
        ),
        cost_estimate=pl.CostEstimate(
            flops=8 * side**3 + 2 * blocks * blocks * entries,
            bytes_accessed=6 * blocks * entries + 12 * side * side,
            transcendentals=2 * blocks * entries,
        ),
    )(
        *(
            pltpu.with_memory_space_constraint(operand, pltpu.HBM)
            for operand in (
                grad,
                moment,
                order,
                left_stat[0],
                right_stat[0],
                left_root[0],
                right_root[0],
            )
        )
    )
    update, moment_new, left_new, right_new = pl.pallas_call(
        write,
        out_shape=(
            jax.ShapeDtypeStruct((blocks, entries), bf16),
            entry_shapes,
            stat_shapes,
            stat_shapes,
        ),
        in_specs=[vmem] * 4 + [hbm],
        out_specs=(hbm,) * 4,
        scratch_shapes=[
            pltpu.VMEM((1, blocks), jnp.int32),
            pltpu.VMEM((blocks * SUBLANES, LANES), f32),
            pltpu.VMEM((blocks, entries), bf16),
            pltpu.SemaphoreType.DMA((8,)),
        ],
        compiler_params=pltpu.CompilerParams(vmem_limit_bytes=40 * 1024 * 1024),
        cost_estimate=pl.CostEstimate(
            flops=2 * blocks * blocks * entries,
            bytes_accessed=6 * blocks * entries + 8 * side * side,
            transcendentals=0,
        ),
    )(
        landed,
        moment_new,
        left_new,
        right_new,
        pltpu.with_memory_space_constraint(order, pltpu.HBM),
    )
    return (update, moment_new, left_new[None], right_new[None])


def solution(mesh):
    across = 4 if mesh.shape["fsdp"] == 32 else 2
    placed = (
        P(None, ("group", "fsdp")),
        P(None, ("group", "fsdp")),
        P(),
        P(("group", "fsdp"), None, None),
        P(("group", "fsdp"), None, None),
        P(("group", "fsdp"), None, None),
        P(("group", "fsdp"), None, None),
    )
    return jax.shard_map(
        functools.partial(shards, across),
        mesh=mesh,
        in_specs=placed,
        out_specs=(
            P(None, ("group", "fsdp")),
            P(None, ("group", "fsdp")),
            P(("group", "fsdp"), None, None),
            P(("group", "fsdp"), None, None),
        ),
        check_vma=False,
    )
```

```python
import functools

import jax
import jax.numpy as jnp
from jax import lax
from jax.experimental import pallas as pl
from jax.experimental.pallas import tpu as pltpu
from jax.sharding import PartitionSpec as P

MOMENT_DECAY = 0.95
STAT_DECAY = 0.9
ADAM_EPS = 1e-08
PRECON_EPS = 1e-06

LANES = 128
SUBLANES = 8
MESH = pl.DeviceIdType.MESH


def matmul(a, b, a_dim=1, b_dim=0):
    return lax.dot_general(
        a, b, (((a_dim,), (b_dim,)), ((), ())), preferred_element_type=jnp.float32
    )


def widen(source, wide):
    depth, fan = source.shape[:2]
    step = min(fan, 32)
    for i in range(depth):
        for j in range(0, fan, step):
            part = source[i, j : j + step].astype(jnp.float32)
            start = (i * fan + j) * SUBLANES
            wide[start : start + step * SUBLANES, :] = part.reshape(step * SUBLANES, LANES)


def alternate(count):
    return sorted(range(1, count), key=lambda k: (-min(k, count - k), k))


def exchange(
    depth,
    across,
    grad_hbm,
    moment_hbm,
    order_hbm,
    left_stat_hbm,
    right_stat_hbm,
    left_root_hbm,
    right_root_hbm,
    landed_back,
    moment,
    left_stat,
    right_stat,
    order,
    grad,
    left_root,
    right_root,
    wide,
    sent,
    relay,
    landed,
    sent_back,
    relay_back,
    block,
    norms,
    norms_z,
    norms_z_sum,
    norms_f,
    hop,
    hop_back,
    load_sem,
    z_send,
    z_recv,
    hop_recv,
    f_send,
    f_recv,
    norm_send,
    norm_recv,
):
    fan = relay.shape[0]
    row = fan // across
    blocks = depth * fan
    side = block.shape[0]
    pieces = side // LANES
    g = lax.axis_index("group")
    f = lax.axis_index("fsdp")
    x = f // row
    me = g * fan + f
    hops = int(depth % 4 == 0)
    leg = depth // 4 + f % 2 * (depth // 2)

    loads = [
        pltpu.make_async_copy(source, target, load_sem.at[i])
        for i, (source, target) in enumerate(
            (
                (order_hbm, order),
                (grad_hbm, grad),
                (moment_hbm, moment),
                (left_root_hbm, left_root),
                (right_root_hbm, right_root),
                (left_stat_hbm, left_stat),
                (right_stat_hbm, right_stat),
            )
        )
    ]
    for load in loads:
        load.start()

    barrier = pltpu.get_barrier_semaphore()

    def greet_z(k, carry):
        pl.semaphore_signal(barrier, inc=1, device_id=((g + k) % depth, f), device_id_type=MESH)
        return carry

    def greet_f(k, carry):
        pl.semaphore_signal(barrier, inc=1, device_id=(g, (f + k) % fan), device_id_type=MESH)
        return carry

    lax.fori_loop(1, depth, greet_z, 0)
    lax.fori_loop(1, fan, greet_f, 0)

    loads[0].wait()
    which = lax.broadcasted_iota(jnp.int32, (blocks, blocks), 0)
    holds = jnp.where(which == order[...], 1.0, 0.0)
    slots_half = holds.T.astype(jnp.bfloat16)

    def narrow(target):
        step = min(blocks, 32)
        for i in range(0, blocks, step):
            part = wide[i * SUBLANES : (i + step) * SUBLANES, :]
            target[i : i + step] = part.reshape(step, SUBLANES, LANES).astype(jnp.bfloat16)

    def chunk_of(k):
        return ((x + k) % across) * row

    def send_z(k, source, through, way):
        start = chunk_of(k)

        for j in alternate(depth):
            if hops and j == depth // 2:
                continue
            to = (g + j) % depth
            pltpu.make_async_remote_copy(
                src_ref=source.at[pl.ds(to * fan + start, row)],
                dst_ref=through.at[pl.ds(start, row), g],
                send_sem=z_send.at[way],
                recv_sem=z_recv.at[way, k],
                device_id=(to, f),
                device_id_type=MESH,
            ).start()
        pltpu.make_async_copy(
            source.at[pl.ds(g * fan + start, row)],
            through.at[pl.ds(start, row), g],
            z_recv.at[way, k],
        ).start()

    def send_hop(source, hop, way):
        pltpu.make_async_remote_copy(
            src_ref=source.at[pl.ds((g + depth // 2) % depth * fan, fan)],
            dst_ref=hop,
            send_sem=z_send.at[way],
            recv_sem=hop_recv.at[way],
            device_id=((g + leg) % depth, f),
            device_id_type=MESH,
        ).start()

    def pass_on(hop, through, way):
        pltpu.make_async_copy(hop, hop, hop_recv.at[way]).wait()
        for k in chunks:
            rows = pl.ds(chunk_of(k), row)
            pltpu.make_async_remote_copy(
                src_ref=hop.at[rows],
                dst_ref=through.at[rows, (g + depth - leg) % depth],
                send_sem=z_send.at[way],
                recv_sem=z_recv.at[way, k],
                device_id=((g + leg) % depth, f),
                device_id_type=MESH,
            ).start()

    def send_z_all(source, hop, through, way):
        if hops:
            send_hop(source, hop, way)
        for i, k in enumerate(chunks):
            send_z(k, source, through, way)
            if hops and i == 1:
                pass_on(hop, through, way)

    def send_f(k, through, target, way):
        start = chunk_of(k)
        arrived = through.at[pl.ds(start, row)]
        pltpu.make_async_copy(arrived, arrived, z_recv.at[way, k]).wait()
        place = f % row

        for j in alternate(row) + ([] if k == 0 else [0]):
            to = start + (place + j) % row
            pltpu.make_async_remote_copy(
                src_ref=through.at[to],
                dst_ref=target.at[:, f],
                send_sem=f_send.at[way],
                recv_sem=f_recv.at[way],
                device_id=(g, to),
                device_id_type=MESH,
            ).start()
        if k == 0:
            pltpu.make_async_copy(through.at[f], target.at[:, f], f_recv.at[way]).start()

    def wait_all(target, way):
        pltpu.make_async_copy(target, target, f_recv.at[way]).wait()

    def wait_sent(source, through, way):
        part = source.at[pl.ds(0, (depth - 1 + hops) * fan)]
        pltpu.make_async_copy(part, part, z_send.at[way]).wait()
        part = through.at[pl.ds(0, fan - 1)]
        pltpu.make_async_copy(part, part, f_send.at[way]).wait()

    chunks = sorted(range(across), key=lambda k: -min(k, across - k))

    loads[1].wait()
    for c in range(0, SUBLANES, 2):
        pair = matmul(slots_half, grad[:, c * LANES : (c + 2) * LANES])
        wide[pl.ds(c, blocks, stride=SUBLANES), :] = pair[:, :LANES]
        wide[pl.ds(c + 1, blocks, stride=SUBLANES), :] = pair[:, LANES:]
    narrow(sent)
    pl.semaphore_wait(barrier, depth - 1 + fan - 1)
    send_z_all(sent, hop, relay, 0)

    loads[2].wait()
    tall = min(blocks, 32)
    share = jnp.zeros((1, blocks), jnp.float32)
    for i in range(0, blocks, tall):
        rows = pl.ds(i, tall)
        gradient = grad[rows, :].astype(jnp.float32)
        second = MOMENT_DECAY * moment[rows, :] + (1.0 - MOMENT_DECAY) * gradient * gradient
        moment[rows, :] = second
        direction = gradient / (jnp.sqrt(second) + ADAM_EPS)
        squares = jnp.sum(direction * direction, axis=1, keepdims=True)
        share = share + jnp.sum(holds[i : i + tall, :] * squares, axis=0, keepdims=True)
    norms[...] = share
    for k in chunks:
        send_f(k, relay, landed, 0)

    def norm_z(j, carry):
        pltpu.make_async_remote_copy(
            src_ref=norms,
            dst_ref=norms_z.at[g],
            send_sem=norm_send.at[0],
            recv_sem=norm_recv.at[0],
            device_id=((g + j) % depth, f),
            device_id_type=MESH,
        ).start()
        return carry

    lax.fori_loop(1, depth, norm_z, 0)
    pltpu.make_async_copy(norms, norms_z.at[g], norm_recv.at[0]).start()
    pltpu.make_async_copy(norms_z, norms_z, norm_recv.at[0]).wait()
    norms_z_sum[...] = jnp.sum(norms_z[...], axis=0)

    def norm_f(j, carry):
        pltpu.make_async_remote_copy(
            src_ref=norms_z_sum,
            dst_ref=norms_f.at[f],
            send_sem=norm_send.at[1],
            recv_sem=norm_recv.at[1],
            device_id=(g, (f + j) % fan),
            device_id_type=MESH,
        ).start()
        return carry

    lax.fori_loop(1, fan, norm_f, 0)
    pltpu.make_async_copy(norms_z_sum, norms_f.at[f], norm_recv.at[1]).start()

    wait_all(landed, 0)
    widen(landed, wide)
    for c in range(pieces):
        block[:, c * LANES : (c + 1) * LANES] = wide[pl.ds(c, side, stride=pieces), :].astype(
            jnp.bfloat16
        )
    loads[3].wait()
    loads[4].wait()
    half = matmul(left_root[...], block[...]).astype(jnp.bfloat16)
    full = matmul(half, right_root[...])
    precon_sq = jnp.sum(full * full, keepdims=True)
    precon = full.astype(jnp.bfloat16).astype(jnp.float32)
    pltpu.make_async_copy(norms_f, norms_f, norm_recv.at[1]).wait()
    totals = jnp.sum(norms_f[...], axis=0)
    lane = lax.broadcasted_iota(jnp.int32, (1, blocks), 1)
    adam_sq = jnp.sum(jnp.where(lane == me, totals, 0.0), keepdims=True)
    scale = jnp.sqrt(adam_sq) / (jnp.sqrt(precon_sq) + PRECON_EPS)
    scaled = precon * scale
    for c in range(pieces):
        wide[pl.ds(c, side, stride=pieces), :] = scaled[:, c * LANES : (c + 1) * LANES]
    narrow(sent_back)

    send_z_all(sent_back, hop_back, relay_back, 1)
    loads[5].wait()
    left = matmul(block[...], block[...], 1, 1)
    left_stat[...] = STAT_DECAY * left_stat[...] + (1.0 - STAT_DECAY) * left / side
    loads[6].wait()
    right = matmul(block[...], block[...], 0, 0)
    right_stat[...] = STAT_DECAY * right_stat[...] + (1.0 - STAT_DECAY) * right / side
    for k in chunks:
        send_f(k, relay_back, landed_back, 1)
    wait_all(landed_back, 1)
    wait_sent(sent, relay, 0)
    wait_sent(sent_back, relay_back, 1)
    part = norms_z.at[pl.ds(0, depth - 1)]
    pltpu.make_async_copy(part, part, norm_send.at[0]).wait()
    part = norms_f.at[pl.ds(0, fan - 1)]
    pltpu.make_async_copy(part, part, norm_send.at[1]).wait()


def write(
    landed,
    moment,
    left_stat,
    right_stat,
    order_hbm,
    update_hbm,
    moment_hbm,
    left_hbm,
    right_hbm,
    order,
    wide,
    update,
    sems,
):
    load = pltpu.make_async_copy(order_hbm, order, sems.at[0])
    load.start()
    stores = [
        pltpu.make_async_copy(moment, moment_hbm, sems.at[1]),
        pltpu.make_async_copy(left_stat, left_hbm, sems.at[2]),
        pltpu.make_async_copy(right_stat, right_hbm, sems.at[3]),
    ]
    for store in stores:
        store.start()
    widen(landed, wide)
    load.wait()
    blocks = update.shape[0]
    which = lax.broadcasted_iota(jnp.int32, (blocks, blocks), 0)
    holds = jnp.where(which == order[...], 1.0, 0.0).astype(jnp.bfloat16)
    for c in range(0, SUBLANES, 2):
        pair = jnp.concatenate(
            [wide[pl.ds(c + i, blocks, stride=SUBLANES), :] for i in range(2)], axis=1
        ).astype(jnp.bfloat16)
        columns = pl.ds(c * LANES, 2 * LANES)
        update[:, columns] = matmul(holds, pair).astype(jnp.bfloat16)
        stores.append(
            pltpu.make_async_copy(update.at[:, columns], update_hbm.at[:, columns], sems.at[4 + c // 2])
        )
        stores[-1].start()
    for store in stores:
        store.wait()


def shards(across, grad, moment, order, left_stat, right_stat, left_root, right_root):
    depth = lax.axis_size("group")
    fan = lax.axis_size("fsdp")
    blocks, entries = grad.shape
    side = left_stat.shape[-1]
    f32, bf16 = jnp.float32, jnp.bfloat16
    tile = (SUBLANES, LANES)
    hbm = pl.BlockSpec(memory_space=pltpu.HBM)
    vmem = pl.BlockSpec(memory_space=pltpu.VMEM)
    order = order.reshape(1, blocks)
    entry_shapes = jax.ShapeDtypeStruct((blocks, entries), f32)
    stat_shapes = jax.ShapeDtypeStruct((side, side), f32)
    landed, moment_new, left_new, right_new = pl.pallas_call(
        functools.partial(exchange, depth, across),
        out_shape=(
            jax.ShapeDtypeStruct((depth, fan, *tile), bf16),
            entry_shapes,
            stat_shapes,
            stat_shapes,
        ),
        in_specs=[hbm] * 7,
        out_specs=(vmem,) * 4,
        scratch_shapes=[
            pltpu.VMEM((1, blocks), jnp.int32),
            pltpu.VMEM((blocks, entries), bf16),
            pltpu.VMEM((side, side), bf16),
            pltpu.VMEM((side, side), bf16),
            pltpu.VMEM((blocks * SUBLANES, LANES), f32),
            pltpu.VMEM((blocks, *tile), bf16),
            pltpu.VMEM((fan, depth, *tile), bf16),
            pltpu.VMEM((depth, fan, *tile), bf16),
            pltpu.VMEM((blocks, *tile), bf16),
            pltpu.VMEM((fan, depth, *tile), bf16),
            pltpu.VMEM((side, side), bf16),
            pltpu.VMEM((1, blocks), f32),
            pltpu.VMEM((depth, 1, blocks), f32),
            pltpu.VMEM((1, blocks), f32),
            pltpu.VMEM((fan, 1, blocks), f32),
            pltpu.VMEM((fan, *tile), bf16),
            pltpu.VMEM((fan, *tile), bf16),
            pltpu.SemaphoreType.DMA((7,)),
            pltpu.SemaphoreType.DMA((2,)),
            pltpu.SemaphoreType.DMA((2, across)),
            pltpu.SemaphoreType.DMA((2,)),
            pltpu.SemaphoreType.DMA((2,)),
            pltpu.SemaphoreType.DMA((2,)),
            pltpu.SemaphoreType.DMA((2,)),
            pltpu.SemaphoreType.DMA((2,)),
        ],
        compiler_params=pltpu.CompilerParams(
            collective_id=0, has_side_effects=True, vmem_limit_bytes=40 * 1024 * 1024
        ),
        cost_estimate=pl.CostEstimate(
            flops=8 * side**3 + 2 * blocks * blocks * entries,
            bytes_accessed=6 * blocks * entries + 12 * side * side,
            transcendentals=2 * blocks * entries,
        ),
    )(
        *(
            pltpu.with_memory_space_constraint(operand, pltpu.HBM)
            for operand in (
                grad,
                moment,
                order,
                left_stat[0],
                right_stat[0],
                left_root[0],
                right_root[0],
            )
        )
    )
    update, moment_new, left_new, right_new = pl.pallas_call(
        write,
        out_shape=(
            jax.ShapeDtypeStruct((blocks, entries), bf16),
            entry_shapes,
            stat_shapes,
            stat_shapes,
        ),
        in_specs=[vmem] * 4 + [hbm],
        out_specs=(hbm,) * 4,
        scratch_shapes=[
            pltpu.VMEM((1, blocks), jnp.int32),
            pltpu.VMEM((blocks * SUBLANES, LANES), f32),
            pltpu.VMEM((blocks, entries), bf16),
            pltpu.SemaphoreType.DMA((8,)),
        ],
        compiler_params=pltpu.CompilerParams(vmem_limit_bytes=40 * 1024 * 1024),
        cost_estimate=pl.CostEstimate(
            flops=2 * blocks * blocks * entries,
            bytes_accessed=6 * blocks * entries + 8 * side * side,
            transcendentals=0,
        ),
    )(
        landed,
        moment_new,
        left_new,
        right_new,
        pltpu.with_memory_space_constraint(order, pltpu.HBM),
    )
    return (update, moment_new, left_new[None], right_new[None])


def solution(mesh):
    across = 4 if mesh.shape["fsdp"] == 32 else 2
    placed = (
        P(None, ("group", "fsdp")),
        P(None, ("group", "fsdp")),
        P(),
        P(("group", "fsdp"), None, None),
        P(("group", "fsdp"), None, None),
        P(("group", "fsdp"), None, None),
        P(("group", "fsdp"), None, None),
    )
    return jax.shard_map(
        functools.partial(shards, across),
        mesh=mesh,
        in_specs=placed,
        out_specs=(
            P(None, ("group", "fsdp")),
            P(None, ("group", "fsdp")),
            P(("group", "fsdp"), None, None),
            P(("group", "fsdp"), None, None),
        ),
        check_vma=False,
    )
```

```python
import functools

import jax
import jax.numpy as jnp
from jax import lax
from jax.experimental import pallas as pl
from jax.experimental.pallas import tpu as pltpu
from jax.sharding import PartitionSpec as P

MOMENT_DECAY = 0.95
STAT_DECAY = 0.9
ADAM_EPS = 1e-08
PRECON_EPS = 1e-06

LANES = 128
SUBLANES = 8
MESH = pl.DeviceIdType.MESH


def matmul(a, b, a_dim=1, b_dim=0):
    return lax.dot_general(
        a, b, (((a_dim,), (b_dim,)), ((), ())), preferred_element_type=jnp.float32
    )


def widen(source, wide, start, row):
    fan, depth = source.shape[:2]
    for i in range(depth):
        part = source[pl.ds(start, row), i].astype(jnp.float32)
        first = (i * fan + start) * SUBLANES
        wide[pl.ds(first, row * SUBLANES), :] = part.reshape(row * SUBLANES, LANES)


def alternate(count):
    return sorted(range(1, count), key=lambda k: (-min(k, count - k), k))


def exchange(
    depth,
    across,
    grad_hbm,
    moment_hbm,
    order_hbm,
    left_stat_hbm,
    right_stat_hbm,
    left_root_hbm,
    right_root_hbm,
    landed_back,
    moment,
    left_stat,
    right_stat,
    order,
    grad,
    left_root,
    right_root,
    wide,
    sent,
    relay,
    staged,
    landed,
    sent_back,
    relay_back,
    staged_back,
    block,
    norms,
    norms_z,
    norms_z_sum,
    norms_f,
    load_sem,
    z_send,
    z_recv,
    f_send,
    f_recv,
    norm_send,
    norm_recv,
):
    fan = relay.shape[1]
    row = fan // across
    blocks = depth * fan
    side = block.shape[0]
    pieces = side // LANES
    g = lax.axis_index("group")
    f = lax.axis_index("fsdp")
    x = f // row
    me = g * fan + f

    loads = [
        pltpu.make_async_copy(source, target, load_sem.at[i])
        for i, (source, target) in enumerate(
            (
                (order_hbm, order),
                (grad_hbm, grad),
                (moment_hbm, moment),
                (left_root_hbm, left_root),
                (right_root_hbm, right_root),
                (left_stat_hbm, left_stat),
                (right_stat_hbm, right_stat),
            )
        )
    ]
    for load in loads:
        load.start()

    barrier = pltpu.get_barrier_semaphore()

    def greet_z(k, carry):
        pl.semaphore_signal(barrier, inc=1, device_id=((g + k) % depth, f), device_id_type=MESH)
        return carry

    def greet_f(k, carry):
        pl.semaphore_signal(barrier, inc=1, device_id=(g, (f + k) % fan), device_id_type=MESH)
        return carry

    lax.fori_loop(1, depth, greet_z, 0)
    lax.fori_loop(1, fan, greet_f, 0)

    loads[0].wait()
    which = lax.broadcasted_iota(jnp.int32, (blocks, blocks), 0)
    holds = jnp.where(which == order[...], 1.0, 0.0)
    slots_half = holds.T.astype(jnp.bfloat16)

    def narrow(target):
        step = min(blocks, 32)
        for i in range(0, blocks, step):
            part = wide[i * SUBLANES : (i + step) * SUBLANES, :]
            target[i : i + step] = part.reshape(step, SUBLANES, LANES).astype(jnp.bfloat16)

    def chunk_of(k):
        return pl.multiple_of(((x + k) % across) * row, row)

    def send_z(k, source, through, way):
        start = chunk_of(k)
        for j in alternate(depth):
            to = (g + j) % depth
            pltpu.make_async_remote_copy(
                src_ref=source.at[pl.ds(to * fan + start, row)],
                dst_ref=through.at[g, pl.ds(start, row)],
                send_sem=z_send.at[way],
                recv_sem=z_recv.at[way, k],
                device_id=(to, f),
                device_id_type=MESH,
            ).start()

    def send_f(k, source, through, turned, target, way):
        start = chunk_of(k)
        arrived = through.at[pl.ds(0, depth - 1), pl.ds(start, row)]
        pltpu.make_async_copy(arrived, arrived, z_recv.at[way, k]).wait()
        through[g, pl.ds(start, row)] = source[pl.ds(g * fan + start, row)]
        for i in range(depth):
            turned[pl.ds(start, row), i] = through[i, pl.ds(start, row)]
        place = f % row
        for j in alternate(row) + ([] if k == 0 else [0]):
            to = start + (place + j) % row
            pltpu.make_async_remote_copy(
                src_ref=turned.at[to],
                dst_ref=target.at[f],
                send_sem=f_send.at[way],
                recv_sem=f_recv.at[way, k],
                device_id=(g, to),
                device_id_type=MESH,
            ).start()

    def wait_chunk(k, turned, target, way):
        start = pl.multiple_of(((x + across - k) % across) * row, row)
        arrived = target.at[pl.ds(0, row - (k == 0))]
        pltpu.make_async_copy(arrived, arrived, f_recv.at[way, k]).wait()
        if k == 0:
            target[f] = turned[f]
        return start

    def wait_sent(source, through, way):
        part = source.at[pl.ds(0, (depth - 1) * fan)]
        pltpu.make_async_copy(part, part, z_send.at[way]).wait()
        part = through.at[pl.ds(0, fan - 1)]
        pltpu.make_async_copy(part, part, f_send.at[way]).wait()

    chunks = sorted(range(across), key=lambda k: -min(k, across - k))

    loads[1].wait()
    for c in range(0, SUBLANES, 2):
        pair = matmul(slots_half, grad[:, c * LANES : (c + 2) * LANES])
        wide[pl.ds(c, blocks, stride=SUBLANES), :] = pair[:, :LANES]
        wide[pl.ds(c + 1, blocks, stride=SUBLANES), :] = pair[:, LANES:]
    narrow(sent)
    pl.semaphore_wait(barrier, depth - 1 + fan - 1)
    for k in chunks:
        send_z(k, sent, relay, 0)

    loads[2].wait()
    tall = min(blocks, 32)
    share = jnp.zeros((1, blocks), jnp.float32)
    for i in range(0, blocks, tall):
        rows = pl.ds(i, tall)
        gradient = grad[rows, :].astype(jnp.float32)
        second = MOMENT_DECAY * moment[rows, :] + (1.0 - MOMENT_DECAY) * gradient * gradient
        moment[rows, :] = second
        direction = gradient / (jnp.sqrt(second) + ADAM_EPS)
        squares = jnp.sum(direction * direction, axis=1, keepdims=True)
        share = share + jnp.sum(holds[i : i + tall, :] * squares, axis=0, keepdims=True)
    norms[...] = share
    def norm_z(j, carry):
        pltpu.make_async_remote_copy(
            src_ref=norms,
            dst_ref=norms_z.at[g],
            send_sem=norm_send.at[0],
            recv_sem=norm_recv.at[0],
            device_id=((g + j) % depth, f),
            device_id_type=MESH,
        ).start()
        return carry

    lax.fori_loop(1, depth, norm_z, 0)

    def norm_f(j, carry):
        pltpu.make_async_remote_copy(
            src_ref=norms_z_sum,
            dst_ref=norms_f.at[f],
            send_sem=norm_send.at[1],
            recv_sem=norm_recv.at[1],
            device_id=(g, (f + j) % fan),
            device_id_type=MESH,
        ).start()
        return carry

    for i, k in enumerate(chunks):
        send_f(k, sent, relay, staged, landed, 0)
        if i == min(1, across - 1):
            arrived = norms_z.at[pl.ds(0, depth - 1)]
            pltpu.make_async_copy(arrived, arrived, norm_recv.at[0]).wait()
            norms_z[g] = norms[...]
            norms_z_sum[...] = jnp.sum(norms_z[...], axis=0)
            lax.fori_loop(1, fan, norm_f, 0)

    for k in chunks:
        start = wait_chunk(k, staged, landed, 0)
        widen(landed, wide, start, row)
        tall = row * SUBLANES // pieces
        for i in range(depth):
            first = (i * fan + start) * SUBLANES
            rows = pl.ds(pl.multiple_of((i * fan + start) * SUBLANES // pieces, tall), tall)
            for c in range(pieces):
                block[rows, c * LANES : (c + 1) * LANES] = wide[
                    pl.ds(first + c, tall, stride=pieces), :
                ].astype(jnp.bfloat16)
    loads[3].wait()
    loads[4].wait()
    half = matmul(left_root[...], block[...]).astype(jnp.bfloat16)
    full = matmul(half, right_root[...])
    precon_sq = jnp.sum(full * full, keepdims=True)
    precon = full.astype(jnp.bfloat16).astype(jnp.float32)
    arrived = norms_f.at[pl.ds(0, fan - 1)]
    pltpu.make_async_copy(arrived, arrived, norm_recv.at[1]).wait()
    norms_f[f] = norms_z_sum[...]
    totals = jnp.sum(norms_f[...], axis=0)
    lane = lax.broadcasted_iota(jnp.int32, (1, blocks), 1)
    adam_sq = jnp.sum(jnp.where(lane == me, totals, 0.0), keepdims=True)
    scale = jnp.sqrt(adam_sq) / (jnp.sqrt(precon_sq) + PRECON_EPS)
    scaled = precon * scale
    for c in range(pieces):
        wide[pl.ds(c, side, stride=pieces), :] = scaled[:, c * LANES : (c + 1) * LANES]
    narrow(sent_back)

    for k in chunks:
        send_z(k, sent_back, relay_back, 1)
    loads[5].wait()
    left = matmul(block[...], block[...], 1, 1)
    left_stat[...] = STAT_DECAY * left_stat[...] + (1.0 - STAT_DECAY) * left / side
    loads[6].wait()
    right = matmul(block[...], block[...], 0, 0)
    right_stat[...] = STAT_DECAY * right_stat[...] + (1.0 - STAT_DECAY) * right / side
    for k in chunks:
        send_f(k, sent_back, relay_back, staged_back, landed_back, 1)
    for k in chunks:
        wait_chunk(k, staged_back, landed_back, 1)
    wait_sent(sent, staged, 0)
    wait_sent(sent_back, staged_back, 1)
    part = norms_z.at[pl.ds(0, depth - 1)]
    pltpu.make_async_copy(part, part, norm_send.at[0]).wait()
    part = norms_f.at[pl.ds(0, fan - 1)]
    pltpu.make_async_copy(part, part, norm_send.at[1]).wait()


def write(
    landed,
    moment,
    left_stat,
    right_stat,
    order_hbm,
    update_hbm,
    moment_hbm,
    left_hbm,
    right_hbm,
    order,
    wide,
    update,
    sems,
):
    load = pltpu.make_async_copy(order_hbm, order, sems.at[0])
    load.start()
    stores = [
        pltpu.make_async_copy(moment, moment_hbm, sems.at[1]),
        pltpu.make_async_copy(left_stat, left_hbm, sems.at[2]),
        pltpu.make_async_copy(right_stat, right_hbm, sems.at[3]),
    ]
    for store in stores:
        store.start()
    widen(landed, wide, 0, landed.shape[0])
    load.wait()
    blocks = update.shape[0]
    which = lax.broadcasted_iota(jnp.int32, (blocks, blocks), 0)
    holds = jnp.where(which == order[...], 1.0, 0.0).astype(jnp.bfloat16)
    for c in range(0, SUBLANES, 2):
        pair = jnp.concatenate(
            [wide[pl.ds(c + i, blocks, stride=SUBLANES), :] for i in range(2)], axis=1
        ).astype(jnp.bfloat16)
        columns = pl.ds(c * LANES, 2 * LANES)
        update[:, columns] = matmul(holds, pair).astype(jnp.bfloat16)
        stores.append(
            pltpu.make_async_copy(update.at[:, columns], update_hbm.at[:, columns], sems.at[4 + c // 2])
        )
        stores[-1].start()
    for store in stores:
        store.wait()


def shards(across, grad, moment, order, left_stat, right_stat, left_root, right_root):
    depth = lax.axis_size("group")
    fan = lax.axis_size("fsdp")
    blocks, entries = grad.shape
    side = left_stat.shape[-1]
    f32, bf16 = jnp.float32, jnp.bfloat16
    tile = (SUBLANES, LANES)
    hbm = pl.BlockSpec(memory_space=pltpu.HBM)
    vmem = pl.BlockSpec(memory_space=pltpu.VMEM)
    order = order.reshape(1, blocks)
    entry_shapes = jax.ShapeDtypeStruct((blocks, entries), f32)
    stat_shapes = jax.ShapeDtypeStruct((side, side), f32)
    landed, moment_new, left_new, right_new = pl.pallas_call(
        functools.partial(exchange, depth, across),
        out_shape=(
            jax.ShapeDtypeStruct((fan, depth, *tile), bf16),
            entry_shapes,
            stat_shapes,
            stat_shapes,
        ),
        in_specs=[hbm] * 7,
        out_specs=(vmem,) * 4,
        scratch_shapes=[
            pltpu.VMEM((1, blocks), jnp.int32),
            pltpu.VMEM((blocks, entries), bf16),
            pltpu.VMEM((side, side), bf16),
            pltpu.VMEM((side, side), bf16),
            pltpu.VMEM((blocks * SUBLANES, LANES), f32),
            pltpu.VMEM((blocks, *tile), bf16),
            pltpu.VMEM((depth, fan, *tile), bf16),
            pltpu.VMEM((fan, depth, *tile), bf16),
            pltpu.VMEM((fan, depth, *tile), bf16),
            pltpu.VMEM((blocks, *tile), bf16),
            pltpu.VMEM((depth, fan, *tile), bf16),
            pltpu.VMEM((fan, depth, *tile), bf16),
            pltpu.VMEM((side, side), bf16),
            pltpu.VMEM((1, blocks), f32),
            pltpu.VMEM((depth, 1, blocks), f32),
            pltpu.VMEM((1, blocks), f32),
            pltpu.VMEM((fan, 1, blocks), f32),
            pltpu.SemaphoreType.DMA((7,)),
            pltpu.SemaphoreType.DMA((2,)),
            pltpu.SemaphoreType.DMA((2, across)),
            pltpu.SemaphoreType.DMA((2,)),
            pltpu.SemaphoreType.DMA((2, across)),
            pltpu.SemaphoreType.DMA((2,)),
            pltpu.SemaphoreType.DMA((2,)),
        ],
        compiler_params=pltpu.CompilerParams(
            collective_id=0, has_side_effects=True, vmem_limit_bytes=40 * 1024 * 1024
        ),
        cost_estimate=pl.CostEstimate(
            flops=8 * side**3 + 2 * blocks * blocks * entries,
            bytes_accessed=6 * blocks * entries + 12 * side * side,
            transcendentals=2 * blocks * entries,
        ),
    )(
        *(
            pltpu.with_memory_space_constraint(operand, pltpu.HBM)
            for operand in (
                grad,
                moment,
                order,
                left_stat[0],
                right_stat[0],
                left_root[0],
                right_root[0],
            )
        )
    )
    update, moment_new, left_new, right_new = pl.pallas_call(
        write,
        out_shape=(
            jax.ShapeDtypeStruct((blocks, entries), bf16),
            entry_shapes,
            stat_shapes,
            stat_shapes,
        ),
        in_specs=[vmem] * 4 + [hbm],
        out_specs=(hbm,) * 4,
        scratch_shapes=[
            pltpu.VMEM((1, blocks), jnp.int32),
            pltpu.VMEM((blocks * SUBLANES, LANES), f32),
            pltpu.VMEM((blocks, entries), bf16),
            pltpu.SemaphoreType.DMA((8,)),
        ],
        compiler_params=pltpu.CompilerParams(vmem_limit_bytes=40 * 1024 * 1024),
        cost_estimate=pl.CostEstimate(
            flops=2 * blocks * blocks * entries,
            bytes_accessed=6 * blocks * entries + 8 * side * side,
            transcendentals=0,
        ),
    )(
        landed,
        moment_new,
        left_new,
        right_new,
        pltpu.with_memory_space_constraint(order, pltpu.HBM),
    )
    return (update, moment_new, left_new[None], right_new[None])


def solution(mesh):
    across = 4 if mesh.shape["fsdp"] == 32 else 2
    placed = (
        P(None, ("group", "fsdp")),
        P(None, ("group", "fsdp")),
        P(),
        P(("group", "fsdp"), None, None),
        P(("group", "fsdp"), None, None),
        P(("group", "fsdp"), None, None),
        P(("group", "fsdp"), None, None),
    )
    return jax.shard_map(
        functools.partial(shards, across),
        mesh=mesh,
        in_specs=placed,
        out_specs=(
            P(None, ("group", "fsdp")),
            P(None, ("group", "fsdp")),
            P(("group", "fsdp"), None, None),
            P(("group", "fsdp"), None, None),
        ),
        check_vma=False,
    )
```

```python
import functools

import jax
import jax.numpy as jnp
from jax import lax
from jax.experimental import pallas as pl
from jax.experimental.pallas import tpu as pltpu
from jax.sharding import PartitionSpec as P

MOMENT_DECAY = 0.95
STAT_DECAY = 0.9
ADAM_EPS = 1e-08
PRECON_EPS = 1e-06

LANES = 128
SUBLANES = 8
MESH = pl.DeviceIdType.MESH


def matmul(a, b, a_dim=1, b_dim=0):
    return lax.dot_general(
        a, b, (((a_dim,), (b_dim,)), ((), ())), preferred_element_type=jnp.float32
    )


def alternate(count):
    return sorted(range(1, count), key=lambda k: (-min(k, count - k), k))


def exchange(
    depth,
    across,
    grad_hbm,
    moment_hbm,
    order_hbm,
    left_stat_hbm,
    right_stat_hbm,
    left_root_hbm,
    right_root_hbm,
    wide_back,
    totals,
    moment,
    left_stat,
    right_stat,
    order,
    grad,
    left_root,
    right_root,
    wide,
    sent,
    via_z,
    turned_z,
    landed_xy,
    turned_xy,
    via_xy,
    turned_back,
    landed_z,
    block,
    norms,
    norms_z,
    norms_z_sum,
    norms_f,
    load_sem,
    z_send,
    z_recv,
    xy_send,
    xy_recv,
    norm_send,
    norm_recv,
):
    plane = via_xy.shape[1]
    deep = plane // across
    fan = plane * 2
    blocks = depth * fan
    side = block.shape[0]
    pieces = side // LANES
    g = lax.axis_index("group")
    f = lax.axis_index("fsdp")
    xy = f // 2
    core = f % 2
    x = xy // deep
    y = xy % deep
    me = g * fan + f

    loads = [
        pltpu.make_async_copy(source, target, load_sem.at[i])
        for i, (source, target) in enumerate(
            (
                (order_hbm, order),
                (grad_hbm, grad),
                (moment_hbm, moment),
                (left_root_hbm, left_root),
                (right_root_hbm, right_root),
                (left_stat_hbm, left_stat),
                (right_stat_hbm, right_stat),
            )
        )
    ]
    for load in loads:
        load.start()

    barrier = pltpu.get_barrier_semaphore()

    def greet_z(k, carry):
        to = lax.rem(g + k, depth)
        pl.semaphore_signal(barrier, inc=1, device_id=(to, f), device_id_type=MESH)
        return carry

    def greet_f(k, carry):
        to = lax.rem(f + k, fan)
        pl.semaphore_signal(barrier, inc=1, device_id=(g, to), device_id_type=MESH)
        return carry

    lax.fori_loop(1, depth, greet_z, 0)
    lax.fori_loop(1, fan, greet_f, 0)

    loads[0].wait()
    which = lax.broadcasted_iota(jnp.int32, (blocks, blocks), 0)
    holds = jnp.where(which == order[...], 1.0, 0.0)
    slots_half = holds.T.astype(jnp.bfloat16)

    def narrow():
        rows = fan * SUBLANES
        for i in range(depth):
            part = wide[i * rows : (i + 1) * rows, :].reshape(plane, 2, SUBLANES, LANES)
            for c in range(2):
                sent[way, c, i] = part[:, c].astype(jnp.bfloat16)

    def widen(target, i, c, part):
        part = part.astype(jnp.float32)
        first = pl.multiple_of((i * fan + c) * SUBLANES, SUBLANES)
        for j in range(plane):
            target[pl.ds(first + j * 2 * SUBLANES, SUBLANES), :] = part[j]

    near_first = sorted(
        range(1, plane),
        key=lambda j: (
            min(j // deep, across - j // deep) + min(j % deep, deep - j % deep),
            j,
        ),
    )

    def place(j):
        tx = lax.rem(x + j // deep, across)
        ty = lax.rem(y + j % deep, deep)
        return tx * deep + ty

    def send_z(source, target, half):
        for j in alternate(depth):
            to = lax.rem(g + j, depth)
            pltpu.make_async_remote_copy(
                src_ref=source(to),
                dst_ref=target.at[way, g],
                send_sem=z_send.at[way, half],
                recv_sem=z_recv.at[way, half],
                device_id=(to, f),
                device_id_type=MESH,
            ).start()

    def send_xy(source, target, half, to_core, places):
        for j in places:
            to = place(j)
            pltpu.make_async_remote_copy(
                src_ref=source.at[way, to],
                dst_ref=target.at[way, xy],
                send_sem=xy_send.at[way, half],
                recv_sem=xy_recv.at[way, half],
                device_id=(g, to * 2 + to_core),
                device_id_type=MESH,
            ).start()

    def wait(part, sem):
        pltpu.make_async_copy(part, part, sem).wait()

    def begin():
        send_z(lambda to: sent.at[way, core, to], via_z, 0)
        via_z[way, g] = sent[way, core, g]
        for i in range(depth):
            turned_xy[way, :, i] = sent[way, 1 - core, i]
        send_xy(turned_xy, via_xy, 1, 1 - core, near_first[::-1] + [0])

    def go_on_z():
        wait(via_xy.at[way], xy_recv.at[way, 1])
        for i in range(depth):
            turned_back[way, i] = via_xy[way, :, i]
        send_z(lambda to: turned_back.at[way, to], landed_z, 1)
        landed_z[way, g] = turned_back[way, g]

    def go_on_xy():
        wait(via_z.at[way, pl.ds(0, depth - 1)], z_recv.at[way, 0])
        for i in range(depth):
            turned_z[way, :, i] = via_z[way, i]
        send_xy(turned_z, landed_xy, 0, core, near_first[::-1])
        landed_xy[way, xy] = turned_z[way, xy]

    def end(target):
        wait(landed_xy.at[way, pl.ds(0, plane - 1)], xy_recv.at[way, 0])

        def from_xy(i, carry):
            widen(target, i, core, landed_xy[way, :, i])
            return carry

        lax.fori_loop(0, depth, from_xy, 0)
        wait(landed_z.at[way, pl.ds(0, depth - 1)], z_recv.at[way, 1])

        def from_z(i, carry):
            widen(target, i, 1 - core, landed_z[way, i])
            return carry

        lax.fori_loop(0, depth, from_z, 0)

    way = 0
    loads[1].wait()
    for c in range(0, SUBLANES, 2):
        pair = matmul(slots_half, grad[:, c * LANES : (c + 2) * LANES])
        wide[pl.ds(c, blocks, stride=SUBLANES), :] = pair[:, :LANES]
        wide[pl.ds(c + 1, blocks, stride=SUBLANES), :] = pair[:, LANES:]
    narrow()
    pl.semaphore_wait(barrier, depth - 1 + fan - 1)
    begin()

    loads[2].wait()
    tall = min(blocks, 32)
    share = jnp.zeros((1, blocks), jnp.float32)
    for i in range(0, blocks, tall):
        rows = pl.ds(i, tall)
        gradient = grad[rows, :].astype(jnp.float32)
        second = MOMENT_DECAY * moment[rows, :] + (1.0 - MOMENT_DECAY) * gradient * gradient
        moment[rows, :] = second
        direction = gradient / (jnp.sqrt(second) + ADAM_EPS)
        squares = jnp.sum(direction * direction, axis=1, keepdims=True)
        share = share + jnp.sum(holds[i : i + tall, :] * squares, axis=0, keepdims=True)
    norms[0:1, :] = share
    go_on_z()
    go_on_xy()

    end(wide)
    for c in range(pieces):
        block[:, c * LANES : (c + 1) * LANES] = wide[pl.ds(c, side, stride=pieces), :].astype(
            jnp.bfloat16
        )
    loads[3].wait()
    loads[4].wait()
    half = matmul(left_root[...], block[...]).astype(jnp.bfloat16)
    full = matmul(half, right_root[...])
    for c in range(pieces):
        wide[pl.ds(c, side, stride=pieces), :] = full[:, c * LANES : (c + 1) * LANES]

    way = 1
    narrow()
    begin()

    lane = lax.broadcasted_iota(jnp.int32, (1, blocks), 1)
    precon_sq = jnp.sum(full * full, keepdims=True)
    norms[1:2, :] = jnp.where(lane == me, precon_sq, 0.0)

    def norm_z(j, carry):
        pltpu.make_async_remote_copy(
            src_ref=norms,
            dst_ref=norms_z.at[g],
            send_sem=norm_send.at[0],
            recv_sem=norm_recv.at[0],
            device_id=((g + j) % depth, f),
            device_id_type=MESH,
        ).start()
        return carry

    def norm_f(j, carry):
        pltpu.make_async_remote_copy(
            src_ref=norms_z_sum,
            dst_ref=norms_f.at[f],
            send_sem=norm_send.at[1],
            recv_sem=norm_recv.at[1],
            device_id=(g, (f + j) % fan),
            device_id_type=MESH,
        ).start()
        return carry

    lax.fori_loop(1, depth, norm_z, 0)

    loads[5].wait()
    left = matmul(block[...], block[...], 1, 1)
    left_stat[...] = STAT_DECAY * left_stat[...] + (1.0 - STAT_DECAY) * left / side
    loads[6].wait()
    right = matmul(block[...], block[...], 0, 0)
    right_stat[...] = STAT_DECAY * right_stat[...] + (1.0 - STAT_DECAY) * right / side
    go_on_z()
    arrived = norms_z.at[pl.ds(0, depth - 1)]
    pltpu.make_async_copy(arrived, arrived, norm_recv.at[0]).wait()
    norms_z[g] = norms[...]
    norms_z_sum[...] = jnp.sum(norms_z[...], axis=0)
    lax.fori_loop(1, fan, norm_f, 0)
    go_on_xy()
    end(wide_back)
    arrived = norms_f.at[pl.ds(0, fan - 1)]
    pltpu.make_async_copy(arrived, arrived, norm_recv.at[1]).wait()
    norms_f[f] = norms_z_sum[...]
    totals[...] = jnp.sum(norms_f[...], axis=0)

    for way in range(2):
        wait(via_z.at[way, pl.ds(0, depth - 1)], z_send.at[way, 0])
        wait(landed_z.at[way, pl.ds(0, depth - 1)], z_send.at[way, 1])
        wait(landed_xy.at[way, pl.ds(0, plane - 1)], xy_send.at[way, 0])
        wait(via_xy.at[way], xy_send.at[way, 1])
    part = norms_z.at[pl.ds(0, depth - 1)]
    pltpu.make_async_copy(part, part, norm_send.at[0]).wait()
    part = norms_f.at[pl.ds(0, fan - 1)]
    pltpu.make_async_copy(part, part, norm_send.at[1]).wait()


def write(
    wide,
    totals,
    moment,
    left_stat,
    right_stat,
    order_hbm,
    update_hbm,
    moment_hbm,
    left_hbm,
    right_hbm,
    order,
    update,
    sems,
):
    load = pltpu.make_async_copy(order_hbm, order, sems.at[0])
    load.start()
    stores = [
        pltpu.make_async_copy(moment, moment_hbm, sems.at[1]),
        pltpu.make_async_copy(left_stat, left_hbm, sems.at[2]),
        pltpu.make_async_copy(right_stat, right_hbm, sems.at[3]),
    ]
    for store in stores:
        store.start()
    load.wait()
    blocks = update.shape[0]
    which = lax.broadcasted_iota(jnp.int32, (blocks, blocks), 0)
    holds = jnp.where(which == order[...], 1.0, 0.0)
    scale = jnp.sqrt(totals[0:1, :]) / (jnp.sqrt(totals[1:2, :]) + PRECON_EPS)
    scale = jnp.sum(holds * scale, axis=1, keepdims=True)
    holds = holds.astype(jnp.bfloat16)
    for c in range(0, SUBLANES, 2):
        pair = jnp.concatenate(
            [wide[pl.ds(c + i, blocks, stride=SUBLANES), :] for i in range(2)], axis=1
        ).astype(jnp.bfloat16)
        columns = pl.ds(c * LANES, 2 * LANES)
        update[:, columns] = (matmul(holds, pair) * scale).astype(jnp.bfloat16)
        stores.append(
            pltpu.make_async_copy(update.at[:, columns], update_hbm.at[:, columns], sems.at[4 + c // 2])
        )
        stores[-1].start()
    for store in stores:
        store.wait()


def shards(across, grad, moment, order, left_stat, right_stat, left_root, right_root):
    depth = lax.axis_size("group")
    fan = lax.axis_size("fsdp")
    plane = fan // 2
    blocks, entries = grad.shape
    side = left_stat.shape[-1]
    f32, bf16 = jnp.float32, jnp.bfloat16
    tile = (SUBLANES, LANES)
    hbm = pl.BlockSpec(memory_space=pltpu.HBM)
    vmem = pl.BlockSpec(memory_space=pltpu.VMEM)
    order = order.reshape(1, blocks)
    entry_shapes = jax.ShapeDtypeStruct((blocks, entries), f32)
    stat_shapes = jax.ShapeDtypeStruct((side, side), f32)
    wide, totals, moment_new, left_new, right_new = pl.pallas_call(
        functools.partial(exchange, depth, across),
        out_shape=(
            jax.ShapeDtypeStruct((blocks * SUBLANES, LANES), f32),
            jax.ShapeDtypeStruct((2, blocks), f32),
            entry_shapes,
            stat_shapes,
            stat_shapes,
        ),
        in_specs=[hbm] * 7,
        out_specs=(vmem,) * 5,
        scratch_shapes=[
            pltpu.VMEM((1, blocks), jnp.int32),
            pltpu.VMEM((blocks, entries), bf16),
            pltpu.VMEM((side, side), bf16),
            pltpu.VMEM((side, side), bf16),
            pltpu.VMEM((blocks * SUBLANES, LANES), f32),
            pltpu.VMEM((2, 2, depth, plane, *tile), bf16),
            pltpu.VMEM((2, depth, plane, *tile), bf16),
            pltpu.VMEM((2, plane, depth, *tile), bf16),
            pltpu.VMEM((2, plane, depth, *tile), bf16),
            pltpu.VMEM((2, plane, depth, *tile), bf16),
            pltpu.VMEM((2, plane, depth, *tile), bf16),
            pltpu.VMEM((2, depth, plane, *tile), bf16),
            pltpu.VMEM((2, depth, plane, *tile), bf16),
            pltpu.VMEM((side, side), bf16),
            pltpu.VMEM((2, blocks), f32),
            pltpu.VMEM((depth, 2, blocks), f32),
            pltpu.VMEM((2, blocks), f32),
            pltpu.VMEM((fan, 2, blocks), f32),
            pltpu.SemaphoreType.DMA((7,)),
            pltpu.SemaphoreType.DMA((2, 2)),
            pltpu.SemaphoreType.DMA((2, 2)),
            pltpu.SemaphoreType.DMA((2, 2)),
            pltpu.SemaphoreType.DMA((2, 2)),
            pltpu.SemaphoreType.DMA((2,)),
            pltpu.SemaphoreType.DMA((2,)),
        ],
        compiler_params=pltpu.CompilerParams(
            collective_id=0, has_side_effects=True, vmem_limit_bytes=40 * 1024 * 1024
        ),
        cost_estimate=pl.CostEstimate(
            flops=8 * side**3 + 2 * blocks * blocks * entries,
            bytes_accessed=6 * blocks * entries + 12 * side * side,
            transcendentals=2 * blocks * entries,
        ),
    )(
        *(
            pltpu.with_memory_space_constraint(operand, pltpu.HBM)
            for operand in (
                grad,
                moment,
                order,
                left_stat[0],
                right_stat[0],
                left_root[0],
                right_root[0],
            )
        )
    )
    update, moment_new, left_new, right_new = pl.pallas_call(
        write,
        out_shape=(
            jax.ShapeDtypeStruct((blocks, entries), bf16),
            entry_shapes,
            stat_shapes,
            stat_shapes,
        ),
        in_specs=[vmem] * 5 + [hbm],
        out_specs=(hbm,) * 4,
        scratch_shapes=[
            pltpu.VMEM((1, blocks), jnp.int32),
            pltpu.VMEM((blocks, entries), bf16),
            pltpu.SemaphoreType.DMA((8,)),
        ],
        compiler_params=pltpu.CompilerParams(vmem_limit_bytes=40 * 1024 * 1024),
        cost_estimate=pl.CostEstimate(
            flops=2 * blocks * blocks * entries,
            bytes_accessed=6 * blocks * entries + 8 * side * side,
            transcendentals=0,
        ),
    )(
        wide,
        totals,
        moment_new,
        left_new,
        right_new,
        pltpu.with_memory_space_constraint(order, pltpu.HBM),
    )
    return (update, moment_new, left_new[None], right_new[None])


def solution(mesh):
    across = 4 if mesh.shape["fsdp"] == 32 else 2
    placed = (
        P(None, ("group", "fsdp")),
        P(None, ("group", "fsdp")),
        P(),
        P(("group", "fsdp"), None, None),
        P(("group", "fsdp"), None, None),
        P(("group", "fsdp"), None, None),
        P(("group", "fsdp"), None, None),
    )
    return jax.shard_map(
        functools.partial(shards, across),
        mesh=mesh,
        in_specs=placed,
        out_specs=(
            P(None, ("group", "fsdp")),
            P(None, ("group", "fsdp")),
            P(("group", "fsdp"), None, None),
            P(("group", "fsdp"), None, None),
        ),
        check_vma=False,
    )
```

```python
import functools

import jax
import jax.numpy as jnp
from jax import lax
from jax.experimental import pallas as pl
from jax.experimental.pallas import tpu as pltpu
from jax.sharding import PartitionSpec as P

MOMENT_DECAY = 0.95
STAT_DECAY = 0.9
ADAM_EPS = 1e-08
PRECON_EPS = 1e-06

LANES = 128
SUBLANES = 8
MESH = pl.DeviceIdType.MESH


def matmul(a, b, a_dim=1, b_dim=0):
    return lax.dot_general(
        a, b, (((a_dim,), (b_dim,)), ((), ())), preferred_element_type=jnp.float32
    )


def alternate(count):
    return sorted(range(1, count), key=lambda k: (-min(k, count - k), k))


def exchange(
    depth,
    across,
    grad_hbm,
    moment_hbm,
    order_hbm,
    left_stat_hbm,
    right_stat_hbm,
    left_root_hbm,
    right_root_hbm,
    wide_back,
    totals,
    holds_half,
    moment,
    left_stat,
    right_stat,
    order,
    grad,
    left_root,
    right_root,
    wide,
    sent,
    via_z,
    turned_z,
    landed_xy,
    turned_xy,
    via_xy,
    turned_back,
    landed_z,
    block,
    norms,
    norms_core,
    norms_core_sum,
    norms_z,
    norms_z_sum,
    norms_xy,
    load_sem,
    z_send,
    z_recv,
    xy_send,
    xy_recv,
    norm_send,
    norm_recv,
):
    plane = via_xy.shape[1]
    deep = plane // across
    fan = plane * 2
    blocks = depth * fan
    side = block.shape[0]
    pieces = side // LANES
    g = lax.axis_index("group")
    f = lax.axis_index("fsdp")
    xy = f // 2
    core = f % 2
    x = xy // deep
    y = xy % deep
    me = g * fan + f

    loads = [
        pltpu.make_async_copy(source, target, load_sem.at[i])
        for i, (source, target) in enumerate(
            (
                (order_hbm, order),
                (grad_hbm, grad),
                (moment_hbm, moment),
                (left_root_hbm, left_root),
                (right_root_hbm, right_root),
                (left_stat_hbm, left_stat),
                (right_stat_hbm, right_stat),
            )
        )
    ]
    for load in loads:
        load.start()

    barrier = pltpu.get_barrier_semaphore()

    def greet_z(k, carry):
        to = lax.rem(g + k, depth)
        pl.semaphore_signal(barrier, inc=1, device_id=(to, f), device_id_type=MESH)
        return carry

    def greet_f(k, carry):
        to = lax.rem(f + k, fan)
        pl.semaphore_signal(barrier, inc=1, device_id=(g, to), device_id_type=MESH)
        return carry

    lax.fori_loop(1, depth, greet_z, 0)
    lax.fori_loop(1, fan, greet_f, 0)

    loads[0].wait()
    which = lax.broadcasted_iota(jnp.int32, (blocks, blocks), 0)
    holds = jnp.where(which == order[...], 1.0, 0.0)
    holds_half[...] = holds.astype(jnp.bfloat16)
    slots_half = holds.T.astype(jnp.bfloat16)

    def tile(i, j, c):
        first = pl.multiple_of((i * fan + j * 2 + c) * SUBLANES, SUBLANES)
        return wide[pl.ds(first, SUBLANES), :].astype(jnp.bfloat16)

    def widen(target, i, c, part):
        part = part.astype(jnp.float32)
        first = pl.multiple_of((i * fan + c) * SUBLANES, SUBLANES)
        for j in range(plane):
            target[pl.ds(first + j * 2 * SUBLANES, SUBLANES), :] = part[j]

    near_first = sorted(
        range(1, plane),
        key=lambda j: (
            min(j // deep, across - j // deep) + min(j % deep, deep - j % deep),
            j,
        ),
    )

    def place(j):
        tx = lax.rem(x + j // deep, across)
        ty = lax.rem(y + j % deep, deep)
        return tx * deep + ty

    def send_z(j, source, target, half):
        to = lax.rem(g + j, depth)
        pltpu.make_async_remote_copy(
            src_ref=source.at[way, to],
            dst_ref=target.at[way, g],
            send_sem=z_send.at[way, half],
            recv_sem=z_recv.at[way, half],
            device_id=(to, f),
            device_id_type=MESH,
        ).start()

    def send_xy(source, target, half, to_core, places):
        for j in places:
            to = place(j)
            pltpu.make_async_remote_copy(
                src_ref=source.at[way, to],
                dst_ref=target.at[way, xy],
                send_sem=xy_send.at[way, half],
                recv_sem=xy_recv.at[way, half],
                device_id=(g, to * 2 + to_core),
                device_id_type=MESH,
            ).start()

    def wait(part, sem):
        pltpu.make_async_copy(part, part, sem).wait()

    def begin():
        for k in alternate(depth):
            to = lax.rem(g + k, depth)
            for j in range(plane):
                sent[way, to, j] = tile(to, j, core)
            send_z(k, sent, via_z, 0)

        def fill(i, carry):
            for j in range(plane):
                turned_xy[way, j, i] = tile(i, j, 1 - core)
            return carry

        lax.fori_loop(0, depth, fill, 0)
        send_xy(turned_xy, via_xy, 1, 1 - core, near_first[::-1] + [0])
        for j in range(plane):
            via_z[way, g, j] = tile(g, j, core)

    def go_on_z():
        wait(via_xy.at[way], xy_recv.at[way, 1])
        for i in range(depth):
            turned_back[way, i] = via_xy[way, :, i]
        for k in alternate(depth):
            send_z(k, turned_back, landed_z, 1)
        landed_z[way, g] = turned_back[way, g]

    def go_on_xy():
        wait(via_z.at[way, pl.ds(0, depth - 1)], z_recv.at[way, 0])
        for i in range(depth):
            turned_z[way, :, i] = via_z[way, i]
        send_xy(turned_z, landed_xy, 0, core, near_first[::-1])
        landed_xy[way, xy] = turned_z[way, xy]

    def end(target):
        wait(landed_xy.at[way, pl.ds(0, plane - 1)], xy_recv.at[way, 0])

        def from_xy(i, carry):
            widen(target, i, core, landed_xy[way, :, i])
            return carry

        lax.fori_loop(0, depth, from_xy, 0)
        wait(landed_z.at[way, pl.ds(0, depth - 1)], z_recv.at[way, 1])

        def from_z(i, carry):
            widen(target, i, 1 - core, landed_z[way, i])
            return carry

        lax.fori_loop(0, depth, from_z, 0)

    way = 0
    loads[1].wait()
    for c in range(0, SUBLANES, 2):
        pair = matmul(slots_half, grad[:, c * LANES : (c + 2) * LANES])
        wide[pl.ds(c, blocks, stride=SUBLANES), :] = pair[:, :LANES]
        wide[pl.ds(c + 1, blocks, stride=SUBLANES), :] = pair[:, LANES:]
    pl.semaphore_wait(barrier, depth - 1 + fan - 1)
    begin()

    loads[2].wait()
    tall = min(blocks, 32)
    share = jnp.zeros((1, blocks), jnp.float32)
    for i in range(0, blocks, tall):
        rows = pl.ds(i, tall)
        gradient = grad[rows, :].astype(jnp.float32)
        second = MOMENT_DECAY * moment[rows, :] + (1.0 - MOMENT_DECAY) * gradient * gradient
        moment[rows, :] = second
        direction = gradient / (jnp.sqrt(second) + ADAM_EPS)
        squares = jnp.sum(direction * direction, axis=1, keepdims=True)
        share = share + jnp.sum(holds[i : i + tall, :] * squares, axis=0, keepdims=True)
    norms[0:1, :] = share
    go_on_z()
    go_on_xy()

    end(wide)
    for c in range(pieces):
        block[:, c * LANES : (c + 1) * LANES] = wide[pl.ds(c, side, stride=pieces), :].astype(
            jnp.bfloat16
        )
    loads[3].wait()
    loads[4].wait()
    half = matmul(left_root[...], block[...]).astype(jnp.bfloat16)
    full = matmul(half, right_root[...])
    for c in range(pieces):
        wide[pl.ds(c, side, stride=pieces), :] = full[:, c * LANES : (c + 1) * LANES]

    way = 1
    begin()

    lane = lax.broadcasted_iota(jnp.int32, (1, blocks), 1)
    precon_sq = jnp.sum(full * full, keepdims=True)
    norms[1:2, :] = jnp.where(lane == me, precon_sq, 0.0)

    swap = pltpu.make_async_remote_copy(
        src_ref=norms,
        dst_ref=norms_core,
        send_sem=norm_send.at[0],
        recv_sem=norm_recv.at[0],
        device_id=(g, xy * 2 + 1 - core),
        device_id_type=MESH,
    )
    swap.start()

    def norm_z(j, carry):
        pltpu.make_async_remote_copy(
            src_ref=norms_core_sum,
            dst_ref=norms_z.at[g],
            send_sem=norm_send.at[1],
            recv_sem=norm_recv.at[1],
            device_id=(lax.rem(g + j, depth), f),
            device_id_type=MESH,
        ).start()
        return carry

    loads[5].wait()
    left = matmul(block[...], block[...], 1, 1)
    left_stat[...] = STAT_DECAY * left_stat[...] + (1.0 - STAT_DECAY) * left / side
    swap.wait()
    norms_core_sum[...] = norms[...] + norms_core[...]
    lax.fori_loop(1, depth, norm_z, 0)
    loads[6].wait()
    right = matmul(block[...], block[...], 0, 0)
    right_stat[...] = STAT_DECAY * right_stat[...] + (1.0 - STAT_DECAY) * right / side
    go_on_z()
    go_on_xy()
    wait(norms_z.at[pl.ds(0, depth - 1)], norm_recv.at[1])
    norms_z[g] = norms_core_sum[...]
    norms_z_sum[...] = jnp.sum(norms_z[...], axis=0)
    for j in near_first:
        pltpu.make_async_remote_copy(
            src_ref=norms_z_sum,
            dst_ref=norms_xy.at[xy],
            send_sem=norm_send.at[2],
            recv_sem=norm_recv.at[2],
            device_id=(g, place(j) * 2 + core),
            device_id_type=MESH,
        ).start()
    end(wide_back)
    wait(norms_xy.at[pl.ds(0, plane - 1)], norm_recv.at[2])
    norms_xy[xy] = norms_z_sum[...]
    totals[...] = jnp.sum(norms_xy[...], axis=0)

    for way in range(2):
        wait(via_z.at[way, pl.ds(0, depth - 1)], z_send.at[way, 0])
        wait(landed_z.at[way, pl.ds(0, depth - 1)], z_send.at[way, 1])
        wait(landed_xy.at[way, pl.ds(0, plane - 1)], xy_send.at[way, 0])
        wait(via_xy.at[way], xy_send.at[way, 1])
    wait(norms_z.at[pl.ds(0, depth - 1)], norm_send.at[1])
    wait(norms_xy.at[pl.ds(0, plane - 1)], norm_send.at[2])


def write(
    wide,
    totals,
    holds,
    moment,
    left_stat,
    right_stat,
    update_hbm,
    moment_hbm,
    left_hbm,
    right_hbm,
    update,
    sems,
):
    stores = [
        pltpu.make_async_copy(moment, moment_hbm, sems.at[0]),
        pltpu.make_async_copy(left_stat, left_hbm, sems.at[1]),
        pltpu.make_async_copy(right_stat, right_hbm, sems.at[2]),
    ]
    for store in stores:
        store.start()
    blocks = update.shape[0]
    scale = jnp.sqrt(totals[0:1, :]) / (jnp.sqrt(totals[1:2, :]) + PRECON_EPS)
    scale = jnp.sum(holds[...].astype(jnp.float32) * scale, axis=1, keepdims=True)
    for c in range(0, SUBLANES, 2):
        pair = jnp.concatenate(
            [wide[pl.ds(c + i, blocks, stride=SUBLANES), :] for i in range(2)], axis=1
        ).astype(jnp.bfloat16)
        columns = pl.ds(c * LANES, 2 * LANES)
        update[:, columns] = (matmul(holds[...], pair) * scale).astype(jnp.bfloat16)
        stores.append(
            pltpu.make_async_copy(update.at[:, columns], update_hbm.at[:, columns], sems.at[3 + c // 2])
        )
        stores[-1].start()
    for store in stores:
        store.wait()


def shards(across, grad, moment, order, left_stat, right_stat, left_root, right_root):
    depth = lax.axis_size("group")
    fan = lax.axis_size("fsdp")
    plane = fan // 2
    blocks, entries = grad.shape
    side = left_stat.shape[-1]
    f32, bf16 = jnp.float32, jnp.bfloat16
    tile = (SUBLANES, LANES)
    hbm = pl.BlockSpec(memory_space=pltpu.HBM)
    vmem = pl.BlockSpec(memory_space=pltpu.VMEM)
    order = order.reshape(1, blocks)
    entry_shapes = jax.ShapeDtypeStruct((blocks, entries), f32)
    stat_shapes = jax.ShapeDtypeStruct((side, side), f32)
    wide, totals, holds, moment_new, left_new, right_new = pl.pallas_call(
        functools.partial(exchange, depth, across),
        out_shape=(
            jax.ShapeDtypeStruct((blocks * SUBLANES, LANES), f32),
            jax.ShapeDtypeStruct((2, blocks), f32),
            jax.ShapeDtypeStruct((blocks, blocks), bf16),
            entry_shapes,
            stat_shapes,
            stat_shapes,
        ),
        in_specs=[hbm] * 7,
        out_specs=(vmem,) * 6,
        scratch_shapes=[
            pltpu.VMEM((1, blocks), jnp.int32),
            pltpu.VMEM((blocks, entries), bf16),
            pltpu.VMEM((side, side), bf16),
            pltpu.VMEM((side, side), bf16),
            pltpu.VMEM((blocks * SUBLANES, LANES), f32),
            pltpu.VMEM((2, depth, plane, *tile), bf16),
            pltpu.VMEM((2, depth, plane, *tile), bf16),
            pltpu.VMEM((2, plane, depth, *tile), bf16),
            pltpu.VMEM((2, plane, depth, *tile), bf16),
            pltpu.VMEM((2, plane, depth, *tile), bf16),
            pltpu.VMEM((2, plane, depth, *tile), bf16),
            pltpu.VMEM((2, depth, plane, *tile), bf16),
            pltpu.VMEM((2, depth, plane, *tile), bf16),
            pltpu.VMEM((side, side), bf16),
            pltpu.VMEM((2, blocks), f32),
            pltpu.VMEM((2, blocks), f32),
            pltpu.VMEM((2, blocks), f32),
            pltpu.VMEM((depth, 2, blocks), f32),
            pltpu.VMEM((2, blocks), f32),
            pltpu.VMEM((plane, 2, blocks), f32),
            pltpu.SemaphoreType.DMA((7,)),
            pltpu.SemaphoreType.DMA((2, 2)),
            pltpu.SemaphoreType.DMA((2, 2)),
            pltpu.SemaphoreType.DMA((2, 2)),
            pltpu.SemaphoreType.DMA((2, 2)),
            pltpu.SemaphoreType.DMA((3,)),
            pltpu.SemaphoreType.DMA((3,)),
        ],
        compiler_params=pltpu.CompilerParams(
            collective_id=0, has_side_effects=True, vmem_limit_bytes=40 * 1024 * 1024
        ),
        cost_estimate=pl.CostEstimate(
            flops=8 * side**3 + 2 * blocks * blocks * entries,
            bytes_accessed=6 * blocks * entries + 12 * side * side,
            transcendentals=2 * blocks * entries,
        ),
    )(
        *(
            pltpu.with_memory_space_constraint(operand, pltpu.HBM)
            for operand in (
                grad,
                moment,
                order,
                left_stat[0],
                right_stat[0],
                left_root[0],
                right_root[0],
            )
        )
    )
    update, moment_new, left_new, right_new = pl.pallas_call(
        write,
        out_shape=(
            jax.ShapeDtypeStruct((blocks, entries), bf16),
            entry_shapes,
            stat_shapes,
            stat_shapes,
        ),
        in_specs=[vmem] * 6,
        out_specs=(hbm,) * 4,
        scratch_shapes=[
            pltpu.VMEM((blocks, entries), bf16),
            pltpu.SemaphoreType.DMA((7,)),
        ],
        compiler_params=pltpu.CompilerParams(vmem_limit_bytes=40 * 1024 * 1024),
        cost_estimate=pl.CostEstimate(
            flops=2 * blocks * blocks * entries,
            bytes_accessed=6 * blocks * entries + 8 * side * side,
            transcendentals=0,
        ),
    )(wide, totals, holds, moment_new, left_new, right_new)
    return (update, moment_new, left_new[None], right_new[None])


def solution(mesh):
    across = 4 if mesh.shape["fsdp"] == 32 else 2
    placed = (
        P(None, ("group", "fsdp")),
        P(None, ("group", "fsdp")),
        P(),
        P(("group", "fsdp"), None, None),
        P(("group", "fsdp"), None, None),
        P(("group", "fsdp"), None, None),
        P(("group", "fsdp"), None, None),
    )
    return jax.shard_map(
        functools.partial(shards, across),
        mesh=mesh,
        in_specs=placed,
        out_specs=(
            P(None, ("group", "fsdp")),
            P(None, ("group", "fsdp")),
            P(("group", "fsdp"), None, None),
            P(("group", "fsdp"), None, None),
        ),
        check_vma=False,
    )
```

```python
import functools

import jax
import jax.numpy as jnp
from jax import lax
from jax.experimental import pallas as pl
from jax.experimental.pallas import tpu as pltpu
from jax.sharding import PartitionSpec as P

MOMENT_DECAY = 0.95
STAT_DECAY = 0.9
ADAM_EPS = 1e-08
PRECON_EPS = 1e-06

LANES = 128
SUBLANES = 8
MESH = pl.DeviceIdType.MESH


def matmul(a, b, a_dim=1, b_dim=0):
    return lax.dot_general(
        a, b, (((a_dim,), (b_dim,)), ((), ())), preferred_element_type=jnp.float32
    )


def alternate(count):
    return sorted(range(1, count), key=lambda k: (-min(k, count - k), k))


def exchange(
    depth,
    across,
    grad_hbm,
    moment_hbm,
    order_hbm,
    left_stat_hbm,
    right_stat_hbm,
    left_root_hbm,
    right_root_hbm,
    wide_back,
    totals,
    holds_half,
    moment,
    left_stat,
    right_stat,
    order,
    grad,
    left_root,
    right_root,
    wide,
    sent,
    via_z,
    turned_z,
    landed_xy,
    turned_xy,
    via_xy,
    turned_back,
    landed_z,
    hop,
    block,
    norms,
    norms_core,
    norms_core_sum,
    norms_z,
    norms_z_sum,
    norms_xy,
    load_sem,
    z_send,
    z_recv,
    xy_send,
    xy_recv,
    hop_send,
    hop_recv,
    norm_send,
    norm_recv,
):
    plane = via_xy.shape[1]
    deep = plane // across
    fan = plane * 2
    blocks = depth * fan
    side = block.shape[0]
    pieces = side // LANES
    g = lax.axis_index("group")
    f = lax.axis_index("fsdp")
    xy = f // 2
    core = f % 2
    x = xy // deep
    y = xy % deep
    me = g * fan + f

    loads = [
        pltpu.make_async_copy(source, target, load_sem.at[i])
        for i, (source, target) in enumerate(
            (
                (order_hbm, order),
                (grad_hbm, grad),
                (moment_hbm, moment),
                (left_root_hbm, left_root),
                (right_root_hbm, right_root),
                (left_stat_hbm, left_stat),
                (right_stat_hbm, right_stat),
            )
        )
    ]
    for load in loads:
        load.start()

    barrier = pltpu.get_barrier_semaphore()

    def greet_z(k, carry):
        to = lax.rem(g + k, depth)
        pl.semaphore_signal(barrier, inc=1, device_id=(to, f), device_id_type=MESH)
        return carry

    def greet_f(k, carry):
        to = lax.rem(f + k, fan)
        pl.semaphore_signal(barrier, inc=1, device_id=(g, to), device_id_type=MESH)
        return carry

    lax.fori_loop(1, depth, greet_z, 0)
    lax.fori_loop(1, fan, greet_f, 0)

    loads[0].wait()
    which = lax.broadcasted_iota(jnp.int32, (blocks, blocks), 0)
    holds = jnp.where(which == order[...], 1.0, 0.0)
    holds_half[...] = holds.astype(jnp.bfloat16)
    slots_half = holds.T.astype(jnp.bfloat16)

    def tile(i, j, c):
        first = pl.multiple_of((i * fan + j * 2 + c) * SUBLANES, SUBLANES)
        return wide[pl.ds(first, SUBLANES), :].astype(jnp.bfloat16)

    def widen(target, i, c, part):
        part = part.astype(jnp.float32)
        first = pl.multiple_of((i * fan + c) * SUBLANES, SUBLANES)
        for j in range(plane):
            target[pl.ds(first + j * 2 * SUBLANES, SUBLANES), :] = part[j]

    near_first = sorted(
        range(1, plane),
        key=lambda j: (
            min(j // deep, across - j // deep) + min(j % deep, deep - j % deep),
            j,
        ),
    )

    def place(j):
        tx = lax.rem(x + j // deep, across)
        ty = lax.rem(y + j % deep, deep)
        return tx * deep + ty

    hops = depth % 4 == 0
    leg = depth // 4 + core * (depth // 2)

    def send_hop(source, half):
        pltpu.make_async_remote_copy(
            src_ref=source.at[way, lax.rem(g + depth // 2, depth)],
            dst_ref=hop.at[way, half],
            send_sem=hop_send.at[way, half],
            recv_sem=hop_recv.at[way, half],
            device_id=(lax.rem(g + leg, depth), f),
            device_id_type=MESH,
        ).start()

    def pass_hop(target, half):
        if not hops:
            return
        wait(hop.at[way, half], hop_recv.at[way, half])
        pltpu.make_async_remote_copy(
            src_ref=hop.at[way, half],
            dst_ref=target.at[way, lax.rem(g + depth - leg, depth)],
            send_sem=z_send.at[way, half],
            recv_sem=z_recv.at[way, half],
            device_id=(lax.rem(g + leg, depth), f),
            device_id_type=MESH,
        ).start()

    def send_z(j, source, target, half):
        if hops and j == depth // 2:
            send_hop(source, half)
            return
        to = lax.rem(g + j, depth)
        pltpu.make_async_remote_copy(
            src_ref=source.at[way, to],
            dst_ref=target.at[way, g],
            send_sem=z_send.at[way, half],
            recv_sem=z_recv.at[way, half],
            device_id=(to, f),
            device_id_type=MESH,
        ).start()

    def send_xy(source, target, half, to_core, places):
        for j in places:
            to = place(j)
            pltpu.make_async_remote_copy(
                src_ref=source.at[way, to],
                dst_ref=target.at[way, xy],
                send_sem=xy_send.at[way, half],
                recv_sem=xy_recv.at[way, half],
                device_id=(g, to * 2 + to_core),
                device_id_type=MESH,
            ).start()

    def wait(part, sem):
        pltpu.make_async_copy(part, part, sem).wait()

    def begin():
        for k in alternate(depth):
            to = lax.rem(g + k, depth)
            for j in range(plane):
                sent[way, to, j] = tile(to, j, core)
            send_z(k, sent, via_z, 0)

        def fill(i, carry):
            for j in range(plane):
                turned_xy[way, j, i] = tile(i, j, 1 - core)
            return carry

        lax.fori_loop(0, depth, fill, 0)
        send_xy(turned_xy, via_xy, 1, 1 - core, near_first[::-1] + [0])
        for j in range(plane):
            via_z[way, g, j] = tile(g, j, core)
        pass_hop(via_z, 0)

    def go_on_z():
        wait(via_xy.at[way], xy_recv.at[way, 1])
        for i in range(depth):
            turned_back[way, i] = via_xy[way, :, i]
        for k in alternate(depth):
            send_z(k, turned_back, landed_z, 1)
        landed_z[way, g] = turned_back[way, g]

    def go_on_xy():
        wait(via_z.at[way, pl.ds(0, depth - 1)], z_recv.at[way, 0])
        for i in range(depth):
            turned_z[way, :, i] = via_z[way, i]
        send_xy(turned_z, landed_xy, 0, core, near_first[::-1])
        landed_xy[way, xy] = turned_z[way, xy]
        pass_hop(landed_z, 1)

    def end(target):
        wait(landed_xy.at[way, pl.ds(0, plane - 1)], xy_recv.at[way, 0])

        def from_xy(i, carry):
            widen(target, i, core, landed_xy[way, :, i])
            return carry

        lax.fori_loop(0, depth, from_xy, 0)
        wait(landed_z.at[way, pl.ds(0, depth - 1)], z_recv.at[way, 1])

        def from_z(i, carry):
            widen(target, i, 1 - core, landed_z[way, i])
            return carry

        lax.fori_loop(0, depth, from_z, 0)

    way = 0
    loads[1].wait()
    for c in range(0, SUBLANES, 2):
        pair = matmul(slots_half, grad[:, c * LANES : (c + 2) * LANES])
        wide[pl.ds(c, blocks, stride=SUBLANES), :] = pair[:, :LANES]
        wide[pl.ds(c + 1, blocks, stride=SUBLANES), :] = pair[:, LANES:]
    pl.semaphore_wait(barrier, depth - 1 + fan - 1)
    begin()

    loads[2].wait()
    tall = min(blocks, 32)
    share = jnp.zeros((1, blocks), jnp.float32)
    for i in range(0, blocks, tall):
        rows = pl.ds(i, tall)
        gradient = grad[rows, :].astype(jnp.float32)
        second = MOMENT_DECAY * moment[rows, :] + (1.0 - MOMENT_DECAY) * gradient * gradient
        moment[rows, :] = second
        direction = gradient / (jnp.sqrt(second) + ADAM_EPS)
        squares = jnp.sum(direction * direction, axis=1, keepdims=True)
        share = share + jnp.sum(holds[i : i + tall, :] * squares, axis=0, keepdims=True)
    norms[0:1, :] = share
    go_on_z()
    go_on_xy()

    end(wide)
    for c in range(pieces):
        block[:, c * LANES : (c + 1) * LANES] = wide[pl.ds(c, side, stride=pieces), :].astype(
            jnp.bfloat16
        )
    loads[3].wait()
    loads[4].wait()
    half = matmul(left_root[...], block[...]).astype(jnp.bfloat16)
    full = matmul(half, right_root[...])
    for c in range(pieces):
        wide[pl.ds(c, side, stride=pieces), :] = full[:, c * LANES : (c + 1) * LANES]

    way = 1
    begin()

    lane = lax.broadcasted_iota(jnp.int32, (1, blocks), 1)
    precon_sq = jnp.sum(full * full, keepdims=True)
    norms[1:2, :] = jnp.where(lane == me, precon_sq, 0.0)

    swap = pltpu.make_async_remote_copy(
        src_ref=norms,
        dst_ref=norms_core,
        send_sem=norm_send.at[0],
        recv_sem=norm_recv.at[0],
        device_id=(g, xy * 2 + 1 - core),
        device_id_type=MESH,
    )
    swap.start()

    def norm_z(j, carry):
        pltpu.make_async_remote_copy(
            src_ref=norms_core_sum,
            dst_ref=norms_z.at[g],
            send_sem=norm_send.at[1],
            recv_sem=norm_recv.at[1],
            device_id=(lax.rem(g + j, depth), f),
            device_id_type=MESH,
        ).start()
        return carry

    loads[5].wait()
    left = matmul(block[...], block[...], 1, 1)
    left_stat[...] = STAT_DECAY * left_stat[...] + (1.0 - STAT_DECAY) * left / side
    swap.wait()
    norms_core_sum[...] = norms[...] + norms_core[...]
    lax.fori_loop(1, depth, norm_z, 0)
    loads[6].wait()
    right = matmul(block[...], block[...], 0, 0)
    right_stat[...] = STAT_DECAY * right_stat[...] + (1.0 - STAT_DECAY) * right / side
    go_on_z()
    go_on_xy()
    wait(norms_z.at[pl.ds(0, depth - 1)], norm_recv.at[1])
    norms_z[g] = norms_core_sum[...]
    norms_z_sum[...] = jnp.sum(norms_z[...], axis=0)
    for j in near_first:
        pltpu.make_async_remote_copy(
            src_ref=norms_z_sum,
            dst_ref=norms_xy.at[xy],
            send_sem=norm_send.at[2],
            recv_sem=norm_recv.at[2],
            device_id=(g, place(j) * 2 + core),
            device_id_type=MESH,
        ).start()
    end(wide_back)
    wait(norms_xy.at[pl.ds(0, plane - 1)], norm_recv.at[2])
    norms_xy[xy] = norms_z_sum[...]
    totals[...] = jnp.sum(norms_xy[...], axis=0)

    for way in range(2):
        wait(via_z.at[way, pl.ds(0, depth - 1)], z_send.at[way, 0])
        wait(landed_z.at[way, pl.ds(0, depth - 1)], z_send.at[way, 1])
        wait(landed_xy.at[way, pl.ds(0, plane - 1)], xy_send.at[way, 0])
        wait(via_xy.at[way], xy_send.at[way, 1])
        if hops:
            for half in range(2):
                wait(hop.at[way, half], hop_send.at[way, half])
    wait(norms_z.at[pl.ds(0, depth - 1)], norm_send.at[1])
    wait(norms_xy.at[pl.ds(0, plane - 1)], norm_send.at[2])


def write(
    wide,
    totals,
    holds,
    moment,
    left_stat,
    right_stat,
    update_hbm,
    moment_hbm,
    left_hbm,
    right_hbm,
    update,
    sems,
):
    stores = [
        pltpu.make_async_copy(moment, moment_hbm, sems.at[0]),
        pltpu.make_async_copy(left_stat, left_hbm, sems.at[1]),
        pltpu.make_async_copy(right_stat, right_hbm, sems.at[2]),
    ]
    for store in stores:
        store.start()
    blocks = update.shape[0]
    scale = jnp.sqrt(totals[0:1, :]) / (jnp.sqrt(totals[1:2, :]) + PRECON_EPS)
    scale = jnp.sum(holds[...].astype(jnp.float32) * scale, axis=1, keepdims=True)
    for c in range(0, SUBLANES, 2):
        pair = jnp.concatenate(
            [wide[pl.ds(c + i, blocks, stride=SUBLANES), :] for i in range(2)], axis=1
        ).astype(jnp.bfloat16)
        columns = pl.ds(c * LANES, 2 * LANES)
        update[:, columns] = (matmul(holds[...], pair) * scale).astype(jnp.bfloat16)
        stores.append(
            pltpu.make_async_copy(update.at[:, columns], update_hbm.at[:, columns], sems.at[3 + c // 2])
        )
        stores[-1].start()
    for store in stores:
        store.wait()


def shards(across, grad, moment, order, left_stat, right_stat, left_root, right_root):
    depth = lax.axis_size("group")
    fan = lax.axis_size("fsdp")
    plane = fan // 2
    blocks, entries = grad.shape
    side = left_stat.shape[-1]
    f32, bf16 = jnp.float32, jnp.bfloat16
    tile = (SUBLANES, LANES)
    hbm = pl.BlockSpec(memory_space=pltpu.HBM)
    vmem = pl.BlockSpec(memory_space=pltpu.VMEM)
    order = order.reshape(1, blocks)
    entry_shapes = jax.ShapeDtypeStruct((blocks, entries), f32)
    stat_shapes = jax.ShapeDtypeStruct((side, side), f32)
    wide, totals, holds, moment_new, left_new, right_new = pl.pallas_call(
        functools.partial(exchange, depth, across),
        out_shape=(
            jax.ShapeDtypeStruct((blocks * SUBLANES, LANES), f32),
            jax.ShapeDtypeStruct((2, blocks), f32),
            jax.ShapeDtypeStruct((blocks, blocks), bf16),
            entry_shapes,
            stat_shapes,
            stat_shapes,
        ),
        in_specs=[hbm] * 7,
        out_specs=(vmem,) * 6,
        scratch_shapes=[
            pltpu.VMEM((1, blocks), jnp.int32),
            pltpu.VMEM((blocks, entries), bf16),
            pltpu.VMEM((side, side), bf16),
            pltpu.VMEM((side, side), bf16),
            pltpu.VMEM((blocks * SUBLANES, LANES), f32),
            pltpu.VMEM((2, depth, plane, *tile), bf16),
            pltpu.VMEM((2, depth, plane, *tile), bf16),
            pltpu.VMEM((2, plane, depth, *tile), bf16),
            pltpu.VMEM((2, plane, depth, *tile), bf16),
            pltpu.VMEM((2, plane, depth, *tile), bf16),
            pltpu.VMEM((2, plane, depth, *tile), bf16),
            pltpu.VMEM((2, depth, plane, *tile), bf16),
            pltpu.VMEM((2, depth, plane, *tile), bf16),
            pltpu.VMEM((2, 2, plane, *tile), bf16),
            pltpu.VMEM((side, side), bf16),
            pltpu.VMEM((2, blocks), f32),
            pltpu.VMEM((2, blocks), f32),
            pltpu.VMEM((2, blocks), f32),
            pltpu.VMEM((depth, 2, blocks), f32),
            pltpu.VMEM((2, blocks), f32),
            pltpu.VMEM((plane, 2, blocks), f32),
            pltpu.SemaphoreType.DMA((7,)),
            pltpu.SemaphoreType.DMA((2, 2)),
            pltpu.SemaphoreType.DMA((2, 2)),
            pltpu.SemaphoreType.DMA((2, 2)),
            pltpu.SemaphoreType.DMA((2, 2)),
            pltpu.SemaphoreType.DMA((2, 2)),
            pltpu.SemaphoreType.DMA((2, 2)),
            pltpu.SemaphoreType.DMA((3,)),
            pltpu.SemaphoreType.DMA((3,)),
        ],
        compiler_params=pltpu.CompilerParams(
            collective_id=0, has_side_effects=True, vmem_limit_bytes=40 * 1024 * 1024
        ),
        cost_estimate=pl.CostEstimate(
            flops=8 * side**3 + 2 * blocks * blocks * entries,
            bytes_accessed=6 * blocks * entries + 12 * side * side,
            transcendentals=2 * blocks * entries,
        ),
    )(
        *(
            pltpu.with_memory_space_constraint(operand, pltpu.HBM)
            for operand in (
                grad,
                moment,
                order,
                left_stat[0],
                right_stat[0],
                left_root[0],
                right_root[0],
            )
        )
    )
    update, moment_new, left_new, right_new = pl.pallas_call(
        write,
        out_shape=(
            jax.ShapeDtypeStruct((blocks, entries), bf16),
            entry_shapes,
            stat_shapes,
            stat_shapes,
        ),
        in_specs=[vmem] * 6,
        out_specs=(hbm,) * 4,
        scratch_shapes=[
            pltpu.VMEM((blocks, entries), bf16),
            pltpu.SemaphoreType.DMA((7,)),
        ],
        compiler_params=pltpu.CompilerParams(vmem_limit_bytes=40 * 1024 * 1024),
        cost_estimate=pl.CostEstimate(
            flops=2 * blocks * blocks * entries,
            bytes_accessed=6 * blocks * entries + 8 * side * side,
            transcendentals=0,
        ),
    )(wide, totals, holds, moment_new, left_new, right_new)
    return (update, moment_new, left_new[None], right_new[None])


def solution(mesh):
    across = 4 if mesh.shape["fsdp"] == 32 else 2
    placed = (
        P(None, ("group", "fsdp")),
        P(None, ("group", "fsdp")),
        P(),
        P(("group", "fsdp"), None, None),
        P(("group", "fsdp"), None, None),
        P(("group", "fsdp"), None, None),
        P(("group", "fsdp"), None, None),
    )
    return jax.shard_map(
        functools.partial(shards, across),
        mesh=mesh,
        in_specs=placed,
        out_specs=(
            P(None, ("group", "fsdp")),
            P(None, ("group", "fsdp")),
            P(("group", "fsdp"), None, None),
            P(("group", "fsdp"), None, None),
        ),
        check_vma=False,
    )
```

```python
import functools

import jax
import jax.numpy as jnp
from jax import lax
from jax.experimental import pallas as pl
from jax.experimental.pallas import tpu as pltpu
from jax.sharding import PartitionSpec as P

MOMENT_DECAY = 0.95
STAT_DECAY = 0.9
ADAM_EPS = 1e-08
PRECON_EPS = 1e-06

LANES = 128
SUBLANES = 8
MESH = pl.DeviceIdType.MESH


def matmul(a, b, a_dim=1, b_dim=0):
    return lax.dot_general(
        a, b, (((a_dim,), (b_dim,)), ((), ())), preferred_element_type=jnp.float32
    )


def alternate(count):
    return sorted(range(1, count), key=lambda k: (-min(k, count - k), k))


def exchange(
    depth,
    across,
    grad_hbm,
    moment_hbm,
    order_hbm,
    left_stat_hbm,
    right_stat_hbm,
    left_root_hbm,
    right_root_hbm,
    wide_back,
    totals,
    holds_half,
    moment,
    left_stat,
    right_stat,
    order,
    grad,
    left_root,
    right_root,
    wide,
    sent,
    via_z,
    turned_z,
    landed_xy,
    turned_xy,
    via_xy,
    turned_back,
    landed_z,
    block,
    norms,
    norms_core,
    norms_core_sum,
    norms_z,
    norms_z_sum,
    norms_xy,
    load_sem,
    z_send,
    z_recv,
    xy_send,
    xy_recv,
    norm_send,
    norm_recv,
):
    plane = via_xy.shape[1]
    deep = plane // across
    fan = plane * 2
    blocks = depth * fan
    side = block.shape[0]
    pieces = side // LANES
    g = lax.axis_index("group")
    f = lax.axis_index("fsdp")
    xy = f // 2
    core = f % 2
    x = xy // deep
    y = xy % deep
    me = g * fan + f

    loads = [
        pltpu.make_async_copy(source, target, load_sem.at[i])
        for i, (source, target) in enumerate(
            (
                (order_hbm, order),
                (grad_hbm, grad),
                (moment_hbm, moment),
                (left_root_hbm, left_root),
                (right_root_hbm, right_root),
                (left_stat_hbm, left_stat),
                (right_stat_hbm, right_stat),
            )
        )
    ]
    for load in loads:
        load.start()

    barrier = pltpu.get_barrier_semaphore()

    def greet_z(k, carry):
        to = lax.rem(g + k, depth)
        pl.semaphore_signal(barrier, inc=1, device_id=(to, f), device_id_type=MESH)
        return carry

    def greet_f(k, carry):
        to = lax.rem(f + k, fan)
        pl.semaphore_signal(barrier, inc=1, device_id=(g, to), device_id_type=MESH)
        return carry

    lax.fori_loop(1, depth, greet_z, 0, unroll=True)
    lax.fori_loop(1, fan, greet_f, 0, unroll=True)

    loads[0].wait()
    which = lax.broadcasted_iota(jnp.int32, (blocks, blocks), 0)
    holds = jnp.where(which == order[...], 1.0, 0.0)
    holds_half[...] = holds.astype(jnp.bfloat16)
    slots_half = holds.T.astype(jnp.bfloat16)

    def tile(i, j, c):
        first = pl.multiple_of((i * fan + j * 2 + c) * SUBLANES, SUBLANES)
        return wide[pl.ds(first, SUBLANES), :].astype(jnp.bfloat16)

    def widen(target, i, c, part):
        part = part.astype(jnp.float32)
        first = pl.multiple_of((i * fan + c) * SUBLANES, SUBLANES)
        for j in range(plane):
            target[pl.ds(first + j * 2 * SUBLANES, SUBLANES), :] = part[j]

    near_first = sorted(
        range(1, plane),
        key=lambda j: (
            min(j // deep, across - j // deep) + min(j % deep, deep - j % deep),
            j,
        ),
    )

    def place(j):
        tx = lax.rem(x + j // deep, across)
        ty = lax.rem(y + j % deep, deep)
        return tx * deep + ty

    def send_z(j, source, target, half):
        to = lax.rem(g + j, depth)
        pltpu.make_async_remote_copy(
            src_ref=source.at[way, to],
            dst_ref=target.at[way, g],
            send_sem=z_send.at[way, half],
            recv_sem=z_recv.at[way, half],
            device_id=(to, f),
            device_id_type=MESH,
        ).start()

    def send_xy(source, target, half, to_core, places):
        for j in places:
            to = place(j)
            pltpu.make_async_remote_copy(
                src_ref=source.at[way, to],
                dst_ref=target.at[way, xy],
                send_sem=xy_send.at[way, half],
                recv_sem=xy_recv.at[way, half],
                device_id=(g, to * 2 + to_core),
                device_id_type=MESH,
            ).start()

    def wait(part, sem):
        pltpu.make_async_copy(part, part, sem).wait()

    def begin():
        for k in alternate(depth):
            to = lax.rem(g + k, depth)
            for j in range(plane):
                sent[way, to, j] = tile(to, j, core)
            send_z(k, sent, via_z, 0)

        def fill(i, carry):
            for j in range(plane):
                turned_xy[way, j, i] = tile(i, j, 1 - core)
            return carry

        lax.fori_loop(0, depth, fill, 0)
        send_xy(turned_xy, via_xy, 1, 1 - core, near_first[::-1] + [0])
        for j in range(plane):
            via_z[way, g, j] = tile(g, j, core)

    def go_on_z():
        wait(via_xy.at[way], xy_recv.at[way, 1])
        for i in range(depth):
            turned_back[way, i] = via_xy[way, :, i]
        for k in alternate(depth):
            send_z(k, turned_back, landed_z, 1)
        landed_z[way, g] = turned_back[way, g]

    def go_on_xy():
        wait(via_z.at[way, pl.ds(0, depth - 1)], z_recv.at[way, 0])
        for i in range(depth):
            turned_z[way, :, i] = via_z[way, i]
        send_xy(turned_z, landed_xy, 0, core, near_first[::-1])
        landed_xy[way, xy] = turned_z[way, xy]

    def end(target):
        wait(landed_xy.at[way, pl.ds(0, plane - 1)], xy_recv.at[way, 0])

        def from_xy(i, carry):
            widen(target, i, core, landed_xy[way, :, i])
            return carry

        lax.fori_loop(0, depth, from_xy, 0)
        wait(landed_z.at[way, pl.ds(0, depth - 1)], z_recv.at[way, 1])

        def from_z(i, carry):
            widen(target, i, 1 - core, landed_z[way, i])
            return carry

        lax.fori_loop(0, depth, from_z, 0)

    way = 0
    loads[1].wait()
    for c in range(0, SUBLANES, 2):
        pair = matmul(slots_half, grad[:, c * LANES : (c + 2) * LANES])
        wide[pl.ds(c, blocks, stride=SUBLANES), :] = pair[:, :LANES]
        wide[pl.ds(c + 1, blocks, stride=SUBLANES), :] = pair[:, LANES:]
    pl.semaphore_wait(barrier, depth - 1 + fan - 1)
    begin()

    def adam(first, last):
        tall = min(blocks, 32)
        share = jnp.zeros((1, blocks), jnp.float32)
        for i in range(first, last, tall):
            rows = pl.ds(i, tall)
            gradient = grad[rows, :].astype(jnp.float32)
            second = MOMENT_DECAY * moment[rows, :] + (1.0 - MOMENT_DECAY) * gradient * gradient
            moment[rows, :] = second
            direction = gradient / (jnp.sqrt(second) + ADAM_EPS)
            squares = jnp.sum(direction * direction, axis=1, keepdims=True)
            share = share + jnp.sum(holds[i : i + tall, :] * squares, axis=0, keepdims=True)
        return share

    loads[2].wait()
    split = blocks // 2 if blocks > 32 else blocks
    norms[0:1, :] = adam(0, split)
    go_on_z()
    norms[0:1, :] += adam(split, blocks)
    go_on_xy()

    end(wide)
    for c in range(pieces):
        block[:, c * LANES : (c + 1) * LANES] = wide[pl.ds(c, side, stride=pieces), :].astype(
            jnp.bfloat16
        )
    loads[3].wait()
    loads[4].wait()
    half = matmul(left_root[...], block[...]).astype(jnp.bfloat16)
    full = matmul(half, right_root[...])
    for c in range(pieces):
        wide[pl.ds(c, side, stride=pieces), :] = full[:, c * LANES : (c + 1) * LANES]

    way = 1
    begin()

    lane = lax.broadcasted_iota(jnp.int32, (1, blocks), 1)
    precon_sq = jnp.sum(full * full, keepdims=True)
    norms[1:2, :] = jnp.where(lane == me, precon_sq, 0.0)

    swap = pltpu.make_async_remote_copy(
        src_ref=norms,
        dst_ref=norms_core,
        send_sem=norm_send.at[0],
        recv_sem=norm_recv.at[0],
        device_id=(g, xy * 2 + 1 - core),
        device_id_type=MESH,
    )
    swap.start()

    def norm_z(j, carry):
        pltpu.make_async_remote_copy(
            src_ref=norms_core_sum,
            dst_ref=norms_z.at[g],
            send_sem=norm_send.at[1],
            recv_sem=norm_recv.at[1],
            device_id=(lax.rem(g + j, depth), f),
            device_id_type=MESH,
        ).start()
        return carry

    loads[5].wait()
    left = matmul(block[...], block[...], 1, 1)
    left_stat[...] = STAT_DECAY * left_stat[...] + (1.0 - STAT_DECAY) * left / side
    go_on_z()
    swap.wait()
    norms_core_sum[...] = norms[...] + norms_core[...]
    lax.fori_loop(1, depth, norm_z, 0)
    loads[6].wait()
    right = matmul(block[...], block[...], 0, 0)
    right_stat[...] = STAT_DECAY * right_stat[...] + (1.0 - STAT_DECAY) * right / side
    go_on_xy()
    wait(norms_z.at[pl.ds(0, depth - 1)], norm_recv.at[1])
    norms_z[g] = norms_core_sum[...]
    norms_z_sum[...] = jnp.sum(norms_z[...], axis=0)
    for j in near_first:
        pltpu.make_async_remote_copy(
            src_ref=norms_z_sum,
            dst_ref=norms_xy.at[xy],
            send_sem=norm_send.at[2],
            recv_sem=norm_recv.at[2],
            device_id=(g, place(j) * 2 + core),
            device_id_type=MESH,
        ).start()
    end(wide_back)
    wait(norms_xy.at[pl.ds(0, plane - 1)], norm_recv.at[2])
    norms_xy[xy] = norms_z_sum[...]
    totals[...] = jnp.sum(norms_xy[...], axis=0)

    for way in range(2):
        wait(via_z.at[way, pl.ds(0, depth - 1)], z_send.at[way, 0])
        wait(landed_z.at[way, pl.ds(0, depth - 1)], z_send.at[way, 1])
        wait(landed_xy.at[way, pl.ds(0, plane - 1)], xy_send.at[way, 0])
        wait(via_xy.at[way], xy_send.at[way, 1])
    wait(norms_z.at[pl.ds(0, depth - 1)], norm_send.at[1])
    wait(norms_xy.at[pl.ds(0, plane - 1)], norm_send.at[2])


def write(
    wide,
    totals,
    holds,
    moment,
    left_stat,
    right_stat,
    update_hbm,
    moment_hbm,
    left_hbm,
    right_hbm,
    update,
    sems,
):
    stores = [
        pltpu.make_async_copy(moment, moment_hbm, sems.at[0]),
        pltpu.make_async_copy(left_stat, left_hbm, sems.at[1]),
        pltpu.make_async_copy(right_stat, right_hbm, sems.at[2]),
    ]
    for store in stores:
        store.start()
    blocks = update.shape[0]
    scale = jnp.sqrt(totals[0:1, :]) / (jnp.sqrt(totals[1:2, :]) + PRECON_EPS)
    scale = jnp.sum(holds[...].astype(jnp.float32) * scale, axis=1, keepdims=True)
    for c in range(0, SUBLANES, 2):
        pair = jnp.concatenate(
            [wide[pl.ds(c + i, blocks, stride=SUBLANES), :] for i in range(2)], axis=1
        ).astype(jnp.bfloat16)
        columns = pl.ds(c * LANES, 2 * LANES)
        update[:, columns] = (matmul(holds[...], pair) * scale).astype(jnp.bfloat16)
        stores.append(
            pltpu.make_async_copy(update.at[:, columns], update_hbm.at[:, columns], sems.at[3 + c // 2])
        )
        stores[-1].start()
    for store in stores:
        store.wait()


def shards(across, grad, moment, order, left_stat, right_stat, left_root, right_root):
    depth = lax.axis_size("group")
    fan = lax.axis_size("fsdp")
    plane = fan // 2
    blocks, entries = grad.shape
    side = left_stat.shape[-1]
    f32, bf16 = jnp.float32, jnp.bfloat16
    tile = (SUBLANES, LANES)
    hbm = pl.BlockSpec(memory_space=pltpu.HBM)
    vmem = pl.BlockSpec(memory_space=pltpu.VMEM)
    order = order.reshape(1, blocks)
    entry_shapes = jax.ShapeDtypeStruct((blocks, entries), f32)
    stat_shapes = jax.ShapeDtypeStruct((side, side), f32)
    wide, totals, holds, moment_new, left_new, right_new = pl.pallas_call(
        functools.partial(exchange, depth, across),
        out_shape=(
            jax.ShapeDtypeStruct((blocks * SUBLANES, LANES), f32),
            jax.ShapeDtypeStruct((2, blocks), f32),
            jax.ShapeDtypeStruct((blocks, blocks), bf16),
            entry_shapes,
            stat_shapes,
            stat_shapes,
        ),
        in_specs=[hbm] * 7,
        out_specs=(vmem,) * 6,
        scratch_shapes=[
            pltpu.VMEM((1, blocks), jnp.int32),
            pltpu.VMEM((blocks, entries), bf16),
            pltpu.VMEM((side, side), bf16),
            pltpu.VMEM((side, side), bf16),
            pltpu.VMEM((blocks * SUBLANES, LANES), f32),
            pltpu.VMEM((2, depth, plane, *tile), bf16),
            pltpu.VMEM((2, depth, plane, *tile), bf16),
            pltpu.VMEM((2, plane, depth, *tile), bf16),
            pltpu.VMEM((2, plane, depth, *tile), bf16),
            pltpu.VMEM((2, plane, depth, *tile), bf16),
            pltpu.VMEM((2, plane, depth, *tile), bf16),
            pltpu.VMEM((2, depth, plane, *tile), bf16),
            pltpu.VMEM((2, depth, plane, *tile), bf16),
            pltpu.VMEM((side, side), bf16),
            pltpu.VMEM((2, blocks), f32),
            pltpu.VMEM((2, blocks), f32),
            pltpu.VMEM((2, blocks), f32),
            pltpu.VMEM((depth, 2, blocks), f32),
            pltpu.VMEM((2, blocks), f32),
            pltpu.VMEM((plane, 2, blocks), f32),
            pltpu.SemaphoreType.DMA((7,)),
            pltpu.SemaphoreType.DMA((2, 2)),
            pltpu.SemaphoreType.DMA((2, 2)),
            pltpu.SemaphoreType.DMA((2, 2)),
            pltpu.SemaphoreType.DMA((2, 2)),
            pltpu.SemaphoreType.DMA((3,)),
            pltpu.SemaphoreType.DMA((3,)),
        ],
        compiler_params=pltpu.CompilerParams(
            collective_id=0, has_side_effects=True, vmem_limit_bytes=40 * 1024 * 1024
        ),
        cost_estimate=pl.CostEstimate(
            flops=8 * side**3 + 2 * blocks * blocks * entries,
            bytes_accessed=6 * blocks * entries + 12 * side * side,
            transcendentals=2 * blocks * entries,
        ),
    )(
        *(
            pltpu.with_memory_space_constraint(operand, pltpu.HBM)
            for operand in (
                grad,
                moment,
                order,
                left_stat[0],
                right_stat[0],
                left_root[0],
                right_root[0],
            )
        )
    )
    update, moment_new, left_new, right_new = pl.pallas_call(
        write,
        out_shape=(
            jax.ShapeDtypeStruct((blocks, entries), bf16),
            entry_shapes,
            stat_shapes,
            stat_shapes,
        ),
        in_specs=[vmem] * 6,
        out_specs=(hbm,) * 4,
        scratch_shapes=[
            pltpu.VMEM((blocks, entries), bf16),
            pltpu.SemaphoreType.DMA((7,)),
        ],
        compiler_params=pltpu.CompilerParams(vmem_limit_bytes=40 * 1024 * 1024),
        cost_estimate=pl.CostEstimate(
            flops=2 * blocks * blocks * entries,
            bytes_accessed=6 * blocks * entries + 8 * side * side,
            transcendentals=0,
        ),
    )(wide, totals, holds, moment_new, left_new, right_new)
    return (update, moment_new, left_new[None], right_new[None])


def solution(mesh):
    across = 4 if mesh.shape["fsdp"] == 32 else 2
    placed = (
        P(None, ("group", "fsdp")),
        P(None, ("group", "fsdp")),
        P(),
        P(("group", "fsdp"), None, None),
        P(("group", "fsdp"), None, None),
        P(("group", "fsdp"), None, None),
        P(("group", "fsdp"), None, None),
    )
    return jax.shard_map(
        functools.partial(shards, across),
        mesh=mesh,
        in_specs=placed,
        out_specs=(
            P(None, ("group", "fsdp")),
            P(None, ("group", "fsdp")),
            P(("group", "fsdp"), None, None),
            P(("group", "fsdp"), None, None),
        ),
        check_vma=False,
    )
```

```python
import functools

import jax
import jax.numpy as jnp
from jax import lax
from jax.experimental import pallas as pl
from jax.experimental.pallas import tpu as pltpu
from jax.sharding import PartitionSpec as P

MOMENT_DECAY = 0.95
STAT_DECAY = 0.9
ADAM_EPS = 1e-08
PRECON_EPS = 1e-06

LANES = 128
SUBLANES = 8
MESH = pl.DeviceIdType.MESH


def matmul(a, b, a_dim=1, b_dim=0):
    return lax.dot_general(
        a, b, (((a_dim,), (b_dim,)), ((), ())), preferred_element_type=jnp.float32
    )


def alternate(count):
    return sorted(range(1, count), key=lambda k: (-min(k, count - k), k))


def exchange(
    depth,
    across,
    grad_hbm,
    moment_hbm,
    order_hbm,
    left_stat_hbm,
    right_stat_hbm,
    left_root_hbm,
    right_root_hbm,
    wide_back,
    totals,
    holds_half,
    moment,
    left_stat,
    right_stat,
    order,
    grad,
    left_root,
    right_root,
    wide,
    sent,
    via_z,
    turned_z,
    landed_xy,
    turned_xy,
    via_xy,
    turned_back,
    landed_z,
    block,
    norms,
    norms_core,
    norms_core_sum,
    norms_z,
    norms_z_sum,
    norms_xy,
    load_sem,
    z_send,
    z_recv,
    xy_send,
    xy_recv,
    norm_send,
    norm_recv,
):
    plane = via_xy.shape[1]
    deep = plane // across
    fan = plane * 2
    blocks = depth * fan
    side = block.shape[0]
    pieces = side // LANES
    g = lax.axis_index("group")
    f = lax.axis_index("fsdp")
    xy = f // 2
    core = f % 2
    x = xy // deep
    y = xy % deep
    me = g * fan + f

    loads = [
        pltpu.make_async_copy(source, target, load_sem.at[i])
        for i, (source, target) in enumerate(
            (
                (order_hbm, order),
                (grad_hbm, grad),
                (moment_hbm, moment),
                (left_root_hbm, left_root),
                (right_root_hbm, right_root),
                (left_stat_hbm, left_stat),
                (right_stat_hbm, right_stat),
            )
        )
    ]
    for load in loads:
        load.start()

    barrier = pltpu.get_barrier_semaphore()

    def greet_z(k, carry):
        to = lax.rem(g + k, depth)
        pl.semaphore_signal(barrier, inc=1, device_id=(to, f), device_id_type=MESH)
        return carry

    def greet_f(k, carry):
        to = lax.rem(f + k, fan)
        pl.semaphore_signal(barrier, inc=1, device_id=(g, to), device_id_type=MESH)
        return carry

    lax.fori_loop(1, depth, greet_z, 0)
    lax.fori_loop(1, fan, greet_f, 0)

    loads[0].wait()
    which = lax.broadcasted_iota(jnp.int32, (blocks, blocks), 0)
    holds = jnp.where(which == order[...], 1.0, 0.0)
    holds_half[...] = holds.astype(jnp.bfloat16)
    slots_half = holds.T.astype(jnp.bfloat16)

    def rows_of(i, j, c):
        return pl.ds(pl.multiple_of((i * fan + j * 2 + c) * SUBLANES, SUBLANES), SUBLANES)

    def tile(i, j, c):
        return wide[rows_of(i, j, c), :].astype(jnp.bfloat16)

    apart = [k for k in range(1, across, 2)] + [k for k in range(2, across, 2)] + [0]
    part = plane // 2
    chunks = [pl.ds(k * part, part) for k in range(2)]

    def place(r, sign):
        k = apart[r // deep]
        return lax.rem(x + (k if sign > 0 else across - k), across) * deep + r % deep

    def send_z(j, k, source, target, half):
        to = lax.rem(g + j, depth)
        pltpu.make_async_remote_copy(
            src_ref=source.at[way, to, chunks[k]],
            dst_ref=target.at[way, g, chunks[k]],
            send_sem=z_send.at[way, half],
            recv_sem=z_recv.at[way, half, k if half == 0 else 0],
            device_id=(to, f),
            device_id_type=MESH,
        ).start()

    def send_xy(k, source, target, half, to_core, skip_self):
        for r in range(k * part, (k + 1) * part):
            dx = apart[r // deep]
            turns = [j for j in (alternate(deep) + [0]) if dx or j or not skip_self]
            if r % deep >= len(turns):
                continue
            to_x = lax.rem(x + dx, across)
            to_y = lax.rem(y + turns[r % deep], deep)
            to = to_x * deep + to_y
            pltpu.make_async_remote_copy(
                src_ref=source.at[way, r // deep * deep + to_y],
                dst_ref=target.at[way, r // deep * deep + y if half else xy],
                send_sem=xy_send.at[way, half],
                recv_sem=xy_recv.at[way, half, k if half else 0],
                device_id=(g, to * 2 + to_core),
                device_id_type=MESH,
            ).start()

    def wait(arrived, sem):
        pltpu.make_async_copy(arrived, arrived, sem).wait()

    def begin():
        for k in range(2):
            for j in alternate(depth):
                to = lax.rem(g + j, depth)
                for r in range(k * part, (k + 1) * part):
                    sent[way, to, r] = tile(to, place(r, 1), core)
                send_z(j, k, sent, via_z, 0)

            def fill(i, carry, k=k):
                for r in range(k * part, (k + 1) * part):
                    turned_xy[way, r, i] = tile(i, place(r, 1), 1 - core)
                return carry

            lax.fori_loop(0, depth, fill, 0)
            send_xy(k, turned_xy, via_xy, 1, 1 - core, False)
        for r in range(plane):
            via_z[way, g, r] = tile(g, place(r, 1), core)

    def go_on_z(k):
        wait(via_xy.at[way, chunks[k]], xy_recv.at[way, 1, k])
        for i in range(depth):
            turned_back[way, i, chunks[k]] = via_xy[way, chunks[k], i]
        for j in alternate(depth):
            send_z(j, k, turned_back, landed_z, 1)

    def go_on_xy(k):
        wait(via_z.at[way, pl.ds(0, depth - 1), chunks[k]], z_recv.at[way, 0, k])
        for i in range(depth):
            turned_z[way, chunks[k], i] = via_z[way, i, chunks[k]]
        send_xy(k, turned_z, landed_xy, 0, core, True)

    def go_on():
        for k in range(2):
            go_on_z(k)
            go_on_xy(k)
        landed_z[way, g] = turned_back[way, g]
        landed_xy[way, xy] = turned_z[way, (len(apart) - 1) * deep + y]

    def end(target):
        wait(landed_xy.at[way, pl.ds(0, plane - 1)], xy_recv.at[way, 0, 0])

        def from_xy(i, carry):
            arrived = landed_xy[way, :, i].astype(jnp.float32)
            for j in range(plane):
                target[rows_of(i, j, core), :] = arrived[j]
            return carry

        lax.fori_loop(0, depth, from_xy, 0)
        wait(landed_z.at[way, pl.ds(0, depth - 1)], z_recv.at[way, 1, 0])

        def from_z(i, carry):
            arrived = landed_z[way, i].astype(jnp.float32)
            for r in range(plane):
                target[rows_of(i, place(r, -1), 1 - core), :] = arrived[r]
            return carry

        lax.fori_loop(0, depth, from_z, 0)

    way = 0
    loads[1].wait()
    for c in range(0, SUBLANES, 2):
        pair = matmul(slots_half, grad[:, c * LANES : (c + 2) * LANES])
        wide[pl.ds(c, blocks, stride=SUBLANES), :] = pair[:, :LANES]
        wide[pl.ds(c + 1, blocks, stride=SUBLANES), :] = pair[:, LANES:]
    pl.semaphore_wait(barrier, depth - 1 + fan - 1)
    begin()

    loads[2].wait()
    tall = min(blocks, 32)
    share = jnp.zeros((1, blocks), jnp.float32)
    for i in range(0, blocks, tall):
        rows = pl.ds(i, tall)
        gradient = grad[rows, :].astype(jnp.float32)
        second = MOMENT_DECAY * moment[rows, :] + (1.0 - MOMENT_DECAY) * gradient * gradient
        moment[rows, :] = second
        direction = gradient / (jnp.sqrt(second) + ADAM_EPS)
        squares = jnp.sum(direction * direction, axis=1, keepdims=True)
        share = share + jnp.sum(holds[i : i + tall, :] * squares, axis=0, keepdims=True)
    norms[0:1, :] = share
    go_on()

    end(wide)
    for c in range(pieces):
        block[:, c * LANES : (c + 1) * LANES] = wide[pl.ds(c, side, stride=pieces), :].astype(
            jnp.bfloat16
        )
    loads[3].wait()
    loads[4].wait()
    half = matmul(left_root[...], block[...]).astype(jnp.bfloat16)
    full = matmul(half, right_root[...])
    for c in range(pieces):
        wide[pl.ds(c, side, stride=pieces), :] = full[:, c * LANES : (c + 1) * LANES]

    way = 1
    begin()

    lane = lax.broadcasted_iota(jnp.int32, (1, blocks), 1)
    precon_sq = jnp.sum(full * full, keepdims=True)
    norms[1:2, :] = jnp.where(lane == me, precon_sq, 0.0)

    swap = pltpu.make_async_remote_copy(
        src_ref=norms,
        dst_ref=norms_core,
        send_sem=norm_send.at[0],
        recv_sem=norm_recv.at[0],
        device_id=(g, xy * 2 + 1 - core),
        device_id_type=MESH,
    )
    swap.start()

    def norm_z(j, carry):
        pltpu.make_async_remote_copy(
            src_ref=norms_core_sum,
            dst_ref=norms_z.at[g],
            send_sem=norm_send.at[1],
            recv_sem=norm_recv.at[1],
            device_id=(lax.rem(g + j, depth), f),
            device_id_type=MESH,
        ).start()
        return carry

    loads[5].wait()
    left = matmul(block[...], block[...], 1, 1)
    left_stat[...] = STAT_DECAY * left_stat[...] + (1.0 - STAT_DECAY) * left / side
    swap.wait()
    norms_core_sum[...] = norms[...] + norms_core[...]
    lax.fori_loop(1, depth, norm_z, 0)
    loads[6].wait()
    right = matmul(block[...], block[...], 0, 0)
    right_stat[...] = STAT_DECAY * right_stat[...] + (1.0 - STAT_DECAY) * right / side
    go_on()
    wait(norms_z.at[pl.ds(0, depth - 1)], norm_recv.at[1])
    norms_z[g] = norms_core_sum[...]
    norms_z_sum[...] = jnp.sum(norms_z[...], axis=0)

    def norm_xy(j, carry):
        to = lax.rem(xy + j, plane)
        pltpu.make_async_remote_copy(
            src_ref=norms_z_sum,
            dst_ref=norms_xy.at[xy],
            send_sem=norm_send.at[2],
            recv_sem=norm_recv.at[2],
            device_id=(g, to * 2 + core),
            device_id_type=MESH,
        ).start()
        return carry

    lax.fori_loop(1, plane, norm_xy, 0)
    end(wide_back)
    wait(norms_xy.at[pl.ds(0, plane - 1)], norm_recv.at[2])
    norms_xy[xy] = norms_z_sum[...]
    totals[...] = jnp.sum(norms_xy[...], axis=0)

    for way in range(2):
        wait(via_z.at[way, pl.ds(0, depth - 1)], z_send.at[way, 0])
        wait(landed_z.at[way, pl.ds(0, depth - 1)], z_send.at[way, 1])
        wait(landed_xy.at[way, pl.ds(0, plane - 1)], xy_send.at[way, 0])
        wait(via_xy.at[way], xy_send.at[way, 1])
    wait(norms_z.at[pl.ds(0, depth - 1)], norm_send.at[1])
    wait(norms_xy.at[pl.ds(0, plane - 1)], norm_send.at[2])


def write(
    wide,
    totals,
    holds,
    moment,
    left_stat,
    right_stat,
    update_hbm,
    moment_hbm,
    left_hbm,
    right_hbm,
    update,
    sems,
):
    stores = [
        pltpu.make_async_copy(moment, moment_hbm, sems.at[0]),
        pltpu.make_async_copy(left_stat, left_hbm, sems.at[1]),
        pltpu.make_async_copy(right_stat, right_hbm, sems.at[2]),
    ]
    for store in stores:
        store.start()
    blocks = update.shape[0]
    scale = jnp.sqrt(totals[0:1, :]) / (jnp.sqrt(totals[1:2, :]) + PRECON_EPS)
    scale = jnp.sum(holds[...].astype(jnp.float32) * scale, axis=1, keepdims=True)
    for c in range(0, SUBLANES, 2):
        pair = jnp.concatenate(
            [wide[pl.ds(c + i, blocks, stride=SUBLANES), :] for i in range(2)], axis=1
        ).astype(jnp.bfloat16)
        columns = pl.ds(c * LANES, 2 * LANES)
        update[:, columns] = (matmul(holds[...], pair) * scale).astype(jnp.bfloat16)
        stores.append(
            pltpu.make_async_copy(update.at[:, columns], update_hbm.at[:, columns], sems.at[3 + c // 2])
        )
        stores[-1].start()
    for store in stores:
        store.wait()


def shards(across, grad, moment, order, left_stat, right_stat, left_root, right_root):
    depth = lax.axis_size("group")
    fan = lax.axis_size("fsdp")
    plane = fan // 2
    blocks, entries = grad.shape
    side = left_stat.shape[-1]
    f32, bf16 = jnp.float32, jnp.bfloat16
    tile = (SUBLANES, LANES)
    hbm = pl.BlockSpec(memory_space=pltpu.HBM)
    vmem = pl.BlockSpec(memory_space=pltpu.VMEM)
    order = order.reshape(1, blocks)
    entry_shapes = jax.ShapeDtypeStruct((blocks, entries), f32)
    stat_shapes = jax.ShapeDtypeStruct((side, side), f32)
    wide, totals, holds, moment_new, left_new, right_new = pl.pallas_call(
        functools.partial(exchange, depth, across),
        out_shape=(
            jax.ShapeDtypeStruct((blocks * SUBLANES, LANES), f32),
            jax.ShapeDtypeStruct((2, blocks), f32),
            jax.ShapeDtypeStruct((blocks, blocks), bf16),
            entry_shapes,
            stat_shapes,
            stat_shapes,
        ),
        in_specs=[hbm] * 7,
        out_specs=(vmem,) * 6,
        scratch_shapes=[
            pltpu.VMEM((1, blocks), jnp.int32),
            pltpu.VMEM((blocks, entries), bf16),
            pltpu.VMEM((side, side), bf16),
            pltpu.VMEM((side, side), bf16),
            pltpu.VMEM((blocks * SUBLANES, LANES), f32),
            pltpu.VMEM((2, depth, plane, *tile), bf16),
            pltpu.VMEM((2, depth, plane, *tile), bf16),
            pltpu.VMEM((2, plane, depth, *tile), bf16),
            pltpu.VMEM((2, plane, depth, *tile), bf16),
            pltpu.VMEM((2, plane, depth, *tile), bf16),
            pltpu.VMEM((2, plane, depth, *tile), bf16),
            pltpu.VMEM((2, depth, plane, *tile), bf16),
            pltpu.VMEM((2, depth, plane, *tile), bf16),
            pltpu.VMEM((side, side), bf16),
            pltpu.VMEM((2, blocks), f32),
            pltpu.VMEM((2, blocks), f32),
            pltpu.VMEM((2, blocks), f32),
            pltpu.VMEM((depth, 2, blocks), f32),
            pltpu.VMEM((2, blocks), f32),
            pltpu.VMEM((plane, 2, blocks), f32),
            pltpu.SemaphoreType.DMA((7,)),
            pltpu.SemaphoreType.DMA((2, 2)),
            pltpu.SemaphoreType.DMA((2, 2, 2)),
            pltpu.SemaphoreType.DMA((2, 2)),
            pltpu.SemaphoreType.DMA((2, 2, 2)),
            pltpu.SemaphoreType.DMA((3,)),
            pltpu.SemaphoreType.DMA((3,)),
        ],
        compiler_params=pltpu.CompilerParams(
            collective_id=0, has_side_effects=True, vmem_limit_bytes=40 * 1024 * 1024
        ),
        cost_estimate=pl.CostEstimate(
            flops=8 * side**3 + 2 * blocks * blocks * entries,
            bytes_accessed=6 * blocks * entries + 12 * side * side,
            transcendentals=2 * blocks * entries,
        ),
    )(
        *(
            pltpu.with_memory_space_constraint(operand, pltpu.HBM)
            for operand in (
                grad,
                moment,
                order,
                left_stat[0],
                right_stat[0],
                left_root[0],
                right_root[0],
            )
        )
    )
    update, moment_new, left_new, right_new = pl.pallas_call(
        write,
        out_shape=(
            jax.ShapeDtypeStruct((blocks, entries), bf16),
            entry_shapes,
            stat_shapes,
            stat_shapes,
        ),
        in_specs=[vmem] * 6,
        out_specs=(hbm,) * 4,
        scratch_shapes=[
            pltpu.VMEM((blocks, entries), bf16),
            pltpu.SemaphoreType.DMA((7,)),
        ],
        compiler_params=pltpu.CompilerParams(vmem_limit_bytes=40 * 1024 * 1024),
        cost_estimate=pl.CostEstimate(
            flops=2 * blocks * blocks * entries,
            bytes_accessed=6 * blocks * entries + 8 * side * side,
            transcendentals=0,
        ),
    )(wide, totals, holds, moment_new, left_new, right_new)
    return (update, moment_new, left_new[None], right_new[None])


def solution(mesh):
    across = 4 if mesh.shape["fsdp"] == 32 else 2
    placed = (
        P(None, ("group", "fsdp")),
        P(None, ("group", "fsdp")),
        P(),
        P(("group", "fsdp"), None, None),
        P(("group", "fsdp"), None, None),
        P(("group", "fsdp"), None, None),
        P(("group", "fsdp"), None, None),
    )
    return jax.shard_map(
        functools.partial(shards, across),
        mesh=mesh,
        in_specs=placed,
        out_specs=(
            P(None, ("group", "fsdp")),
            P(None, ("group", "fsdp")),
            P(("group", "fsdp"), None, None),
            P(("group", "fsdp"), None, None),
        ),
        check_vma=False,
    )
```

```python
import functools

import jax
import jax.numpy as jnp
from jax import lax
from jax.experimental import pallas as pl
from jax.experimental.pallas import tpu as pltpu
from jax.sharding import PartitionSpec as P

MOMENT_DECAY = 0.95
STAT_DECAY = 0.9
ADAM_EPS = 1e-08
PRECON_EPS = 1e-06

LANES = 128
SUBLANES = 8
MESH = pl.DeviceIdType.MESH


def matmul(a, b, a_dim=1, b_dim=0):
    return lax.dot_general(
        a, b, (((a_dim,), (b_dim,)), ((), ())), preferred_element_type=jnp.float32
    )


def alternate(count):
    return sorted(range(1, count), key=lambda k: (-min(k, count - k), k))


def exchange(
    depth,
    across,
    grad_hbm,
    moment_hbm,
    order_hbm,
    left_stat_hbm,
    right_stat_hbm,
    left_root_hbm,
    right_root_hbm,
    wide_back,
    totals,
    holds_half,
    moment,
    left_stat,
    right_stat,
    order,
    grad,
    left_root,
    right_root,
    wide,
    sent,
    via_z,
    turned_z,
    landed_xy,
    turned_xy,
    via_xy,
    turned_back,
    landed_z,
    block,
    norms,
    norms_core,
    norms_core_sum,
    norms_z,
    norms_z_sum,
    norms_xy,
    load_sem,
    z_send,
    z_recv,
    xy_send,
    xy_recv,
    norm_send,
    norm_recv,
):
    plane = via_xy.shape[1]
    deep = plane // across
    fan = plane * 2
    blocks = depth * fan
    side = block.shape[0]
    pieces = side // LANES
    g = lax.axis_index("group")
    f = lax.axis_index("fsdp")
    xy = f // 2
    core = f % 2
    x = xy // deep
    y = xy % deep
    me = g * fan + f

    loads = [
        pltpu.make_async_copy(source, target, load_sem.at[i])
        for i, (source, target) in enumerate(
            (
                (order_hbm, order),
                (grad_hbm, grad),
                (moment_hbm, moment),
                (left_root_hbm, left_root),
                (right_root_hbm, right_root),
                (left_stat_hbm, left_stat),
                (right_stat_hbm, right_stat),
            )
        )
    ]
    for load in loads:
        load.start()

    barrier = pltpu.get_barrier_semaphore()

    def greet_z(k, carry):
        to = lax.rem(g + k, depth)
        pl.semaphore_signal(barrier, inc=1, device_id=(to, f), device_id_type=MESH)
        return carry

    def greet_f(k, carry):
        to = lax.rem(f + k, fan)
        pl.semaphore_signal(barrier, inc=1, device_id=(g, to), device_id_type=MESH)
        return carry

    lax.fori_loop(1, depth, greet_z, 0)
    lax.fori_loop(1, fan, greet_f, 0)

    loads[0].wait()
    which = lax.broadcasted_iota(jnp.int32, (blocks, blocks), 0)
    holds = jnp.where(which == order[...], 1.0, 0.0)
    holds_half[...] = holds.astype(jnp.bfloat16)
    slots_half = holds.T.astype(jnp.bfloat16)

    def rows_of(i, j, c):
        return pl.ds(pl.multiple_of((i * fan + j * 2 + c) * SUBLANES, SUBLANES), SUBLANES)

    def tile(i, j, c):
        return wide[rows_of(i, j, c), :].astype(jnp.bfloat16)

    apart = [k for k in range(1, across, 2)] + [k for k in range(2, across, 2)] + [0]
    part = plane // 2
    chunks = [pl.ds(k * part, part) for k in range(2)]

    def place(r, sign):
        k = apart[r // deep]
        return lax.rem(x + (k if sign > 0 else across - k), across) * deep + r % deep

    def send_z(j, k, source, target, half):
        to = lax.rem(g + j, depth)
        pltpu.make_async_remote_copy(
            src_ref=source.at[way, to, chunks[k]],
            dst_ref=target.at[way, g, chunks[k]],
            send_sem=z_send.at[way, half],
            recv_sem=z_recv.at[way, half, k if half == 0 else 0],
            device_id=(to, f),
            device_id_type=MESH,
        ).start()

    def send_xy(k, source, target, half, to_core, skip_self):
        for r in range(k * part, (k + 1) * part):
            dx = apart[r // deep]
            turns = [j for j in (alternate(deep) + [0]) if dx or j or not skip_self]
            if r % deep >= len(turns):
                continue
            to_x = lax.rem(x + dx, across)
            to_y = lax.rem(y + turns[r % deep], deep)
            to = to_x * deep + to_y
            pltpu.make_async_remote_copy(
                src_ref=source.at[way, r // deep * deep + to_y],
                dst_ref=target.at[way, r // deep * deep + y if half else xy],
                send_sem=xy_send.at[way, half],
                recv_sem=xy_recv.at[way, half, k if half else 0],
                device_id=(g, to * 2 + to_core),
                device_id_type=MESH,
            ).start()

    def wait(arrived, sem):
        pltpu.make_async_copy(arrived, arrived, sem).wait()

    def begin():
        for k in range(2):
            for j in alternate(depth):
                to = lax.rem(g + j, depth)
                for r in range(k * part, (k + 1) * part):
                    sent[way, to, r] = tile(to, place(r, 1), core)
                send_z(j, k, sent, via_z, 0)

            def fill(i, carry, k=k):
                for r in range(k * part, (k + 1) * part):
                    turned_xy[way, r, i] = tile(i, place(r, 1), 1 - core)
                return carry

            lax.fori_loop(0, depth, fill, 0)
            send_xy(k, turned_xy, via_xy, 1, 1 - core, False)
        for r in range(plane):
            via_z[way, g, r] = tile(g, place(r, 1), core)

    def go_on_z(k):
        wait(via_xy.at[way, chunks[k]], xy_recv.at[way, 1, k])
        for i in range(depth):
            turned_back[way, i, chunks[k]] = via_xy[way, chunks[k], i]
        for j in alternate(depth):
            send_z(j, k, turned_back, landed_z, 1)

    def go_on_xy(k):
        wait(via_z.at[way, pl.ds(0, depth - 1), chunks[k]], z_recv.at[way, 0, k])
        for i in range(depth):
            turned_z[way, chunks[k], i] = via_z[way, i, chunks[k]]
        send_xy(k, turned_z, landed_xy, 0, core, True)

    def go_on(between=None):
        for k in range(2):
            go_on_z(k)
            go_on_xy(k)
            if between and k == 0:
                between()
        landed_z[way, g] = turned_back[way, g]
        landed_xy[way, xy] = turned_z[way, (len(apart) - 1) * deep + y]

    def end(target):
        wait(landed_xy.at[way, pl.ds(0, plane - 1)], xy_recv.at[way, 0, 0])

        def from_xy(i, carry):
            arrived = landed_xy[way, :, i].astype(jnp.float32)
            for j in range(plane):
                target[rows_of(i, j, core), :] = arrived[j]
            return carry

        lax.fori_loop(0, depth, from_xy, 0)
        wait(landed_z.at[way, pl.ds(0, depth - 1)], z_recv.at[way, 1, 0])

        def from_z(i, carry):
            arrived = landed_z[way, i].astype(jnp.float32)
            for r in range(plane):
                target[rows_of(i, place(r, -1), 1 - core), :] = arrived[r]
            return carry

        lax.fori_loop(0, depth, from_z, 0)

    way = 0
    loads[1].wait()
    for c in range(0, SUBLANES, 2):
        pair = matmul(slots_half, grad[:, c * LANES : (c + 2) * LANES])
        wide[pl.ds(c, blocks, stride=SUBLANES), :] = pair[:, :LANES]
        wide[pl.ds(c + 1, blocks, stride=SUBLANES), :] = pair[:, LANES:]
    pl.semaphore_wait(barrier, depth - 1 + fan - 1)
    begin()

    def adam(first, last):
        tall = min(blocks, 32)
        share = jnp.zeros((1, blocks), jnp.float32)
        for i in range(first, last, tall):
            rows = pl.ds(i, tall)
            gradient = grad[rows, :].astype(jnp.float32)
            second = MOMENT_DECAY * moment[rows, :] + (1.0 - MOMENT_DECAY) * gradient * gradient
            moment[rows, :] = second
            direction = gradient / (jnp.sqrt(second) + ADAM_EPS)
            squares = jnp.sum(direction * direction, axis=1, keepdims=True)
            share = share + jnp.sum(holds[i : i + tall, :] * squares, axis=0, keepdims=True)
        return share

    loads[2].wait()
    split = blocks // 4 if blocks >= 128 else 0
    norms[0:1, :] = adam(0, split)
    go_on()
    norms[0:1, :] += adam(split, blocks)

    end(wide)
    for c in range(pieces):
        block[:, c * LANES : (c + 1) * LANES] = wide[pl.ds(c, side, stride=pieces), :].astype(
            jnp.bfloat16
        )
    loads[3].wait()
    loads[4].wait()
    half = matmul(left_root[...], block[...]).astype(jnp.bfloat16)
    full = matmul(half, right_root[...])
    for c in range(pieces):
        wide[pl.ds(c, side, stride=pieces), :] = full[:, c * LANES : (c + 1) * LANES]

    way = 1
    begin()

    lane = lax.broadcasted_iota(jnp.int32, (1, blocks), 1)
    precon_sq = jnp.sum(full * full, keepdims=True)
    norms[1:2, :] = jnp.where(lane == me, precon_sq, 0.0)

    swap = pltpu.make_async_remote_copy(
        src_ref=norms,
        dst_ref=norms_core,
        send_sem=norm_send.at[0],
        recv_sem=norm_recv.at[0],
        device_id=(g, xy * 2 + 1 - core),
        device_id_type=MESH,
    )
    swap.start()

    def norm_z(j, carry):
        pltpu.make_async_remote_copy(
            src_ref=norms_core_sum,
            dst_ref=norms_z.at[g],
            send_sem=norm_send.at[1],
            recv_sem=norm_recv.at[1],
            device_id=(lax.rem(g + j, depth), f),
            device_id_type=MESH,
        ).start()
        return carry

    def sum_cores():
        swap.wait()
        norms_core_sum[...] = norms[...] + norms_core[...]
        lax.fori_loop(1, depth, norm_z, 0)

    go_on(sum_cores)
    loads[5].wait()
    left = matmul(block[...], block[...], 1, 1)
    left_stat[...] = STAT_DECAY * left_stat[...] + (1.0 - STAT_DECAY) * left / side
    wait(norms_z.at[pl.ds(0, depth - 1)], norm_recv.at[1])
    norms_z[g] = norms_core_sum[...]
    norms_z_sum[...] = jnp.sum(norms_z[...], axis=0)

    def norm_xy(j, carry):
        to = lax.rem(xy + j, plane)
        pltpu.make_async_remote_copy(
            src_ref=norms_z_sum,
            dst_ref=norms_xy.at[xy],
            send_sem=norm_send.at[2],
            recv_sem=norm_recv.at[2],
            device_id=(g, to * 2 + core),
            device_id_type=MESH,
        ).start()
        return carry

    lax.fori_loop(1, plane, norm_xy, 0)
    loads[6].wait()
    right = matmul(block[...], block[...], 0, 0)
    right_stat[...] = STAT_DECAY * right_stat[...] + (1.0 - STAT_DECAY) * right / side
    end(wide_back)
    wait(norms_xy.at[pl.ds(0, plane - 1)], norm_recv.at[2])
    norms_xy[xy] = norms_z_sum[...]
    totals[...] = jnp.sum(norms_xy[...], axis=0)

    for way in range(2):
        wait(via_z.at[way, pl.ds(0, depth - 1)], z_send.at[way, 0])
        wait(landed_z.at[way, pl.ds(0, depth - 1)], z_send.at[way, 1])
        wait(landed_xy.at[way, pl.ds(0, plane - 1)], xy_send.at[way, 0])
        wait(via_xy.at[way], xy_send.at[way, 1])
    wait(norms_z.at[pl.ds(0, depth - 1)], norm_send.at[1])
    wait(norms_xy.at[pl.ds(0, plane - 1)], norm_send.at[2])


def write(
    wide,
    totals,
    holds,
    moment,
    left_stat,
    right_stat,
    update_hbm,
    moment_hbm,
    left_hbm,
    right_hbm,
    update,
    sems,
):
    stores = [
        pltpu.make_async_copy(moment, moment_hbm, sems.at[0]),
        pltpu.make_async_copy(left_stat, left_hbm, sems.at[1]),
        pltpu.make_async_copy(right_stat, right_hbm, sems.at[2]),
    ]
    for store in stores:
        store.start()
    blocks = update.shape[0]
    scale = jnp.sqrt(totals[0:1, :]) / (jnp.sqrt(totals[1:2, :]) + PRECON_EPS)
    scale = jnp.sum(holds[...].astype(jnp.float32) * scale, axis=1, keepdims=True)
    for c in range(0, SUBLANES, 2):
        pair = jnp.concatenate(
            [wide[pl.ds(c + i, blocks, stride=SUBLANES), :] for i in range(2)], axis=1
        ).astype(jnp.bfloat16)
        columns = pl.ds(c * LANES, 2 * LANES)
        update[:, columns] = (matmul(holds[...], pair) * scale).astype(jnp.bfloat16)
        stores.append(
            pltpu.make_async_copy(update.at[:, columns], update_hbm.at[:, columns], sems.at[3 + c // 2])
        )
        stores[-1].start()
    for store in stores:
        store.wait()


def shards(across, grad, moment, order, left_stat, right_stat, left_root, right_root):
    depth = lax.axis_size("group")
    fan = lax.axis_size("fsdp")
    plane = fan // 2
    blocks, entries = grad.shape
    side = left_stat.shape[-1]
    f32, bf16 = jnp.float32, jnp.bfloat16
    tile = (SUBLANES, LANES)
    hbm = pl.BlockSpec(memory_space=pltpu.HBM)
    vmem = pl.BlockSpec(memory_space=pltpu.VMEM)
    order = order.reshape(1, blocks)
    entry_shapes = jax.ShapeDtypeStruct((blocks, entries), f32)
    stat_shapes = jax.ShapeDtypeStruct((side, side), f32)
    wide, totals, holds, moment_new, left_new, right_new = pl.pallas_call(
        functools.partial(exchange, depth, across),
        out_shape=(
            jax.ShapeDtypeStruct((blocks * SUBLANES, LANES), f32),
            jax.ShapeDtypeStruct((2, blocks), f32),
            jax.ShapeDtypeStruct((blocks, blocks), bf16),
            entry_shapes,
            stat_shapes,
            stat_shapes,
        ),
        in_specs=[hbm] * 7,
        out_specs=(vmem,) * 6,
        scratch_shapes=[
            pltpu.VMEM((1, blocks), jnp.int32),
            pltpu.VMEM((blocks, entries), bf16),
            pltpu.VMEM((side, side), bf16),
            pltpu.VMEM((side, side), bf16),
            pltpu.VMEM((blocks * SUBLANES, LANES), f32),
            pltpu.VMEM((2, depth, plane, *tile), bf16),
            pltpu.VMEM((2, depth, plane, *tile), bf16),
            pltpu.VMEM((2, plane, depth, *tile), bf16),
            pltpu.VMEM((2, plane, depth, *tile), bf16),
            pltpu.VMEM((2, plane, depth, *tile), bf16),
            pltpu.VMEM((2, plane, depth, *tile), bf16),
            pltpu.VMEM((2, depth, plane, *tile), bf16),
            pltpu.VMEM((2, depth, plane, *tile), bf16),
            pltpu.VMEM((side, side), bf16),
            pltpu.VMEM((2, blocks), f32),
            pltpu.VMEM((2, blocks), f32),
            pltpu.VMEM((2, blocks), f32),
            pltpu.VMEM((depth, 2, blocks), f32),
            pltpu.VMEM((2, blocks), f32),
            pltpu.VMEM((plane, 2, blocks), f32),
            pltpu.SemaphoreType.DMA((7,)),
            pltpu.SemaphoreType.DMA((2, 2)),
            pltpu.SemaphoreType.DMA((2, 2, 2)),
            pltpu.SemaphoreType.DMA((2, 2)),
            pltpu.SemaphoreType.DMA((2, 2, 2)),
            pltpu.SemaphoreType.DMA((3,)),
            pltpu.SemaphoreType.DMA((3,)),
        ],
        compiler_params=pltpu.CompilerParams(
            collective_id=0, has_side_effects=True, vmem_limit_bytes=40 * 1024 * 1024
        ),
        cost_estimate=pl.CostEstimate(
            flops=8 * side**3 + 2 * blocks * blocks * entries,
            bytes_accessed=6 * blocks * entries + 12 * side * side,
            transcendentals=2 * blocks * entries,
        ),
    )(
        *(
            pltpu.with_memory_space_constraint(operand, pltpu.HBM)
            for operand in (
                grad,
                moment,
                order,
                left_stat[0],
                right_stat[0],
                left_root[0],
                right_root[0],
            )
        )
    )
    update, moment_new, left_new, right_new = pl.pallas_call(
        write,
        out_shape=(
            jax.ShapeDtypeStruct((blocks, entries), bf16),
            entry_shapes,
            stat_shapes,
            stat_shapes,
        ),
        in_specs=[vmem] * 6,
        out_specs=(hbm,) * 4,
        scratch_shapes=[
            pltpu.VMEM((blocks, entries), bf16),
            pltpu.SemaphoreType.DMA((7,)),
        ],
        compiler_params=pltpu.CompilerParams(vmem_limit_bytes=40 * 1024 * 1024),
        cost_estimate=pl.CostEstimate(
            flops=2 * blocks * blocks * entries,
            bytes_accessed=6 * blocks * entries + 8 * side * side,
            transcendentals=0,
        ),
    )(wide, totals, holds, moment_new, left_new, right_new)
    return (update, moment_new, left_new[None], right_new[None])


def solution(mesh):
    across = 4 if mesh.shape["fsdp"] == 32 else 2
    placed = (
        P(None, ("group", "fsdp")),
        P(None, ("group", "fsdp")),
        P(),
        P(("group", "fsdp"), None, None),
        P(("group", "fsdp"), None, None),
        P(("group", "fsdp"), None, None),
        P(("group", "fsdp"), None, None),
    )
    return jax.shard_map(
        functools.partial(shards, across),
        mesh=mesh,
        in_specs=placed,
        out_specs=(
            P(None, ("group", "fsdp")),
            P(None, ("group", "fsdp")),
            P(("group", "fsdp"), None, None),
            P(("group", "fsdp"), None, None),
        ),
        check_vma=False,
    )
```

```python
import functools

import jax
import jax.numpy as jnp
from jax import lax
from jax.experimental import pallas as pl
from jax.experimental.pallas import tpu as pltpu
from jax.sharding import PartitionSpec as P

MOMENT_DECAY = 0.95
STAT_DECAY = 0.9
ADAM_EPS = 1e-08
PRECON_EPS = 1e-06

LANES = 128
SUBLANES = 8
MESH = pl.DeviceIdType.MESH


def matmul(a, b, a_dim=1, b_dim=0):
    return lax.dot_general(
        a, b, (((a_dim,), (b_dim,)), ((), ())), preferred_element_type=jnp.float32
    )


def alternate(count):
    return sorted(range(1, count), key=lambda k: (-min(k, count - k), k))


def exchange(
    depth,
    across,
    grad_hbm,
    moment_hbm,
    order_hbm,
    left_stat_hbm,
    right_stat_hbm,
    left_root_hbm,
    right_root_hbm,
    wide_back,
    totals,
    holds_half,
    moment,
    left_stat,
    right_stat,
    order,
    grad,
    left_root,
    right_root,
    wide,
    sent,
    via_z,
    turned_z,
    landed_xy,
    turned_xy,
    via_xy,
    turned_back,
    landed_z,
    block,
    gram,
    norms,
    norms_core,
    norms_core_sum,
    norms_z,
    norms_z_sum,
    norms_xy,
    load_sem,
    z_send,
    z_recv,
    xy_send,
    xy_recv,
    norm_send,
    norm_recv,
):
    plane = via_xy.shape[1]
    deep = plane // across
    fan = plane * 2
    blocks = depth * fan
    side = block.shape[0]
    pieces = side // LANES
    g = lax.axis_index("group")
    f = lax.axis_index("fsdp")
    xy = f // 2
    core = f % 2
    x = xy // deep
    y = xy % deep
    me = g * fan + f

    loads = [
        pltpu.make_async_copy(source, target, load_sem.at[i])
        for i, (source, target) in enumerate(
            (
                (order_hbm, order),
                (grad_hbm, grad),
                (moment_hbm, moment),
                (left_root_hbm, left_root),
                (right_root_hbm, right_root),
                (left_stat_hbm, left_stat),
                (right_stat_hbm, right_stat),
            )
        )
    ]
    for load in loads:
        load.start()

    barrier = pltpu.get_barrier_semaphore()

    def greet_z(k, carry):
        to = lax.rem(g + k, depth)
        pl.semaphore_signal(barrier, inc=1, device_id=(to, f), device_id_type=MESH)
        return carry

    def greet_f(k, carry):
        to = lax.rem(f + k, fan)
        pl.semaphore_signal(barrier, inc=1, device_id=(g, to), device_id_type=MESH)
        return carry

    lax.fori_loop(1, depth, greet_z, 0)
    lax.fori_loop(1, fan, greet_f, 0)

    loads[0].wait()
    which = lax.broadcasted_iota(jnp.int32, (blocks, blocks), 0)
    holds = jnp.where(which == order[...], 1.0, 0.0)
    holds_half[...] = holds.astype(jnp.bfloat16)
    slots_half = holds.T.astype(jnp.bfloat16)

    def rows_of(i, j, c):
        return pl.ds(pl.multiple_of((i * fan + j * 2 + c) * SUBLANES, SUBLANES), SUBLANES)

    def tile(i, j, c):
        return wide[rows_of(i, j, c), :].astype(jnp.bfloat16)

    apart = [k for k in range(1, across, 2)] + [k for k in range(2, across, 2)] + [0]
    part = plane // 2
    chunks = [pl.ds(k * part, part) for k in range(2)]

    def place(r, sign):
        k = apart[r // deep]
        return lax.rem(x + (k if sign > 0 else across - k), across) * deep + r % deep

    def send_z(j, k, source, target, half):
        to = lax.rem(g + j, depth)
        pltpu.make_async_remote_copy(
            src_ref=source.at[way, to, chunks[k]],
            dst_ref=target.at[way, g, chunks[k]],
            send_sem=z_send.at[way, half],
            recv_sem=z_recv.at[way, half, k if half == 0 else 0],
            device_id=(to, f),
            device_id_type=MESH,
        ).start()

    def send_xy(k, source, target, half, to_core, skip_self):
        for r in range(k * part, (k + 1) * part):
            dx = apart[r // deep]
            turns = [j for j in (alternate(deep) + [0]) if dx or j or not skip_self]
            if r % deep >= len(turns):
                continue
            to_x = lax.rem(x + dx, across)
            to_y = lax.rem(y + turns[r % deep], deep)
            to = to_x * deep + to_y
            pltpu.make_async_remote_copy(
                src_ref=source.at[way, r // deep * deep + to_y],
                dst_ref=target.at[way, r // deep * deep + y if half else xy],
                send_sem=xy_send.at[way, half],
                recv_sem=xy_recv.at[way, half, k if half else 0],
                device_id=(g, to * 2 + to_core),
                device_id_type=MESH,
            ).start()

    def wait(arrived, sem):
        pltpu.make_async_copy(arrived, arrived, sem).wait()

    def begin():
        for k in range(2):
            for j in alternate(depth):
                to = lax.rem(g + j, depth)
                for r in range(k * part, (k + 1) * part):
                    sent[way, to, r] = tile(to, place(r, 1), core)
                send_z(j, k, sent, via_z, 0)

            def fill(i, carry, k=k):
                for r in range(k * part, (k + 1) * part):
                    turned_xy[way, r, i] = tile(i, place(r, 1), 1 - core)
                return carry

            lax.fori_loop(0, depth, fill, 0)
            send_xy(k, turned_xy, via_xy, 1, 1 - core, False)
        for r in range(plane):
            via_z[way, g, r] = tile(g, place(r, 1), core)

    def go_on_z(k):
        wait(via_xy.at[way, chunks[k]], xy_recv.at[way, 1, k])
        for i in range(depth):
            turned_back[way, i, chunks[k]] = via_xy[way, chunks[k], i]
        for j in alternate(depth):
            send_z(j, k, turned_back, landed_z, 1)

    def go_on_xy(k):
        wait(via_z.at[way, pl.ds(0, depth - 1), chunks[k]], z_recv.at[way, 0, k])
        for i in range(depth):
            turned_z[way, chunks[k], i] = via_z[way, i, chunks[k]]
        send_xy(k, turned_z, landed_xy, 0, core, True)

    def go_on():
        for k in range(2):
            go_on_z(k)
            go_on_xy(k)
        landed_z[way, g] = turned_back[way, g]
        landed_xy[way, xy] = turned_z[way, (len(apart) - 1) * deep + y]

    def end(target):
        wait(landed_xy.at[way, pl.ds(0, plane - 1)], xy_recv.at[way, 0, 0])

        def from_xy(i, carry):
            arrived = landed_xy[way, :, i].astype(jnp.float32)
            for j in range(plane):
                target[rows_of(i, j, core), :] = arrived[j]
            return carry

        lax.fori_loop(0, depth, from_xy, 0)
        wait(landed_z.at[way, pl.ds(0, depth - 1)], z_recv.at[way, 1, 0])

        def from_z(i, carry):
            arrived = landed_z[way, i].astype(jnp.float32)
            for r in range(plane):
                target[rows_of(i, place(r, -1), 1 - core), :] = arrived[r]
            return carry

        lax.fori_loop(0, depth, from_z, 0)

    way = 0
    loads[1].wait()
    for c in range(0, SUBLANES, 2):
        pair = matmul(slots_half, grad[:, c * LANES : (c + 2) * LANES])
        wide[pl.ds(c, blocks, stride=SUBLANES), :] = pair[:, :LANES]
        wide[pl.ds(c + 1, blocks, stride=SUBLANES), :] = pair[:, LANES:]
    pl.semaphore_wait(barrier, depth - 1 + fan - 1)
    begin()

    def adam(i, share):
        rows = pl.ds(pl.multiple_of(i * 16, 16), 16)
        squares = jnp.zeros((16, LANES), jnp.float32)
        for first in range(0, SUBLANES * LANES, 4 * LANES):
            columns = pl.ds(first, 4 * LANES)
            gradient = grad[rows, columns].astype(jnp.float32)
            second = (
                MOMENT_DECAY * moment[rows, columns] + (1.0 - MOMENT_DECAY) * gradient * gradient
            )
            moment[rows, columns] = second
            direction = gradient / (jnp.sqrt(second) + ADAM_EPS)
            direction = direction * direction
            for c in range(4):
                squares = squares + direction[:, c * LANES : (c + 1) * LANES]
        squares = jnp.sum(squares, axis=1, keepdims=True)
        return share + holds_half[rows, :].astype(jnp.float32) * squares

    loads[2].wait()
    share = lax.fori_loop(0, blocks // 16, adam, jnp.zeros((16, blocks), jnp.float32))
    norms[0:1, :] = jnp.sum(share, axis=0, keepdims=True)
    go_on()

    end(wide)
    for c in range(pieces):
        block[:, c * LANES : (c + 1) * LANES] = wide[pl.ds(c, side, stride=pieces), :].astype(
            jnp.bfloat16
        )
    loads[3].wait()
    loads[4].wait()
    half = matmul(left_root[...], block[...]).astype(jnp.bfloat16)
    full = matmul(half, right_root[...])
    for c in range(pieces):
        wide[pl.ds(c, side, stride=pieces), :] = full[:, c * LANES : (c + 1) * LANES]

    way = 1
    begin()

    lane = lax.broadcasted_iota(jnp.int32, (1, blocks), 1)

    def add_square(i, total):
        part = wide[pl.ds(pl.multiple_of(i * 64, 64), 64), :]
        return total + part * part

    precon_sq = lax.fori_loop(
        0, blocks * SUBLANES // 64, add_square, jnp.zeros((64, LANES), jnp.float32)
    )
    precon_sq = jnp.sum(precon_sq, keepdims=True)
    norms[1:2, :] = jnp.where(lane == me, precon_sq, 0.0)

    swap = pltpu.make_async_remote_copy(
        src_ref=norms,
        dst_ref=norms_core,
        send_sem=norm_send.at[0],
        recv_sem=norm_recv.at[0],
        device_id=(g, xy * 2 + 1 - core),
        device_id_type=MESH,
    )
    swap.start()

    def norm_z(j, carry):
        pltpu.make_async_remote_copy(
            src_ref=norms_core_sum,
            dst_ref=norms_z.at[g],
            send_sem=norm_send.at[1],
            recv_sem=norm_recv.at[1],
            device_id=(lax.rem(g + j, depth), f),
            device_id_type=MESH,
        ).start()
        return carry

    def blend(stat):
        def one(i, carry):
            rows = pl.ds(pl.multiple_of(i * 16, 16), 16)
            stat[rows, :] = STAT_DECAY * stat[rows, :] + (1.0 - STAT_DECAY) * gram[rows, :] / side
            return carry

        lax.fori_loop(0, side // 16, one, 0)

    loads[5].wait()
    gram[...] = matmul(block[...], block[...], 1, 1)
    blend(left_stat)
    swap.wait()
    norms_core_sum[...] = norms[...] + norms_core[...]
    lax.fori_loop(1, depth, norm_z, 0)
    loads[6].wait()
    gram[...] = matmul(block[...], block[...], 0, 0)
    blend(right_stat)
    go_on()
    wait(norms_z.at[pl.ds(0, depth - 1)], norm_recv.at[1])
    norms_z[g] = norms_core_sum[...]
    norms_z_sum[...] = jnp.sum(norms_z[...], axis=0)

    def norm_xy(j, carry):
        to = lax.rem(xy + j, plane)
        pltpu.make_async_remote_copy(
            src_ref=norms_z_sum,
            dst_ref=norms_xy.at[xy],
            send_sem=norm_send.at[2],
            recv_sem=norm_recv.at[2],
            device_id=(g, to * 2 + core),
            device_id_type=MESH,
        ).start()
        return carry

    lax.fori_loop(1, plane, norm_xy, 0)
    end(wide_back)
    wait(norms_xy.at[pl.ds(0, plane - 1)], norm_recv.at[2])
    norms_xy[xy] = norms_z_sum[...]
    totals[...] = jnp.sum(norms_xy[...], axis=0)

    for way in range(2):
        wait(via_z.at[way, pl.ds(0, depth - 1)], z_send.at[way, 0])
        wait(landed_z.at[way, pl.ds(0, depth - 1)], z_send.at[way, 1])
        wait(landed_xy.at[way, pl.ds(0, plane - 1)], xy_send.at[way, 0])
        wait(via_xy.at[way], xy_send.at[way, 1])
    wait(norms_z.at[pl.ds(0, depth - 1)], norm_send.at[1])
    wait(norms_xy.at[pl.ds(0, plane - 1)], norm_send.at[2])


def write(
    wide,
    totals,
    holds,
    moment,
    left_stat,
    right_stat,
    update_hbm,
    moment_hbm,
    left_hbm,
    right_hbm,
    update,
    sems,
):
    stores = [
        pltpu.make_async_copy(moment, moment_hbm, sems.at[0]),
        pltpu.make_async_copy(left_stat, left_hbm, sems.at[1]),
        pltpu.make_async_copy(right_stat, right_hbm, sems.at[2]),
    ]
    for store in stores:
        store.start()
    blocks = update.shape[0]
    scale = jnp.sqrt(totals[0:1, :]) / (jnp.sqrt(totals[1:2, :]) + PRECON_EPS)
    scale = jnp.sum(holds[...].astype(jnp.float32) * scale, axis=1, keepdims=True)
    for c in range(0, SUBLANES, 2):
        pair = jnp.concatenate(
            [wide[pl.ds(c + i, blocks, stride=SUBLANES), :] for i in range(2)], axis=1
        ).astype(jnp.bfloat16)
        columns = pl.ds(c * LANES, 2 * LANES)
        update[:, columns] = (matmul(holds[...], pair) * scale).astype(jnp.bfloat16)
        stores.append(
            pltpu.make_async_copy(update.at[:, columns], update_hbm.at[:, columns], sems.at[3 + c // 2])
        )
        stores[-1].start()
    for store in stores:
        store.wait()


def shards(across, grad, moment, order, left_stat, right_stat, left_root, right_root):
    depth = lax.axis_size("group")
    fan = lax.axis_size("fsdp")
    plane = fan // 2
    blocks, entries = grad.shape
    side = left_stat.shape[-1]
    f32, bf16 = jnp.float32, jnp.bfloat16
    tile = (SUBLANES, LANES)
    hbm = pl.BlockSpec(memory_space=pltpu.HBM)
    vmem = pl.BlockSpec(memory_space=pltpu.VMEM)
    order = order.reshape(1, blocks)
    entry_shapes = jax.ShapeDtypeStruct((blocks, entries), f32)
    stat_shapes = jax.ShapeDtypeStruct((side, side), f32)
    wide, totals, holds, moment_new, left_new, right_new = pl.pallas_call(
        functools.partial(exchange, depth, across),
        out_shape=(
            jax.ShapeDtypeStruct((blocks * SUBLANES, LANES), f32),
            jax.ShapeDtypeStruct((2, blocks), f32),
            jax.ShapeDtypeStruct((blocks, blocks), bf16),
            entry_shapes,
            stat_shapes,
            stat_shapes,
        ),
        in_specs=[hbm] * 7,
        out_specs=(vmem,) * 6,
        scratch_shapes=[
            pltpu.VMEM((1, blocks), jnp.int32),
            pltpu.VMEM((blocks, entries), bf16),
            pltpu.VMEM((side, side), bf16),
            pltpu.VMEM((side, side), bf16),
            pltpu.VMEM((blocks * SUBLANES, LANES), f32),
            pltpu.VMEM((2, depth, plane, *tile), bf16),
            pltpu.VMEM((2, depth, plane, *tile), bf16),
            pltpu.VMEM((2, plane, depth, *tile), bf16),
            pltpu.VMEM((2, plane, depth, *tile), bf16),
            pltpu.VMEM((2, plane, depth, *tile), bf16),
            pltpu.VMEM((2, plane, depth, *tile), bf16),
            pltpu.VMEM((2, depth, plane, *tile), bf16),
            pltpu.VMEM((2, depth, plane, *tile), bf16),
            pltpu.VMEM((side, side), bf16),
            pltpu.VMEM((side, side), f32),
            pltpu.VMEM((2, blocks), f32),
            pltpu.VMEM((2, blocks), f32),
            pltpu.VMEM((2, blocks), f32),
            pltpu.VMEM((depth, 2, blocks), f32),
            pltpu.VMEM((2, blocks), f32),
            pltpu.VMEM((plane, 2, blocks), f32),
            pltpu.SemaphoreType.DMA((7,)),
            pltpu.SemaphoreType.DMA((2, 2)),
            pltpu.SemaphoreType.DMA((2, 2, 2)),
            pltpu.SemaphoreType.DMA((2, 2)),
            pltpu.SemaphoreType.DMA((2, 2, 2)),
            pltpu.SemaphoreType.DMA((3,)),
            pltpu.SemaphoreType.DMA((3,)),
        ],
        compiler_params=pltpu.CompilerParams(
            collective_id=0, has_side_effects=True, vmem_limit_bytes=40 * 1024 * 1024
        ),
        cost_estimate=pl.CostEstimate(
            flops=8 * side**3 + 2 * blocks * blocks * entries,
            bytes_accessed=6 * blocks * entries + 12 * side * side,
            transcendentals=2 * blocks * entries,
        ),
    )(
        *(
            pltpu.with_memory_space_constraint(operand, pltpu.HBM)
            for operand in (
                grad,
                moment,
                order,
                left_stat[0],
                right_stat[0],
                left_root[0],
                right_root[0],
            )
        )
    )
    update, moment_new, left_new, right_new = pl.pallas_call(
        write,
        out_shape=(
            jax.ShapeDtypeStruct((blocks, entries), bf16),
            entry_shapes,
            stat_shapes,
            stat_shapes,
        ),
        in_specs=[vmem] * 6,
        out_specs=(hbm,) * 4,
        scratch_shapes=[
            pltpu.VMEM((blocks, entries), bf16),
            pltpu.SemaphoreType.DMA((7,)),
        ],
        compiler_params=pltpu.CompilerParams(vmem_limit_bytes=40 * 1024 * 1024),
        cost_estimate=pl.CostEstimate(
            flops=2 * blocks * blocks * entries,
            bytes_accessed=6 * blocks * entries + 8 * side * side,
            transcendentals=0,
        ),
    )(wide, totals, holds, moment_new, left_new, right_new)
    return (update, moment_new, left_new[None], right_new[None])


def solution(mesh):
    across = 4 if mesh.shape["fsdp"] == 32 else 2
    placed = (
        P(None, ("group", "fsdp")),
        P(None, ("group", "fsdp")),
        P(),
        P(("group", "fsdp"), None, None),
        P(("group", "fsdp"), None, None),
        P(("group", "fsdp"), None, None),
        P(("group", "fsdp"), None, None),
    )
    return jax.shard_map(
        functools.partial(shards, across),
        mesh=mesh,
        in_specs=placed,
        out_specs=(
            P(None, ("group", "fsdp")),
            P(None, ("group", "fsdp")),
            P(("group", "fsdp"), None, None),
            P(("group", "fsdp"), None, None),
        ),
        check_vma=False,
    )
```

```python
import functools

import jax
import jax.numpy as jnp
from jax import lax
from jax.experimental import pallas as pl
from jax.experimental.pallas import tpu as pltpu
from jax.sharding import PartitionSpec as P

MOMENT_DECAY = 0.95
STAT_DECAY = 0.9
ADAM_EPS = 1e-08
PRECON_EPS = 1e-06

LANES = 128
SUBLANES = 8
MESH = pl.DeviceIdType.MESH


def matmul(a, b, a_dim=1, b_dim=0):
    return lax.dot_general(
        a, b, (((a_dim,), (b_dim,)), ((), ())), preferred_element_type=jnp.float32
    )


def alternate(count):
    return sorted(range(1, count), key=lambda k: (-min(k, count - k), k))


def exchange(
    depth,
    across,
    grad_hbm,
    moment_hbm,
    order_hbm,
    left_stat_hbm,
    right_stat_hbm,
    left_root_hbm,
    right_root_hbm,
    wide_back,
    totals,
    holds_half,
    moment,
    left_stat,
    right_stat,
    order,
    grad,
    left_root,
    right_root,
    wide,
    sent,
    via_z,
    turned_z,
    landed_xy,
    turned_xy,
    via_xy,
    turned_back,
    landed_z,
    block,
    gram,
    norms,
    norms_core,
    norms_core_sum,
    norms_z,
    norms_z_sum,
    norms_xy,
    load_sem,
    z_send,
    z_recv,
    xy_send,
    xy_recv,
    norm_send,
    norm_recv,
):
    plane = via_xy.shape[1]
    deep = plane // across
    fan = plane * 2
    blocks = depth * fan
    side = block.shape[0]
    pieces = side // LANES
    g = lax.axis_index("group")
    f = lax.axis_index("fsdp")
    xy = f // 2
    core = f % 2
    x = xy // deep
    y = xy % deep
    me = g * fan + f

    loads = [
        pltpu.make_async_copy(source, target, load_sem.at[i])
        for i, (source, target) in enumerate(
            (
                (order_hbm, order),
                (grad_hbm, grad),
                (moment_hbm, moment),
                (left_root_hbm, left_root),
                (right_root_hbm, right_root),
                (left_stat_hbm, left_stat),
                (right_stat_hbm, right_stat),
            )
        )
    ]
    for load in loads:
        load.start()

    barrier = pltpu.get_barrier_semaphore()

    def greet_z(k, carry):
        to = lax.rem(g + k, depth)
        pl.semaphore_signal(barrier, inc=1, device_id=(to, f), device_id_type=MESH)
        return carry

    def greet_f(k, carry):
        to = lax.rem(f + k, fan)
        pl.semaphore_signal(barrier, inc=1, device_id=(g, to), device_id_type=MESH)
        return carry

    lax.fori_loop(1, depth, greet_z, 0)
    lax.fori_loop(1, fan, greet_f, 0)

    loads[0].wait()
    which = lax.broadcasted_iota(jnp.int32, (blocks, blocks), 0)
    holds = jnp.where(which == order[...], 1.0, 0.0)
    holds_half[...] = holds.astype(jnp.bfloat16)
    slots_half = holds.T.astype(jnp.bfloat16)

    def first_of(i, tx, c):
        return pl.multiple_of((i * fan + tx * (deep * 2) + c) * SUBLANES, SUBLANES)

    def rows_of(first, j):
        return pl.ds(first + j * (2 * SUBLANES), SUBLANES)

    def tile(first, j):
        return wide[rows_of(first, j), :].astype(jnp.bfloat16)

    apart = [k for k in range(1, across, 2)] + [k for k in range(2, across, 2)] + [0]
    part = plane // 2
    chunks = [pl.ds(k * part, part) for k in range(2)]

    def across_by(r, sign):
        k = apart[r // deep]
        return lax.rem(x + (k if sign > 0 else across - k), across)

    def send_z(j, k, source, target, half):
        to = lax.rem(g + j, depth)
        pltpu.make_async_remote_copy(
            src_ref=source.at[way, to, chunks[k]],
            dst_ref=target.at[way, g, chunks[k]],
            send_sem=z_send.at[way, half],
            recv_sem=z_recv.at[way, half, k if half == 0 else 0],
            device_id=(to, f),
            device_id_type=MESH,
        ).start()

    def send_xy(k, source, target, half, to_core, skip_self):
        for r in range(k * part, (k + 1) * part):
            dx = apart[r // deep]
            turns = [j for j in (alternate(deep) + [0]) if dx or j or not skip_self]
            if r % deep >= len(turns):
                continue
            to_x = lax.rem(x + dx, across)
            to_y = lax.rem(y + turns[r % deep], deep)
            to = to_x * deep + to_y
            pltpu.make_async_remote_copy(
                src_ref=source.at[way, r // deep * deep + to_y],
                dst_ref=target.at[way, r // deep * deep + y if half else xy],
                send_sem=xy_send.at[way, half],
                recv_sem=xy_recv.at[way, half, k if half else 0],
                device_id=(g, to * 2 + to_core),
                device_id_type=MESH,
            ).start()

    def wait(arrived, sem):
        pltpu.make_async_copy(arrived, arrived, sem).wait()

    def begin():
        for k in range(2):
            for j in alternate(depth):
                to = lax.rem(g + j, depth)
                for r in range(k * part, (k + 1) * part, deep):
                    first = first_of(to, across_by(r, 1), core)
                    for i in range(deep):
                        sent[way, to, r + i] = tile(first, i)
                send_z(j, k, sent, via_z, 0)

            def fill(i, carry, k=k):
                for r in range(k * part, (k + 1) * part, deep):
                    first = first_of(i, across_by(r, 1), 1 - core)
                    for j in range(deep):
                        turned_xy[way, r + j, i] = tile(first, j)
                return carry

            lax.fori_loop(0, depth, fill, 0)
            send_xy(k, turned_xy, via_xy, 1, 1 - core, False)
        for r in range(0, plane, deep):
            first = first_of(g, across_by(r, 1), core)
            for i in range(deep):
                via_z[way, g, r + i] = tile(first, i)

    def go_on_z(k):
        wait(via_xy.at[way, chunks[k]], xy_recv.at[way, 1, k])
        for i in range(depth):
            turned_back[way, i, chunks[k]] = via_xy[way, chunks[k], i]
        for j in alternate(depth):
            send_z(j, k, turned_back, landed_z, 1)

    def go_on_xy(k):
        wait(via_z.at[way, pl.ds(0, depth - 1), chunks[k]], z_recv.at[way, 0, k])
        for i in range(depth):
            turned_z[way, chunks[k], i] = via_z[way, i, chunks[k]]
        send_xy(k, turned_z, landed_xy, 0, core, True)

    def go_on():
        for k in range(2):
            go_on_z(k)
            go_on_xy(k)
        landed_z[way, g] = turned_back[way, g]
        landed_xy[way, xy] = turned_z[way, (len(apart) - 1) * deep + y]

    def end(target):
        wait(landed_xy.at[way, pl.ds(0, plane - 1)], xy_recv.at[way, 0, 0])

        def from_xy(i, carry):
            arrived = landed_xy[way, :, i].astype(jnp.float32)
            first = first_of(i, 0, core)
            for j in range(plane):
                target[rows_of(first, j), :] = arrived[j]
            return carry

        lax.fori_loop(0, depth, from_xy, 0)
        wait(landed_z.at[way, pl.ds(0, depth - 1)], z_recv.at[way, 1, 0])

        def from_z(i, carry):
            arrived = landed_z[way, i].astype(jnp.float32)
            for r in range(0, plane, deep):
                first = first_of(i, across_by(r, -1), 1 - core)
                for j in range(deep):
                    target[rows_of(first, j), :] = arrived[r + j]
            return carry

        lax.fori_loop(0, depth, from_z, 0)

    way = 0
    loads[1].wait()
    for c in range(0, SUBLANES, 2):
        pair = matmul(slots_half, grad[:, c * LANES : (c + 2) * LANES])
        wide[pl.ds(c, blocks, stride=SUBLANES), :] = pair[:, :LANES]
        wide[pl.ds(c + 1, blocks, stride=SUBLANES), :] = pair[:, LANES:]
    pl.semaphore_wait(barrier, depth - 1 + fan - 1)
    begin()

    def adam(i, share):
        rows = pl.ds(pl.multiple_of(i * 16, 16), 16)
        squares = jnp.zeros((16, LANES), jnp.float32)
        for first in range(0, SUBLANES * LANES, 4 * LANES):
            columns = pl.ds(first, 4 * LANES)
            gradient = grad[rows, columns].astype(jnp.float32)
            second = (
                MOMENT_DECAY * moment[rows, columns] + (1.0 - MOMENT_DECAY) * gradient * gradient
            )
            moment[rows, columns] = second
            direction = gradient / (jnp.sqrt(second) + ADAM_EPS)
            direction = direction * direction
            for c in range(4):
                squares = squares + direction[:, c * LANES : (c + 1) * LANES]
        squares = jnp.sum(squares, axis=1, keepdims=True)
        return share + holds_half[rows, :].astype(jnp.float32) * squares

    loads[2].wait()
    share = lax.fori_loop(0, blocks // 16, adam, jnp.zeros((16, blocks), jnp.float32))
    norms[0:1, :] = jnp.sum(share, axis=0, keepdims=True)
    go_on()

    end(wide)
    for c in range(pieces):
        block[:, c * LANES : (c + 1) * LANES] = wide[pl.ds(c, side, stride=pieces), :].astype(
            jnp.bfloat16
        )
    loads[3].wait()
    loads[4].wait()
    half = matmul(left_root[...], block[...]).astype(jnp.bfloat16)
    full = matmul(half, right_root[...])
    for c in range(pieces):
        wide[pl.ds(c, side, stride=pieces), :] = full[:, c * LANES : (c + 1) * LANES]

    way = 1
    begin()

    lane = lax.broadcasted_iota(jnp.int32, (1, blocks), 1)

    def add_square(i, total):
        part = wide[pl.ds(pl.multiple_of(i * 64, 64), 64), :]
        return total + part * part

    precon_sq = lax.fori_loop(
        0, blocks * SUBLANES // 64, add_square, jnp.zeros((64, LANES), jnp.float32)
    )
    precon_sq = jnp.sum(precon_sq, keepdims=True)
    norms[1:2, :] = jnp.where(lane == me, precon_sq, 0.0)

    swap = pltpu.make_async_remote_copy(
        src_ref=norms,
        dst_ref=norms_core,
        send_sem=norm_send.at[0],
        recv_sem=norm_recv.at[0],
        device_id=(g, xy * 2 + 1 - core),
        device_id_type=MESH,
    )
    swap.start()

    def norm_z(j, carry):
        pltpu.make_async_remote_copy(
            src_ref=norms_core_sum,
            dst_ref=norms_z.at[g],
            send_sem=norm_send.at[1],
            recv_sem=norm_recv.at[1],
            device_id=(lax.rem(g + j, depth), f),
            device_id_type=MESH,
        ).start()
        return carry

    def blend(stat):
        def one(i, carry):
            rows = pl.ds(pl.multiple_of(i * 16, 16), 16)
            stat[rows, :] = STAT_DECAY * stat[rows, :] + (1.0 - STAT_DECAY) * gram[rows, :] / side
            return carry

        lax.fori_loop(0, side // 16, one, 0)

    loads[5].wait()
    gram[...] = matmul(block[...], block[...], 1, 1)
    blend(left_stat)
    swap.wait()
    norms_core_sum[...] = norms[...] + norms_core[...]
    lax.fori_loop(1, depth, norm_z, 0)
    loads[6].wait()
    gram[...] = matmul(block[...], block[...], 0, 0)
    blend(right_stat)
    go_on()
    wait(norms_z.at[pl.ds(0, depth - 1)], norm_recv.at[1])
    norms_z[g] = norms_core_sum[...]
    norms_z_sum[...] = jnp.sum(norms_z[...], axis=0)

    def norm_xy(j, carry):
        to = lax.rem(xy + j, plane)
        pltpu.make_async_remote_copy(
            src_ref=norms_z_sum,
            dst_ref=norms_xy.at[xy],
            send_sem=norm_send.at[2],
            recv_sem=norm_recv.at[2],
            device_id=(g, to * 2 + core),
            device_id_type=MESH,
        ).start()
        return carry

    lax.fori_loop(1, plane, norm_xy, 0)
    end(wide_back)
    wait(norms_xy.at[pl.ds(0, plane - 1)], norm_recv.at[2])
    norms_xy[xy] = norms_z_sum[...]
    totals[...] = jnp.sum(norms_xy[...], axis=0)

    for way in range(2):
        wait(via_z.at[way, pl.ds(0, depth - 1)], z_send.at[way, 0])
        wait(landed_z.at[way, pl.ds(0, depth - 1)], z_send.at[way, 1])
        wait(landed_xy.at[way, pl.ds(0, plane - 1)], xy_send.at[way, 0])
        wait(via_xy.at[way], xy_send.at[way, 1])
    wait(norms_z.at[pl.ds(0, depth - 1)], norm_send.at[1])
    wait(norms_xy.at[pl.ds(0, plane - 1)], norm_send.at[2])


def write(
    wide,
    totals,
    holds,
    moment,
    left_stat,
    right_stat,
    update_hbm,
    moment_hbm,
    left_hbm,
    right_hbm,
    update,
    sems,
):
    stores = []
    for i, (source, target) in enumerate(
        ((moment, moment_hbm), (left_stat, left_hbm), (right_stat, right_hbm))
    ):
        quarter = source.shape[0] // 4
        for j in range(4):
            rows = pl.ds(j * quarter, quarter)
            stores.append(
                pltpu.make_async_copy(source.at[rows], target.at[rows], sems.at[i * 4 + j])
            )
    for store in stores:
        store.start()
    blocks = update.shape[0]
    scale = jnp.sqrt(totals[0:1, :]) / (jnp.sqrt(totals[1:2, :]) + PRECON_EPS)
    scale = jnp.sum(holds[...].astype(jnp.float32) * scale, axis=1, keepdims=True)
    for c in range(0, SUBLANES, 2):
        pair = jnp.concatenate(
            [wide[pl.ds(c + i, blocks, stride=SUBLANES), :] for i in range(2)], axis=1
        ).astype(jnp.bfloat16)
        columns = pl.ds(c * LANES, 2 * LANES)
        update[:, columns] = (matmul(holds[...], pair) * scale).astype(jnp.bfloat16)
        stores.append(
            pltpu.make_async_copy(update.at[:, columns], update_hbm.at[:, columns], sems.at[12 + c // 2])
        )
        stores[-1].start()
    for store in stores:
        store.wait()


def shards(across, grad, moment, order, left_stat, right_stat, left_root, right_root):
    depth = lax.axis_size("group")
    fan = lax.axis_size("fsdp")
    plane = fan // 2
    blocks, entries = grad.shape
    side = left_stat.shape[-1]
    f32, bf16 = jnp.float32, jnp.bfloat16
    tile = (SUBLANES, LANES)
    hbm = pl.BlockSpec(memory_space=pltpu.HBM)
    vmem = pl.BlockSpec(memory_space=pltpu.VMEM)
    order = order.reshape(1, blocks)
    entry_shapes = jax.ShapeDtypeStruct((blocks, entries), f32)
    stat_shapes = jax.ShapeDtypeStruct((side, side), f32)
    wide, totals, holds, moment_new, left_new, right_new = pl.pallas_call(
        functools.partial(exchange, depth, across),
        out_shape=(
            jax.ShapeDtypeStruct((blocks * SUBLANES, LANES), f32),
            jax.ShapeDtypeStruct((2, blocks), f32),
            jax.ShapeDtypeStruct((blocks, blocks), bf16),
            entry_shapes,
            stat_shapes,
            stat_shapes,
        ),
        in_specs=[hbm] * 7,
        out_specs=(vmem,) * 6,
        scratch_shapes=[
            pltpu.VMEM((1, blocks), jnp.int32),
            pltpu.VMEM((blocks, entries), bf16),
            pltpu.VMEM((side, side), bf16),
            pltpu.VMEM((side, side), bf16),
            pltpu.VMEM((blocks * SUBLANES, LANES), f32),
            pltpu.VMEM((2, depth, plane, *tile), bf16),
            pltpu.VMEM((2, depth, plane, *tile), bf16),
            pltpu.VMEM((2, plane, depth, *tile), bf16),
            pltpu.VMEM((2, plane, depth, *tile), bf16),
            pltpu.VMEM((2, plane, depth, *tile), bf16),
            pltpu.VMEM((2, plane, depth, *tile), bf16),
            pltpu.VMEM((2, depth, plane, *tile), bf16),
            pltpu.VMEM((2, depth, plane, *tile), bf16),
            pltpu.VMEM((side, side), bf16),
            pltpu.VMEM((side, side), f32),
            pltpu.VMEM((2, blocks), f32),
            pltpu.VMEM((2, blocks), f32),
            pltpu.VMEM((2, blocks), f32),
            pltpu.VMEM((depth, 2, blocks), f32),
            pltpu.VMEM((2, blocks), f32),
            pltpu.VMEM((plane, 2, blocks), f32),
            pltpu.SemaphoreType.DMA((7,)),
            pltpu.SemaphoreType.DMA((2, 2)),
            pltpu.SemaphoreType.DMA((2, 2, 2)),
            pltpu.SemaphoreType.DMA((2, 2)),
            pltpu.SemaphoreType.DMA((2, 2, 2)),
            pltpu.SemaphoreType.DMA((3,)),
            pltpu.SemaphoreType.DMA((3,)),
        ],
        compiler_params=pltpu.CompilerParams(
            collective_id=0, has_side_effects=True, vmem_limit_bytes=40 * 1024 * 1024
        ),
        cost_estimate=pl.CostEstimate(
            flops=8 * side**3 + 2 * blocks * blocks * entries,
            bytes_accessed=6 * blocks * entries + 12 * side * side,
            transcendentals=2 * blocks * entries,
        ),
    )(
        *(
            pltpu.with_memory_space_constraint(operand, pltpu.HBM)
            for operand in (
                grad,
                moment,
                order,
                left_stat[0],
                right_stat[0],
                left_root[0],
                right_root[0],
            )
        )
    )
    update, moment_new, left_new, right_new = pl.pallas_call(
        write,
        out_shape=(
            jax.ShapeDtypeStruct((blocks, entries), bf16),
            entry_shapes,
            stat_shapes,
            stat_shapes,
        ),
        in_specs=[vmem] * 6,
        out_specs=(hbm,) * 4,
        scratch_shapes=[
            pltpu.VMEM((blocks, entries), bf16),
            pltpu.SemaphoreType.DMA((16,)),
        ],
        compiler_params=pltpu.CompilerParams(vmem_limit_bytes=40 * 1024 * 1024),
        cost_estimate=pl.CostEstimate(
            flops=2 * blocks * blocks * entries,
            bytes_accessed=6 * blocks * entries + 8 * side * side,
            transcendentals=0,
        ),
    )(wide, totals, holds, moment_new, left_new, right_new)
    return (update, moment_new, left_new[None], right_new[None])


def solution(mesh):
    across = 4 if mesh.shape["fsdp"] == 32 else 2
    placed = (
        P(None, ("group", "fsdp")),
        P(None, ("group", "fsdp")),
        P(),
        P(("group", "fsdp"), None, None),
        P(("group", "fsdp"), None, None),
        P(("group", "fsdp"), None, None),
        P(("group", "fsdp"), None, None),
    )
    return jax.shard_map(
        functools.partial(shards, across),
        mesh=mesh,
        in_specs=placed,
        out_specs=(
            P(None, ("group", "fsdp")),
            P(None, ("group", "fsdp")),
            P(("group", "fsdp"), None, None),
            P(("group", "fsdp"), None, None),
        ),
        check_vma=False,
    )
```

```python
import functools

import jax
import jax.numpy as jnp
from jax import lax
from jax.experimental import pallas as pl
from jax.experimental.pallas import tpu as pltpu
from jax.sharding import PartitionSpec as P

MOMENT_DECAY = 0.95
STAT_DECAY = 0.9
ADAM_EPS = 1e-08
PRECON_EPS = 1e-06

LANES = 128
SUBLANES = 8
MESH = pl.DeviceIdType.MESH


def matmul(a, b, a_dim=1, b_dim=0):
    return lax.dot_general(
        a, b, (((a_dim,), (b_dim,)), ((), ())), preferred_element_type=jnp.float32
    )


def alternate(count):
    return sorted(range(1, count), key=lambda k: (-min(k, count - k), k))


def exchange(
    depth,
    across,
    grad_hbm,
    moment_hbm,
    order_hbm,
    left_stat_hbm,
    right_stat_hbm,
    left_root_hbm,
    right_root_hbm,
    wide_back,
    totals,
    holds_half,
    moment,
    left_stat,
    right_stat,
    order,
    grad,
    left_root,
    right_root,
    wide,
    sent,
    via_z,
    turned_z,
    landed_xy,
    turned_xy,
    via_xy,
    turned_back,
    landed_z,
    block,
    gram,
    norms,
    norms_core,
    norms_core_sum,
    norms_z,
    norms_z_sum,
    norms_xy,
    load_sem,
    z_send,
    z_recv,
    xy_send,
    xy_recv,
    norm_send,
    norm_recv,
):
    plane = via_xy.shape[1]
    deep = plane // across
    fan = plane * 2
    blocks = depth * fan
    side = block.shape[0]
    pieces = side // LANES
    g = lax.axis_index("group")
    f = lax.axis_index("fsdp")
    xy = f // 2
    core = f % 2
    x = xy // deep
    y = xy % deep
    me = g * fan + f

    loads = [
        pltpu.make_async_copy(source, target, load_sem.at[i])
        for i, (source, target) in enumerate(
            (
                (order_hbm, order),
                (grad_hbm, grad),
                (moment_hbm, moment),
                (left_root_hbm, left_root),
                (right_root_hbm, right_root),
                (left_stat_hbm, left_stat),
                (right_stat_hbm, right_stat),
            )
        )
    ]
    for load in loads:
        load.start()

    barrier = pltpu.get_barrier_semaphore()

    def greet_z(k, carry):
        to = lax.rem(g + k, depth)
        pl.semaphore_signal(barrier, inc=1, device_id=(to, f), device_id_type=MESH)
        return carry

    def greet_f(k, carry):
        to = lax.rem(f + k, fan)
        pl.semaphore_signal(barrier, inc=1, device_id=(g, to), device_id_type=MESH)
        return carry

    lax.fori_loop(1, depth, greet_z, 0)
    lax.fori_loop(1, fan, greet_f, 0)

    loads[0].wait()
    which = lax.broadcasted_iota(jnp.int32, (blocks, blocks), 0)
    holds = jnp.where(which == order[...], 1.0, 0.0)
    holds_half[...] = holds.astype(jnp.bfloat16)
    slots_half = holds.T.astype(jnp.bfloat16)

    def rows_of(i, j, c):
        return pl.ds(pl.multiple_of((i * fan + j * 2 + c) * SUBLANES, SUBLANES), SUBLANES)

    def tile(i, j, c):
        return wide[rows_of(i, j, c), :].astype(jnp.bfloat16)

    apart = [k for k in range(1, across, 2)] + [k for k in range(2, across, 2)] + [0]
    part = plane // 2
    chunks = [pl.ds(k * part, part) for k in range(2)]

    def place(r, sign):
        k = apart[r // deep]
        return lax.rem(x + (k if sign > 0 else across - k), across) * deep + r % deep

    def send_z(j, k, source, target, half):
        to = lax.rem(g + j, depth)
        pltpu.make_async_remote_copy(
            src_ref=source.at[way, to, chunks[k]],
            dst_ref=target.at[way, g, chunks[k]],
            send_sem=z_send.at[way, half],
            recv_sem=z_recv.at[way, half, k if half == 0 else 0],
            device_id=(to, f),
            device_id_type=MESH,
        ).start()

    def send_xy(k, source, target, half, to_core, skip_self):
        for r in range(k * part, (k + 1) * part):
            dx = apart[r // deep]
            turns = [j for j in (alternate(deep) + [0]) if dx or j or not skip_self]
            if r % deep >= len(turns):
                continue
            to_x = lax.rem(x + dx, across)
            to_y = lax.rem(y + turns[r % deep], deep)
            to = to_x * deep + to_y
            pltpu.make_async_remote_copy(
                src_ref=source.at[way, r // deep * deep + to_y],
                dst_ref=target.at[way, r // deep * deep + y if half else xy],
                send_sem=xy_send.at[way, half],
                recv_sem=xy_recv.at[way, half, k if half else 0],
                device_id=(g, to * 2 + to_core),
                device_id_type=MESH,
            ).start()

    def wait(arrived, sem):
        pltpu.make_async_copy(arrived, arrived, sem).wait()

    def begin():
        for k in range(2):
            def fill(i, carry, k=k):
                for r in range(k * part, (k + 1) * part):
                    turned_xy[way, r, i] = tile(i, place(r, 1), 1 - core)
                return carry

            lax.fori_loop(0, depth, fill, 0)
            send_xy(k, turned_xy, via_xy, 1, 1 - core, False)

            for j in alternate(depth):
                to = lax.rem(g + j, depth)
                for r in range(k * part, (k + 1) * part):
                    sent[way, to, r] = tile(to, place(r, 1), core)
                send_z(j, k, sent, via_z, 0)
        for r in range(plane):
            via_z[way, g, r] = tile(g, place(r, 1), core)

    def go_on_z(k):
        wait(via_xy.at[way, chunks[k]], xy_recv.at[way, 1, k])
        for i in range(depth):
            turned_back[way, i, chunks[k]] = via_xy[way, chunks[k], i]
        for j in alternate(depth):
            send_z(j, k, turned_back, landed_z, 1)

    def go_on_xy(k):
        wait(via_z.at[way, pl.ds(0, depth - 1), chunks[k]], z_recv.at[way, 0, k])
        for i in range(depth):
            turned_z[way, chunks[k], i] = via_z[way, i, chunks[k]]
        send_xy(k, turned_z, landed_xy, 0, core, True)

    def go_on():
        for k in range(2):
            go_on_z(k)
            go_on_xy(k)
        landed_z[way, g] = turned_back[way, g]
        landed_xy[way, xy] = turned_z[way, (len(apart) - 1) * deep + y]

    def end(target):
        wait(landed_xy.at[way, pl.ds(0, plane - 1)], xy_recv.at[way, 0, 0])

        def from_xy(i, carry):
            arrived = landed_xy[way, :, i].astype(jnp.float32)
            for j in range(plane):
                target[rows_of(i, j, core), :] = arrived[j]
            return carry

        lax.fori_loop(0, depth, from_xy, 0)
        wait(landed_z.at[way, pl.ds(0, depth - 1)], z_recv.at[way, 1, 0])

        def from_z(i, carry):
            arrived = landed_z[way, i].astype(jnp.float32)
            for r in range(plane):
                target[rows_of(i, place(r, -1), 1 - core), :] = arrived[r]
            return carry

        lax.fori_loop(0, depth, from_z, 0)

    way = 0
    loads[1].wait()
    for c in range(0, SUBLANES, 2):
        pair = matmul(slots_half, grad[:, c * LANES : (c + 2) * LANES])
        wide[pl.ds(c, blocks, stride=SUBLANES), :] = pair[:, :LANES]
        wide[pl.ds(c + 1, blocks, stride=SUBLANES), :] = pair[:, LANES:]
    pl.semaphore_wait(barrier, depth - 1 + fan - 1)
    begin()

    def adam(i, share):
        rows = pl.ds(pl.multiple_of(i * 16, 16), 16)
        squares = jnp.zeros((16, LANES), jnp.float32)
        for first in range(0, SUBLANES * LANES, 4 * LANES):
            columns = pl.ds(first, 4 * LANES)
            gradient = grad[rows, columns].astype(jnp.float32)
            second = (
                MOMENT_DECAY * moment[rows, columns] + (1.0 - MOMENT_DECAY) * gradient * gradient
            )
            moment[rows, columns] = second
            direction = gradient / (jnp.sqrt(second) + ADAM_EPS)
            direction = direction * direction
            for c in range(4):
                squares = squares + direction[:, c * LANES : (c + 1) * LANES]
        squares = jnp.sum(squares, axis=1, keepdims=True)
        return share + holds_half[rows, :].astype(jnp.float32) * squares

    loads[2].wait()
    share = lax.fori_loop(0, blocks // 16, adam, jnp.zeros((16, blocks), jnp.float32))
    norms[0:1, :] = jnp.sum(share, axis=0, keepdims=True)
    go_on()

    end(wide)
    for c in range(pieces):
        block[:, c * LANES : (c + 1) * LANES] = wide[pl.ds(c, side, stride=pieces), :].astype(
            jnp.bfloat16
        )
    loads[3].wait()
    loads[4].wait()
    half = matmul(left_root[...], block[...]).astype(jnp.bfloat16)
    full = matmul(half, right_root[...])
    for c in range(pieces):
        wide[pl.ds(c, side, stride=pieces), :] = full[:, c * LANES : (c + 1) * LANES]

    way = 1
    begin()

    lane = lax.broadcasted_iota(jnp.int32, (1, blocks), 1)

    def add_square(i, total):
        part = wide[pl.ds(pl.multiple_of(i * 64, 64), 64), :]
        return total + part * part

    precon_sq = lax.fori_loop(
        0, blocks * SUBLANES // 64, add_square, jnp.zeros((64, LANES), jnp.float32)
    )
    precon_sq = jnp.sum(precon_sq, keepdims=True)
    norms[1:2, :] = jnp.where(lane == me, precon_sq, 0.0)

    swap = pltpu.make_async_remote_copy(
        src_ref=norms,
        dst_ref=norms_core,
        send_sem=norm_send.at[0],
        recv_sem=norm_recv.at[0],
        device_id=(g, xy * 2 + 1 - core),
        device_id_type=MESH,
    )
    swap.start()

    def norm_z(j, carry):
        pltpu.make_async_remote_copy(
            src_ref=norms_core_sum,
            dst_ref=norms_z.at[g],
            send_sem=norm_send.at[1],
            recv_sem=norm_recv.at[1],
            device_id=(lax.rem(g + j, depth), f),
            device_id_type=MESH,
        ).start()
        return carry

    def blend(stat):
        def one(i, carry):
            rows = pl.ds(pl.multiple_of(i * 16, 16), 16)
            stat[rows, :] = STAT_DECAY * stat[rows, :] + (1.0 - STAT_DECAY) * gram[rows, :] / side
            return carry

        lax.fori_loop(0, side // 16, one, 0)

    loads[5].wait()
    gram[...] = matmul(block[...], block[...], 1, 1)
    blend(left_stat)
    swap.wait()
    norms_core_sum[...] = norms[...] + norms_core[...]
    lax.fori_loop(1, depth, norm_z, 0)
    loads[6].wait()
    gram[...] = matmul(block[...], block[...], 0, 0)
    blend(right_stat)
    go_on()
    wait(norms_z.at[pl.ds(0, depth - 1)], norm_recv.at[1])
    norms_z[g] = norms_core_sum[...]
    norms_z_sum[...] = jnp.sum(norms_z[...], axis=0)

    def norm_xy(j, carry):
        to = lax.rem(xy + j, plane)
        pltpu.make_async_remote_copy(
            src_ref=norms_z_sum,
            dst_ref=norms_xy.at[xy],
            send_sem=norm_send.at[2],
            recv_sem=norm_recv.at[2],
            device_id=(g, to * 2 + core),
            device_id_type=MESH,
        ).start()
        return carry

    lax.fori_loop(1, plane, norm_xy, 0)
    end(wide_back)
    wait(norms_xy.at[pl.ds(0, plane - 1)], norm_recv.at[2])
    norms_xy[xy] = norms_z_sum[...]
    totals[...] = jnp.sum(norms_xy[...], axis=0)

    for way in range(2):
        wait(via_z.at[way, pl.ds(0, depth - 1)], z_send.at[way, 0])
        wait(landed_z.at[way, pl.ds(0, depth - 1)], z_send.at[way, 1])
        wait(landed_xy.at[way, pl.ds(0, plane - 1)], xy_send.at[way, 0])
        wait(via_xy.at[way], xy_send.at[way, 1])
    wait(norms_z.at[pl.ds(0, depth - 1)], norm_send.at[1])
    wait(norms_xy.at[pl.ds(0, plane - 1)], norm_send.at[2])


def write(
    wide,
    totals,
    holds,
    moment,
    left_stat,
    right_stat,
    update_hbm,
    moment_hbm,
    left_hbm,
    right_hbm,
    update,
    sems,
):
    stores = [
        pltpu.make_async_copy(moment, moment_hbm, sems.at[0]),
        pltpu.make_async_copy(left_stat, left_hbm, sems.at[1]),
        pltpu.make_async_copy(right_stat, right_hbm, sems.at[2]),
    ]
    for store in stores:
        store.start()
    blocks = update.shape[0]
    scale = jnp.sqrt(totals[0:1, :]) / (jnp.sqrt(totals[1:2, :]) + PRECON_EPS)
    scale = jnp.sum(holds[...].astype(jnp.float32) * scale, axis=1, keepdims=True)
    for c in range(0, SUBLANES, 2):
        pair = jnp.concatenate(
            [wide[pl.ds(c + i, blocks, stride=SUBLANES), :] for i in range(2)], axis=1
        ).astype(jnp.bfloat16)
        columns = pl.ds(c * LANES, 2 * LANES)
        update[:, columns] = (matmul(holds[...], pair) * scale).astype(jnp.bfloat16)
        stores.append(
            pltpu.make_async_copy(update.at[:, columns], update_hbm.at[:, columns], sems.at[3 + c // 2])
        )
        stores[-1].start()
    for store in stores:
        store.wait()


def shards(across, grad, moment, order, left_stat, right_stat, left_root, right_root):
    depth = lax.axis_size("group")
    fan = lax.axis_size("fsdp")
    plane = fan // 2
    blocks, entries = grad.shape
    side = left_stat.shape[-1]
    f32, bf16 = jnp.float32, jnp.bfloat16
    tile = (SUBLANES, LANES)
    hbm = pl.BlockSpec(memory_space=pltpu.HBM)
    vmem = pl.BlockSpec(memory_space=pltpu.VMEM)
    order = order.reshape(1, blocks)
    entry_shapes = jax.ShapeDtypeStruct((blocks, entries), f32)
    stat_shapes = jax.ShapeDtypeStruct((side, side), f32)
    wide, totals, holds, moment_new, left_new, right_new = pl.pallas_call(
        functools.partial(exchange, depth, across),
        out_shape=(
            jax.ShapeDtypeStruct((blocks * SUBLANES, LANES), f32),
            jax.ShapeDtypeStruct((2, blocks), f32),
            jax.ShapeDtypeStruct((blocks, blocks), bf16),
            entry_shapes,
            stat_shapes,
            stat_shapes,
        ),
        in_specs=[hbm] * 7,
        out_specs=(vmem,) * 6,
        scratch_shapes=[
            pltpu.VMEM((1, blocks), jnp.int32),
            pltpu.VMEM((blocks, entries), bf16),
            pltpu.VMEM((side, side), bf16),
            pltpu.VMEM((side, side), bf16),
            pltpu.VMEM((blocks * SUBLANES, LANES), f32),
            pltpu.VMEM((2, depth, plane, *tile), bf16),
            pltpu.VMEM((2, depth, plane, *tile), bf16),
            pltpu.VMEM((2, plane, depth, *tile), bf16),
            pltpu.VMEM((2, plane, depth, *tile), bf16),
            pltpu.VMEM((2, plane, depth, *tile), bf16),
            pltpu.VMEM((2, plane, depth, *tile), bf16),
            pltpu.VMEM((2, depth, plane, *tile), bf16),
            pltpu.VMEM((2, depth, plane, *tile), bf16),
            pltpu.VMEM((side, side), bf16),
            pltpu.VMEM((side, side), f32),
            pltpu.VMEM((2, blocks), f32),
            pltpu.VMEM((2, blocks), f32),
            pltpu.VMEM((2, blocks), f32),
            pltpu.VMEM((depth, 2, blocks), f32),
            pltpu.VMEM((2, blocks), f32),
            pltpu.VMEM((plane, 2, blocks), f32),
            pltpu.SemaphoreType.DMA((7,)),
            pltpu.SemaphoreType.DMA((2, 2)),
            pltpu.SemaphoreType.DMA((2, 2, 2)),
            pltpu.SemaphoreType.DMA((2, 2)),
            pltpu.SemaphoreType.DMA((2, 2, 2)),
            pltpu.SemaphoreType.DMA((3,)),
            pltpu.SemaphoreType.DMA((3,)),
        ],
        compiler_params=pltpu.CompilerParams(
            collective_id=0, has_side_effects=True, vmem_limit_bytes=40 * 1024 * 1024
        ),
        cost_estimate=pl.CostEstimate(
            flops=8 * side**3 + 2 * blocks * blocks * entries,
            bytes_accessed=6 * blocks * entries + 12 * side * side,
            transcendentals=2 * blocks * entries,
        ),
    )(
        *(
            pltpu.with_memory_space_constraint(operand, pltpu.HBM)
            for operand in (
                grad,
                moment,
                order,
                left_stat[0],
                right_stat[0],
                left_root[0],
                right_root[0],
            )
        )
    )
    update, moment_new, left_new, right_new = pl.pallas_call(
        write,
        out_shape=(
            jax.ShapeDtypeStruct((blocks, entries), bf16),
            entry_shapes,
            stat_shapes,
            stat_shapes,
        ),
        in_specs=[vmem] * 6,
        out_specs=(hbm,) * 4,
        scratch_shapes=[
            pltpu.VMEM((blocks, entries), bf16),
            pltpu.SemaphoreType.DMA((7,)),
        ],
        compiler_params=pltpu.CompilerParams(vmem_limit_bytes=40 * 1024 * 1024),
        cost_estimate=pl.CostEstimate(
            flops=2 * blocks * blocks * entries,
            bytes_accessed=6 * blocks * entries + 8 * side * side,
            transcendentals=0,
        ),
    )(wide, totals, holds, moment_new, left_new, right_new)
    return (update, moment_new, left_new[None], right_new[None])


def solution(mesh):
    across = 4 if mesh.shape["fsdp"] == 32 else 2
    placed = (
        P(None, ("group", "fsdp")),
        P(None, ("group", "fsdp")),
        P(),
        P(("group", "fsdp"), None, None),
        P(("group", "fsdp"), None, None),
        P(("group", "fsdp"), None, None),
        P(("group", "fsdp"), None, None),
    )
    return jax.shard_map(
        functools.partial(shards, across),
        mesh=mesh,
        in_specs=placed,
        out_specs=(
            P(None, ("group", "fsdp")),
            P(None, ("group", "fsdp")),
            P(("group", "fsdp"), None, None),
            P(("group", "fsdp"), None, None),
        ),
        check_vma=False,
    )
```

```python
import functools

import jax
import jax.numpy as jnp
from jax import lax
from jax.experimental import pallas as pl
from jax.experimental.pallas import tpu as pltpu
from jax.sharding import PartitionSpec as P

MOMENT_DECAY = 0.95
STAT_DECAY = 0.9
ADAM_EPS = 1e-08
PRECON_EPS = 1e-06

LANES = 128
SUBLANES = 8
MESH = pl.DeviceIdType.MESH


def matmul(a, b, a_dim=1, b_dim=0):
    return lax.dot_general(
        a, b, (((a_dim,), (b_dim,)), ((), ())), preferred_element_type=jnp.float32
    )


def alternate(count):
    return sorted(range(1, count), key=lambda k: (-min(k, count - k), k))


def exchange(
    depth,
    across,
    grad_hbm,
    moment_hbm,
    order_hbm,
    left_stat_hbm,
    right_stat_hbm,
    left_root_hbm,
    right_root_hbm,
    wide_back,
    totals,
    holds_half,
    moment,
    left_stat,
    right_stat,
    order,
    grad,
    left_root,
    right_root,
    wide,
    sent,
    via_z,
    turned_z,
    landed_xy,
    turned_xy,
    via_xy,
    turned_back,
    landed_z,
    block,
    gram,
    norms,
    norms_core,
    norms_core_sum,
    norms_z,
    norms_z_sum,
    norms_xy,
    load_sem,
    z_send,
    z_recv,
    xy_send,
    xy_recv,
    norm_send,
    norm_recv,
):
    plane = via_xy.shape[1]
    deep = plane // across
    fan = plane * 2
    blocks = depth * fan
    side = block.shape[0]
    pieces = side // LANES
    g = lax.axis_index("group")
    f = lax.axis_index("fsdp")
    xy = f // 2
    core = f % 2
    x = xy // deep
    y = xy % deep
    me = g * fan + f

    loads = [
        pltpu.make_async_copy(source, target, load_sem.at[i])
        for i, (source, target) in enumerate(
            (
                (order_hbm, order),
                (grad_hbm, grad),
                (moment_hbm, moment),
                (left_root_hbm, left_root),
                (right_root_hbm, right_root),
                (left_stat_hbm, left_stat),
                (right_stat_hbm, right_stat),
            )
        )
    ]
    for load in loads:
        load.start()

    barrier = pltpu.get_barrier_semaphore()

    def greet_z(k, carry):
        to = lax.rem(g + k, depth)
        pl.semaphore_signal(barrier, inc=1, device_id=(to, f), device_id_type=MESH)
        return carry

    def greet_f(k, carry):
        to = lax.rem(f + k, fan)
        pl.semaphore_signal(barrier, inc=1, device_id=(g, to), device_id_type=MESH)
        return carry

    lax.fori_loop(1, depth, greet_z, 0)
    lax.fori_loop(1, fan, greet_f, 0)

    loads[0].wait()
    which = lax.broadcasted_iota(jnp.int32, (blocks, blocks), 0)
    holds = jnp.where(which == order[...], 1.0, 0.0).astype(jnp.bfloat16)
    holds_half[...] = holds
    slots_half = holds.T

    def rows_of(i, j, c):
        return pl.ds(pl.multiple_of((i * fan + j * 2 + c) * SUBLANES, SUBLANES), SUBLANES)

    def tile(i, j, c):
        return wide[rows_of(i, j, c), :].astype(jnp.bfloat16)

    apart = [k for k in range(1, across, 2)] + [k for k in range(2, across, 2)] + [0]
    part = plane // 2
    chunks = [pl.ds(k * part, part) for k in range(2)]

    def place(r, sign):
        k = apart[r // deep]
        return lax.rem(x + (k if sign > 0 else across - k), across) * deep + r % deep

    def send_z(j, k, source, target, half):
        to = lax.rem(g + j, depth)
        pltpu.make_async_remote_copy(
            src_ref=source.at[way, to, chunks[k]],
            dst_ref=target.at[way, g, chunks[k]],
            send_sem=z_send.at[way, half],
            recv_sem=z_recv.at[way, half, k if half == 0 else 0],
            device_id=(to, f),
            device_id_type=MESH,
        ).start()

    def send_xy(k, source, target, half, to_core, skip_self):
        for r in range(k * part, (k + 1) * part):
            dx = apart[r // deep]
            turns = [j for j in (alternate(deep) + [0]) if dx or j or not skip_self]
            if r % deep >= len(turns):
                continue
            to_x = lax.rem(x + dx, across)
            to_y = lax.rem(y + turns[r % deep], deep)
            to = to_x * deep + to_y
            pltpu.make_async_remote_copy(
                src_ref=source.at[way, r // deep * deep + to_y],
                dst_ref=target.at[way, r // deep * deep + y if half else xy],
                send_sem=xy_send.at[way, half],
                recv_sem=xy_recv.at[way, half, k if half else 0],
                device_id=(g, to * 2 + to_core),
                device_id_type=MESH,
            ).start()

    def wait(arrived, sem):
        pltpu.make_async_copy(arrived, arrived, sem).wait()

    def begin():
        for k in range(2):
            for j in alternate(depth):
                to = lax.rem(g + j, depth)
                for r in range(k * part, (k + 1) * part):
                    sent[way, to, r] = tile(to, place(r, 1), core)
                send_z(j, k, sent, via_z, 0)

            def fill(i, carry, k=k):
                for r in range(k * part, (k + 1) * part):
                    turned_xy[way, r, i] = tile(i, place(r, 1), 1 - core)
                return carry

            lax.fori_loop(0, depth, fill, 0)
            send_xy(k, turned_xy, via_xy, 1, 1 - core, False)
        for r in range(plane):
            via_z[way, g, r] = tile(g, place(r, 1), core)

    def go_on_z(k):
        wait(via_xy.at[way, chunks[k]], xy_recv.at[way, 1, k])
        for i in range(depth):
            turned_back[way, i, chunks[k]] = via_xy[way, chunks[k], i]
        for j in alternate(depth):
            send_z(j, k, turned_back, landed_z, 1)

    def go_on_xy(k):
        wait(via_z.at[way, pl.ds(0, depth - 1), chunks[k]], z_recv.at[way, 0, k])
        for i in range(depth):
            turned_z[way, chunks[k], i] = via_z[way, i, chunks[k]]
        send_xy(k, turned_z, landed_xy, 0, core, True)

    def go_on():
        for k in range(2):
            go_on_z(k)
            go_on_xy(k)
        landed_z[way, g] = turned_back[way, g]
        landed_xy[way, xy] = turned_z[way, (len(apart) - 1) * deep + y]

    def end(target):
        wait(landed_xy.at[way, pl.ds(0, plane - 1)], xy_recv.at[way, 0, 0])

        def from_xy(i, carry):
            arrived = landed_xy[way, :, i].astype(jnp.float32)
            for j in range(plane):
                target[rows_of(i, j, core), :] = arrived[j]
            return carry

        lax.fori_loop(0, depth, from_xy, 0)
        wait(landed_z.at[way, pl.ds(0, depth - 1)], z_recv.at[way, 1, 0])

        def from_z(i, carry):
            arrived = landed_z[way, i].astype(jnp.float32)
            for r in range(plane):
                target[rows_of(i, place(r, -1), 1 - core), :] = arrived[r]
            return carry

        lax.fori_loop(0, depth, from_z, 0)

    way = 0
    loads[1].wait()
    for c in range(0, SUBLANES, 2):
        pair = matmul(slots_half, grad[:, c * LANES : (c + 2) * LANES])
        wide[pl.ds(c, blocks, stride=SUBLANES), :] = pair[:, :LANES]
        wide[pl.ds(c + 1, blocks, stride=SUBLANES), :] = pair[:, LANES:]
    pl.semaphore_wait(barrier, depth - 1 + fan - 1)
    begin()

    def adam(i, share):
        rows = pl.ds(pl.multiple_of(i * 16, 16), 16)
        squares = jnp.zeros((16, LANES), jnp.float32)
        for first in range(0, SUBLANES * LANES, 4 * LANES):
            columns = pl.ds(first, 4 * LANES)
            gradient = grad[rows, columns].astype(jnp.float32)
            second = (
                MOMENT_DECAY * moment[rows, columns] + (1.0 - MOMENT_DECAY) * gradient * gradient
            )
            moment[rows, columns] = second
            direction = gradient / (jnp.sqrt(second) + ADAM_EPS)
            direction = direction * direction
            for c in range(4):
                squares = squares + direction[:, c * LANES : (c + 1) * LANES]
        squares = jnp.sum(squares, axis=1, keepdims=True)
        return share + holds_half[rows, :].astype(jnp.float32) * squares

    loads[2].wait()
    share = lax.fori_loop(0, blocks // 16, adam, jnp.zeros((16, blocks), jnp.float32))
    norms[0:1, :] = jnp.sum(share, axis=0, keepdims=True)
    go_on()

    end(wide)
    for c in range(pieces):
        block[:, c * LANES : (c + 1) * LANES] = wide[pl.ds(c, side, stride=pieces), :].astype(
            jnp.bfloat16
        )
    loads[3].wait()
    loads[4].wait()
    half = matmul(left_root[...], block[...]).astype(jnp.bfloat16)
    full = matmul(half, right_root[...])
    for c in range(pieces):
        wide[pl.ds(c, side, stride=pieces), :] = full[:, c * LANES : (c + 1) * LANES]

    way = 1
    begin()

    lane = lax.broadcasted_iota(jnp.int32, (1, blocks), 1)

    def add_square(i, total):
        part = wide[pl.ds(pl.multiple_of(i * 64, 64), 64), :]
        return total + part * part

    precon_sq = lax.fori_loop(
        0, blocks * SUBLANES // 64, add_square, jnp.zeros((64, LANES), jnp.float32)
    )
    precon_sq = jnp.sum(precon_sq, keepdims=True)
    norms[1:2, :] = jnp.where(lane == me, precon_sq, 0.0)

    swap = pltpu.make_async_remote_copy(
        src_ref=norms,
        dst_ref=norms_core,
        send_sem=norm_send.at[0],
        recv_sem=norm_recv.at[0],
        device_id=(g, xy * 2 + 1 - core),
        device_id_type=MESH,
    )
    swap.start()

    def norm_z(j, carry):
        pltpu.make_async_remote_copy(
            src_ref=norms_core_sum,
            dst_ref=norms_z.at[g],
            send_sem=norm_send.at[1],
            recv_sem=norm_recv.at[1],
            device_id=(lax.rem(g + j, depth), f),
            device_id_type=MESH,
        ).start()
        return carry

    def blend(stat):
        def one(i, carry):
            rows = pl.ds(pl.multiple_of(i * 16, 16), 16)
            stat[rows, :] = STAT_DECAY * stat[rows, :] + (1.0 - STAT_DECAY) * gram[rows, :] / side
            return carry

        lax.fori_loop(0, side // 16, one, 0)

    loads[5].wait()
    gram[...] = matmul(block[...], block[...], 1, 1)
    blend(left_stat)
    swap.wait()
    norms_core_sum[...] = norms[...] + norms_core[...]
    lax.fori_loop(1, depth, norm_z, 0)
    loads[6].wait()
    gram[...] = matmul(block[...], block[...], 0, 0)
    blend(right_stat)
    go_on()
    wait(norms_z.at[pl.ds(0, depth - 1)], norm_recv.at[1])
    norms_z[g] = norms_core_sum[...]
    norms_z_sum[...] = jnp.sum(norms_z[...], axis=0)

    def norm_xy(j, carry):
        to = lax.rem(xy + j, plane)
        pltpu.make_async_remote_copy(
            src_ref=norms_z_sum,
            dst_ref=norms_xy.at[xy],
            send_sem=norm_send.at[2],
            recv_sem=norm_recv.at[2],
            device_id=(g, to * 2 + core),
            device_id_type=MESH,
        ).start()
        return carry

    lax.fori_loop(1, plane, norm_xy, 0)
    end(wide_back)
    wait(norms_xy.at[pl.ds(0, plane - 1)], norm_recv.at[2])
    norms_xy[xy] = norms_z_sum[...]
    totals[...] = jnp.sum(norms_xy[...], axis=0)

    for way in range(2):
        wait(via_z.at[way, pl.ds(0, depth - 1)], z_send.at[way, 0])
        wait(landed_z.at[way, pl.ds(0, depth - 1)], z_send.at[way, 1])
        wait(landed_xy.at[way, pl.ds(0, plane - 1)], xy_send.at[way, 0])
        wait(via_xy.at[way], xy_send.at[way, 1])
    wait(norms_z.at[pl.ds(0, depth - 1)], norm_send.at[1])
    wait(norms_xy.at[pl.ds(0, plane - 1)], norm_send.at[2])


def write(
    wide,
    totals,
    holds,
    moment,
    left_stat,
    right_stat,
    update_hbm,
    moment_hbm,
    left_hbm,
    right_hbm,
    update,
    sems,
):
    stores = [
        pltpu.make_async_copy(moment, moment_hbm, sems.at[0]),
        pltpu.make_async_copy(left_stat, left_hbm, sems.at[1]),
        pltpu.make_async_copy(right_stat, right_hbm, sems.at[2]),
    ]
    for store in stores:
        store.start()
    blocks = update.shape[0]
    scale = jnp.sqrt(totals[0:1, :]) / (jnp.sqrt(totals[1:2, :]) + PRECON_EPS)
    scale = jnp.sum(holds[...].astype(jnp.float32) * scale, axis=1, keepdims=True)
    for c in range(0, SUBLANES, 2):
        pair = jnp.concatenate(
            [wide[pl.ds(c + i, blocks, stride=SUBLANES), :] for i in range(2)], axis=1
        ).astype(jnp.bfloat16)
        columns = pl.ds(c * LANES, 2 * LANES)
        update[:, columns] = (matmul(holds[...], pair) * scale).astype(jnp.bfloat16)
        stores.append(
            pltpu.make_async_copy(update.at[:, columns], update_hbm.at[:, columns], sems.at[3 + c // 2])
        )
        stores[-1].start()
    for store in stores:
        store.wait()


def shards(across, grad, moment, order, left_stat, right_stat, left_root, right_root):
    depth = lax.axis_size("group")
    fan = lax.axis_size("fsdp")
    plane = fan // 2
    blocks, entries = grad.shape
    side = left_stat.shape[-1]
    f32, bf16 = jnp.float32, jnp.bfloat16
    tile = (SUBLANES, LANES)
    hbm = pl.BlockSpec(memory_space=pltpu.HBM)
    vmem = pl.BlockSpec(memory_space=pltpu.VMEM)
    order = order.reshape(1, blocks)
    entry_shapes = jax.ShapeDtypeStruct((blocks, entries), f32)
    stat_shapes = jax.ShapeDtypeStruct((side, side), f32)
    wide, totals, holds, moment_new, left_new, right_new = pl.pallas_call(
        functools.partial(exchange, depth, across),
        out_shape=(
            jax.ShapeDtypeStruct((blocks * SUBLANES, LANES), f32),
            jax.ShapeDtypeStruct((2, blocks), f32),
            jax.ShapeDtypeStruct((blocks, blocks), bf16),
            entry_shapes,
            stat_shapes,
            stat_shapes,
        ),
        in_specs=[hbm] * 7,
        out_specs=(vmem,) * 6,
        scratch_shapes=[
            pltpu.VMEM((1, blocks), jnp.int32),
            pltpu.VMEM((blocks, entries), bf16),
            pltpu.VMEM((side, side), bf16),
            pltpu.VMEM((side, side), bf16),
            pltpu.VMEM((blocks * SUBLANES, LANES), f32),
            pltpu.VMEM((2, depth, plane, *tile), bf16),
            pltpu.VMEM((2, depth, plane, *tile), bf16),
            pltpu.VMEM((2, plane, depth, *tile), bf16),
            pltpu.VMEM((2, plane, depth, *tile), bf16),
            pltpu.VMEM((2, plane, depth, *tile), bf16),
            pltpu.VMEM((2, plane, depth, *tile), bf16),
            pltpu.VMEM((2, depth, plane, *tile), bf16),
            pltpu.VMEM((2, depth, plane, *tile), bf16),
            pltpu.VMEM((side, side), bf16),
            pltpu.VMEM((side, side), f32),
            pltpu.VMEM((2, blocks), f32),
            pltpu.VMEM((2, blocks), f32),
            pltpu.VMEM((2, blocks), f32),
            pltpu.VMEM((depth, 2, blocks), f32),
            pltpu.VMEM((2, blocks), f32),
            pltpu.VMEM((plane, 2, blocks), f32),
            pltpu.SemaphoreType.DMA((7,)),
            pltpu.SemaphoreType.DMA((2, 2)),
            pltpu.SemaphoreType.DMA((2, 2, 2)),
            pltpu.SemaphoreType.DMA((2, 2)),
            pltpu.SemaphoreType.DMA((2, 2, 2)),
            pltpu.SemaphoreType.DMA((3,)),
            pltpu.SemaphoreType.DMA((3,)),
        ],
        compiler_params=pltpu.CompilerParams(
            collective_id=0, has_side_effects=True, vmem_limit_bytes=40 * 1024 * 1024
        ),
        cost_estimate=pl.CostEstimate(
            flops=8 * side**3 + 2 * blocks * blocks * entries,
            bytes_accessed=6 * blocks * entries + 12 * side * side,
            transcendentals=2 * blocks * entries,
        ),
    )(
        *(
            pltpu.with_memory_space_constraint(operand, pltpu.HBM)
            for operand in (
                grad,
                moment,
                order,
                left_stat[0],
                right_stat[0],
                left_root[0],
                right_root[0],
            )
        )
    )
    update, moment_new, left_new, right_new = pl.pallas_call(
        write,
        out_shape=(
            jax.ShapeDtypeStruct((blocks, entries), bf16),
            entry_shapes,
            stat_shapes,
            stat_shapes,
        ),
        in_specs=[vmem] * 6,
        out_specs=(hbm,) * 4,
        scratch_shapes=[
            pltpu.VMEM((blocks, entries), bf16),
            pltpu.SemaphoreType.DMA((7,)),
        ],
        compiler_params=pltpu.CompilerParams(vmem_limit_bytes=40 * 1024 * 1024),
        cost_estimate=pl.CostEstimate(
            flops=2 * blocks * blocks * entries,
            bytes_accessed=6 * blocks * entries + 8 * side * side,
            transcendentals=0,
        ),
    )(wide, totals, holds, moment_new, left_new, right_new)
    return (update, moment_new, left_new[None], right_new[None])


def solution(mesh):
    across = 4 if mesh.shape["fsdp"] == 32 else 2
    placed = (
        P(None, ("group", "fsdp")),
        P(None, ("group", "fsdp")),
        P(),
        P(("group", "fsdp"), None, None),
        P(("group", "fsdp"), None, None),
        P(("group", "fsdp"), None, None),
        P(("group", "fsdp"), None, None),
    )
    return jax.shard_map(
        functools.partial(shards, across),
        mesh=mesh,
        in_specs=placed,
        out_specs=(
            P(None, ("group", "fsdp")),
            P(None, ("group", "fsdp")),
            P(("group", "fsdp"), None, None),
            P(("group", "fsdp"), None, None),
        ),
        check_vma=False,
    )
```
